256 devices in a mesh: layer: 8 (over z), plane: 32 (over y, x, core).
Axes of the slice: x: 4, y: 4, z: 8, core: 2. Of those that a mesh axis runs over, the one named last changes fastest.
Arguments:
- leaf_rhs: bfloat16 [2048, 128, 512], P(('layer', 'plane')), may hold values from -6 to 6
- leaf_inverse: bfloat16 [2048, 128, 128], P(('layer', 'plane')), may hold values from -0.5 to 0.5
- leaf_couple: bfloat16 [2048, 3, 1024, 128], P(('layer', 'plane')), may hold values from -0.09375 to 0.09375
- couple_mask: int32 [2048, 3], P(('layer', 'plane')), may hold values 0 or 1
- leaf_diag: float32 [2048, 128], P(('layer', 'plane')), may hold values from 0.5 to 2
- sep_rhs: bfloat16 [7, 1024, 512], P(None, 'plane'), may hold values from -6 to 6
- sep_inverse: bfloat16 [7, 1024, 1024], P(None, 'plane'), may hold values from -0.1875 to 0.1875
- sep_couple: bfloat16 [7, 2, 1024, 1024], P(None, None, 'plane'), may hold values from -0.125 to 0.125
- sep_diag: float32 [7, 1024], P(None, 'plane'), may hold values from 0.5 to 2
Outputs:
- leaf_solution: bfloat16 [2048, 128, 512], P(('layer', 'plane'))
- sep_solution: bfloat16 [8, 3, 1024, 512], P('layer', None, 'plane')
The draws below stay inside these ranges and needn't reach their ends.
All inputs are finite; a program needn't handle non-finite values. No bound on the sum of `couple_mask` on one device may be relied on, other than what follows from the above.
Results may differ from the reference program's by a relative error of at most 0.02.
Values may be sent and summed in bfloat16 or wider, within the bound.
A program may use at most 128 MiB of HBM per device.

```python
import math
import jax
import jax.numpy as jnp
from jax import lax

BLK = 128
SEP = 1024
RHS = 512
LB = 8
LEVELS = 3
NSEP = 7
NBLOCKS = 2048
N_LAYER = 8
N_PLANE = 32


def plant(array, own_key, smallest, top_value):
    place = [jax.random.randint(jax.random.fold_in(own_key, axis), (), 0, length) for axis, length in enumerate(array.shape)]
    main_axis = array.shape.index(max(array.shape))
    neighbour = place[:main_axis] + [(place[main_axis] + 1) % array.shape[main_axis]] + place[main_axis + 1:]
    return array.at[tuple(place)].set(smallest).at[tuple(neighbour)].set(top_value)


def strengthened(array, own_key, source, target, parts, factor):
    owner, partner = [(jnp.arange(array.shape[axis_at]) // (array.shape[axis_at] // parts)).reshape([-1 if axis == axis_at else 1 for axis in range(array.ndim)]) for axis_at in (source, target)]
    chosen = jax.random.permutation(own_key, parts)[partner]
    strong = (owner == chosen) | (owner == (partner + parts // 2) % parts)
    return jnp.where(strong, factor * array, array)


def level_of(key, dims, split, smallest, largest):
    def one(position, blocks):
        steps = jax.random.uniform(jax.random.fold_in(jax.random.fold_in(key, 6), position), (blocks,), jnp.float32, smallest / len(split), largest / len(split))
        return jnp.repeat(jnp.exp(steps), dims[position] // blocks).reshape((-1,) + (1,) * (len(dims) - position - 1))

    factor_of = one(*split[0])
    for cut in split[1:]:
        factor_of = factor_of * one(*cut)
    return factor_of


def scatter_about(key, shape, width, limit, cuts=(), held_as=jnp.bfloat16):
    result = jax.random.normal(key, shape, jnp.float32) * width
    if len(cuts) > 0:
        result = level_of(key, shape, cuts, -0.22, 0.18) * result
    return jnp.clip(result, min=-limit, max=limit).astype(held_as)


def heavy_noise(rng, shape, spread, bound, cuts, heavy, dtype=jnp.bfloat16):
    result = spread * jax.random.normal(rng, shape, jnp.float32)
    if cuts:
        result = result * level_of(rng, shape, cuts, -0.22, 0.18)
    return jnp.clip(strengthened(result, jax.random.fold_in(rng, 3), *heavy), -bound, bound).astype(dtype)


def setup_inputs(seed: int = 0) -> dict:
    streams_of = jax.random.split(jax.random.key(seed), 10)
    leaf_rhs = scatter_about(streams_of[0], (NBLOCKS, BLK, RHS), 1.0, 6.0, ((0, 256),))
    leaf_inverse = scatter_about(streams_of[1], (NBLOCKS, BLK, BLK), BLK ** -0.5, 0.5, ((0, 256),))
    leaf_couple = heavy_noise(streams_of[2], (NBLOCKS, LEVELS, SEP, BLK), (LB * BLK * N_PLANE * 2) ** -0.5, 0.09375, ((0, 256),), (0, 2, 256, 6.0))
    couple_mask = plant((jax.random.randint(streams_of[3], (NBLOCKS, LEVELS), 0, 4) < 3).astype(jnp.int32), jax.random.fold_in(streams_of[3], 1), 0, 1)
    leaf_diag = jnp.clip(jnp.exp(math.log(2.0) - 1.3862944 * jax.random.uniform(streams_of[4], (NBLOCKS, BLK), jnp.float32) ** level_of(streams_of[4], (NBLOCKS, BLK), ((0, 256),), -0.2, 0.2)), 0.5, 2.0)
    sep_rhs = scatter_about(streams_of[5], (NSEP, SEP, RHS), 1.0, 6.0, ((1, 32),))
    sep_inverse = scatter_about(streams_of[6], (NSEP, SEP, SEP), SEP ** -0.5, 0.1875, ((1, 32),))
    sep_couple = scatter_about(streams_of[7], (NSEP, LEVELS - 1, SEP, SEP), (SEP * 2) ** -0.5, 0.125, ((2, 32),))
    sep_diag = jnp.clip(jnp.exp(math.log(2.0) - 1.3862944 * jax.random.uniform(streams_of[8], (NSEP, SEP), jnp.float32) ** level_of(streams_of[8], (NSEP, SEP), ((1, 32),), -0.2, 0.2)), 0.5, 2.0)
    return dict(leaf_rhs=leaf_rhs, leaf_inverse=leaf_inverse, leaf_couple=leaf_couple, couple_mask=couple_mask, leaf_diag=leaf_diag, sep_rhs=sep_rhs, sep_inverse=sep_inverse, sep_couple=sep_couple, sep_diag=sep_diag)


def lower_unit(block, first_row):
    row_count = block.shape[-2]
    col_count = block.shape[-1]
    row_ids = first_row + lax.broadcasted_iota(jnp.int32, (row_count, col_count), 0)
    col_ids = lax.broadcasted_iota(jnp.int32, (row_count, col_count), 1)
    below = jnp.where(col_ids < row_ids, block, jnp.zeros_like(block))
    return jnp.where(col_ids == row_ids, jnp.ones_like(block), below)


def reference(leaf_rhs, leaf_inverse, leaf_couple, couple_mask, leaf_diag, sep_rhs, sep_inverse, sep_couple, sep_diag):
    per_layer = N_PLANE * LB
    leaf_values = []
    leaf_terms = []
    for layer_id in range(N_LAYER):
        first = layer_id * per_layer
        lower_part = lower_unit(leaf_inverse[first:first + per_layer], 0).astype(jnp.float32)
        solved = jnp.einsum("bij,bjr->bir", lower_part, leaf_rhs[first:first + per_layer].astype(jnp.float32)).astype(jnp.bfloat16)
        masked = leaf_couple[first:first + per_layer].astype(jnp.float32) * couple_mask[first:first + per_layer].astype(jnp.float32)[:, :, None, None]
        leaf_terms.append(jnp.einsum("bksc,bcr->ksr", masked, solved.astype(jnp.float32)))
        leaf_values.append(solved)
    group_sums = jnp.stack(leaf_terms)
    sep_z = []
    for level in range(1, LEVELS + 1):
        group_sums = group_sums[0::2] + group_sums[1::2]
        count_here = N_LAYER >> level
        offset = N_LAYER - 2 * count_here
        residual = (sep_rhs[offset:offset + count_here].astype(jnp.float32) - group_sums[:, level - 1]).astype(jnp.bfloat16)
        lower_part = lower_unit(sep_inverse[offset:offset + count_here], 0).astype(jnp.float32)
        solved = jnp.einsum("gij,gjr->gir", lower_part, residual.astype(jnp.float32)).astype(jnp.bfloat16)
        if level < LEVELS:
            blocks = sep_couple[offset:offset + count_here, :LEVELS - level].astype(jnp.float32)
            coupling = jnp.einsum("gjts,gsr->gjtr", blocks, solved.astype(jnp.float32))
            group_sums = group_sums.at[:, level:].add(coupling)
        sep_z.append(solved.astype(jnp.float32) / sep_diag[offset:offset + count_here][:, :, None])
    sep_x = [None] * LEVELS
    for level in range(LEVELS, 0, -1):
        count_here = N_LAYER >> level
        offset = N_LAYER - 2 * count_here
        target_now = sep_z[level - 1]
        if level < LEVELS:
            blocks = sep_couple[offset:offset + count_here, :LEVELS - level].astype(jnp.float32)
            carried = jnp.zeros(target_now.shape, jnp.float32)
            for slot in range(LEVELS - level):
                upper_level = level + 1 + slot
                upper_rows = jnp.repeat(sep_x[upper_level - 1], 2 ** (upper_level - level), axis=0)
                carried = carried + jnp.einsum("gts,gtr->gsr", blocks[:, slot], upper_rows.astype(jnp.float32))
            target_now = target_now - carried
        target_now = target_now.astype(jnp.bfloat16)
        lower_part = lower_unit(sep_inverse[offset:offset + count_here], 0).astype(jnp.float32)
        sep_x[level - 1] = jnp.einsum("gts,gtr->gsr", lower_part, target_now.astype(jnp.float32)).astype(jnp.bfloat16)
    sep_solution = jnp.stack([jnp.repeat(sep_x[level - 1], 2 ** level, axis=0) for level in range(1, LEVELS + 1)], axis=1)
    leaf_outputs = []
    for layer_id in range(N_LAYER):
        first = layer_id * per_layer
        above = jnp.stack([sep_x[level - 1][layer_id >> level] for level in range(1, LEVELS + 1)]).astype(jnp.float32)
        masked = leaf_couple[first:first + per_layer].astype(jnp.float32) * couple_mask[first:first + per_layer].astype(jnp.float32)[:, :, None, None]
        back_terms = jnp.einsum("bksc,ksr->bcr", masked, above)
        leaf_target = (leaf_values[layer_id].astype(jnp.float32) / leaf_diag[first:first + per_layer][:, :, None] - back_terms).astype(jnp.bfloat16)
        lower_part = lower_unit(leaf_inverse[first:first + per_layer], 0).astype(jnp.float32)
        leaf_outputs.append(jnp.einsum("bjc,bjr->bcr", lower_part, leaf_target.astype(jnp.float32)).astype(jnp.bfloat16))
    return jnp.concatenate(leaf_outputs, axis=0), sep_solution
```

```python
import jax
import jax.numpy as jnp
from jax import lax
from jax.experimental import pallas as pl
from jax.experimental.pallas import tpu as pltpu
from jax.sharding import PartitionSpec as P

BF16 = jnp.bfloat16
F32 = jnp.float32
SIDE = 4
CORES = 2
EXTRA = 128
TILE = 256


def dot_rows(left, right):
    return lax.dot_general(left, right, (((1,), (1,)), ((), ())), preferred_element_type=F32)


def dot_cols(left, right):
    return lax.dot_general(left, right, (((1,), (0,)), ((), ())), preferred_element_type=F32)


def unit_lower(block, first_row):
    row_ids = first_row + lax.broadcasted_iota(jnp.int32, block.shape, 0)
    col_ids = lax.broadcasted_iota(jnp.int32, block.shape, 1)
    value = block.astype(F32)
    value = jnp.where(col_ids < row_ids, value, 0.0)
    return jnp.where(col_ids == row_ids, 1.0, value).astype(BF16)


def kernel(
    mask_ref,
    rhs_hbm,
    inverse_hbm,
    couple_hbm,
    diag_hbm,
    sep_rhs_hbm,
    sep_inverse_hbm,
    sep_couple_hbm,
    sep_diag_hbm,
    leaf_out,
    sep_out,
    rhs,
    inverse,
    couple,
    diag,
    sep_rhs,
    own_inverse,
    own_diag,
    mat0,
    mat1,
    mat2,
    leaf_y,
    leaf_ym,
    lower_t,
    part,
    paired,
    chip_sum,
    in1,
    sum1,
    in2,
    total,
    from_odd,
    out_total,
    to_two,
    from_one,
    to_three,
    from_two,
    sep_y,
    sep_z,
    answer,
    back,
    local_sem,
    couple_sem,
    g_send,
    g_recv,
    gc_send,
    gc_recv,
    r_send,
    r_recv,
    rc_send,
    rc_recv,
    a_send,
    a_recv,
    ac_send,
    ac_recv,
    odd_send,
    odd_recv,
    two_send,
    two_recv,
    three_send,
    three_recv,
    x_send,
    x_recv,
):
    blocks, blk, right_sides = rhs.shape
    own_rows = own_inverse.shape[0]
    size = own_inverse.shape[1]
    half = size // 2
    layer = lax.axis_index("layer")
    plane = lax.axis_index("plane")
    layers = lax.axis_size("layer")
    y = plane // (SIDE * CORES)
    x = (plane // CORES) % SIDE
    core = plane % CORES
    first_row = plane * own_rows

    def at_plane(y_at, x_at, core_at):
        return (layer, (y_at * SIDE + x_at) * CORES + core_at)

    def x_peer(d):
        return at_plane(y, (x + d) % SIDE, core)

    def y_peer(d):
        return at_plane((y + d) % SIDE, x, core)

    sibling = at_plane(y, x, 1 - core)

    is_one = layer % 2 == 0
    is_odd = layer % 2 == 1
    is_two = layer % 4 == 1
    is_three = layer == 3
    has_first = layer != 7
    has_second = jnp.logical_or(is_one, is_two)
    sep_of = [layer // 2, 4 + layer // 4, 6 + layer * 0]
    own_sep = jnp.where(is_one, layer // 2, jnp.where(is_two, 4 + layer // 4, 6))

    sends = []

    def remote(parts, when=None):
        def make():
            src, dst, send_sem, recv_sem, device = parts()
            return pltpu.make_async_remote_copy(
                src_ref=src,
                dst_ref=dst,
                send_sem=send_sem,
                recv_sem=recv_sem,
                device_id=device,
                device_id_type=pl.DeviceIdType.MESH,
            )

        make().start()
        sends.append((when, make))

    def arrived(dst, sem):
        pltpu.make_async_copy(dst, dst, sem).wait()

    barrier = pltpu.get_barrier_semaphore()
    peers = [sibling]
    for d in range(1, SIDE):
        peers += [x_peer(d), y_peer(d)]
    for d in range(1, 8):
        peers.append(((layer + d) % 8, plane))
    for peer in peers:
        pl.semaphore_signal(barrier, inc=1, device_id=peer, device_id_type=pl.DeviceIdType.MESH)

    local = [
        pltpu.make_async_copy(sep_inverse_hbm.at[own_sep], own_inverse, local_sem.at[0]),
        pltpu.make_async_copy(sep_diag_hbm, own_diag, local_sem.at[1]),
        pltpu.make_async_copy(sep_couple_hbm.at[own_sep, 0], mat1.at[y, x, core], local_sem.at[2]),
        pltpu.make_async_copy(sep_couple_hbm.at[own_sep, 1], mat2.at[y, x, core], local_sem.at[3]),
        pltpu.make_async_copy(inverse_hbm, inverse, local_sem.at[4]),
        pltpu.make_async_copy(rhs_hbm, rhs, local_sem.at[5]),
        pltpu.make_async_copy(diag_hbm, diag, local_sem.at[6]),
        pltpu.make_async_copy(sep_rhs_hbm.at[sep_of[0]], sep_rhs.at[0], local_sem.at[7]),
        pltpu.make_async_copy(sep_rhs_hbm.at[sep_of[1]], sep_rhs.at[1], local_sem.at[8]),
        pltpu.make_async_copy(sep_rhs_hbm.at[sep_of[2]], sep_rhs.at[2], local_sem.at[9]),
    ]
    for copy in local:
        copy.start()
    couples = []
    for k in range(3):
        couples.append(
            [
                pltpu.make_async_copy(
                    couple_hbm.at[b, k], couple.at[k, :, pl.ds(b * blk, blk)], couple_sem.at[k, b]
                )
                for b in range(blocks)
            ]
        )
        for copy in couples[k]:
            copy.start()

    def lanes(buf, h):
        return pl.ds(0, half) if h == 0 else pl.ds(half, buf().shape[-1] - half)

    def send_first(buf, sems, h, d, when):
        def parts():
            ref = buf().at[y, x, core, :, lanes(buf, h)]
            send, recv = sems(0, h, d - 1)
            return ref, ref, send, recv, x_peer(d) if h == 0 else y_peer(d)

        remote(parts, when)

    def send_second(buf, sems, h, d, when):
        def parts():
            if h == 0:
                ref = buf().at[y, :, core, :, lanes(buf, h)]
            else:
                ref = buf().at[:, x, core, :, lanes(buf, h)]
            send, recv = sems(1, h, d - 1)
            return ref, ref, send, recv, y_peer(d) if h == 0 else x_peer(d)

        remote(parts, when)

    def gather_first(buf, sems, when=None):
        for h in range(2):
            for d in range(1, SIDE):
                send_first(buf, sems, h, d, when)

    def gather_second(buf, sems, when=None):
        for h in range(2):
            for d in range(1, SIDE):
                if h == 0:
                    ref = buf().at[y, (x - d + SIDE) % SIDE, core, :, lanes(buf, h)]
                else:
                    ref = buf().at[(y - d + SIDE) % SIDE, x, core, :, lanes(buf, h)]
                arrived(ref, sems(0, h, d - 1)[1])
            for d in range(1, SIDE):
                send_second(buf, sems, h, d, when)

    def gather_third(buf, sems, c_sems, when=None):
        for h in range(2):
            for d in range(1, SIDE):
                if h == 0:
                    ref = buf().at[(y - d + SIDE) % SIDE, :, core, :, lanes(buf, h)]
                else:
                    ref = buf().at[:, (x - d + SIDE) % SIDE, core, :, lanes(buf, h)]
                arrived(ref, sems(1, h, d - 1)[1])

        def parts():
            ref = buf().at[:, :, core]
            return (ref, ref) + c_sems() + (sibling,)

        remote(parts, when)

    def gather_end(buf, c_recv):
        arrived(buf.at[:, :, 1 - core], c_recv)

    mats = [mat0, mat1, mat2]
    uses = [has_first, has_second, is_one]

    def whole(m):
        return mats[m][:, :, :, :, 0:size].reshape(size, size)

    def mat_parts(m):
        return (
            lambda: mats[m],
            lambda *at: (g_send.at[(m,) + at], g_recv.at[(m,) + at]),
            lambda: (gc_send.at[m], gc_recv.at[m]),
        )

    def mat_first(m):
        buf, sems, _ = mat_parts(m)

        @pl.when(uses[m])
        def _():
            gather_first(buf, sems, uses[m])

    def mat_second(m):
        buf, sems, _ = mat_parts(m)

        @pl.when(uses[m])
        def _():
            gather_second(buf, sems, uses[m])

    def mat_third(m):
        buf, sems, c_sems = mat_parts(m)

        @pl.when(uses[m])
        def _():
            gather_third(buf, sems, c_sems, uses[m])

    def mat_end(m):
        gather_end(mats[m], gc_recv.at[m])

    local[0].wait()
    local[1].wait()
    eye = lax.broadcasted_iota(jnp.int32, (own_rows, own_rows), 0) == lax.broadcasted_iota(
        jnp.int32, (own_rows, own_rows), 1
    )
    sep_rows = lax.broadcasted_iota(jnp.int32, own_diag.shape, 0) == own_sep
    diag_row = jnp.sum(jnp.where(sep_rows, own_diag[...], 0.0), axis=0, keepdims=True)
    diag_col = jnp.sum(jnp.where(eye, diag_row, 0.0), axis=1, keepdims=True)
    high = diag_col.astype(BF16).astype(F32)
    middle = (diag_col - high).astype(BF16).astype(F32)
    low = diag_col - high - middle
    lane = lax.broadcasted_iota(jnp.int32, (own_rows, EXTRA), 1)
    beside = jnp.where(
        lane == 0, high, jnp.where(lane == 1, middle, jnp.where(lane == 2, low, 0.0))
    ).astype(BF16)
    mat0[y, x, core, :, 0:size] = unit_lower(own_inverse[...], first_row)
    mat0[y, x, core, :, size:] = beside
    pl.semaphore_wait(barrier, len(peers))
    mat_first(0)
    local[2].wait()
    local[3].wait()
    mat_first(1)
    mat_first(2)

    for i in range(4, 10):
        local[i].wait()

    def solve_leaf(b, _):
        lower = unit_lower(inverse[b], 0)
        lower_t[b] = lower.astype(F32).T.astype(BF16)
        rhs_t = rhs[b].T
        columns = pl.ds(pl.multiple_of(b * blk, blk), blk)
        leaf_y[:, columns] = dot_rows(rhs_t, lower).astype(BF16)
        return 0

    lax.fori_loop(0, blocks, solve_leaf, 0)

    block_of = lax.broadcasted_iota(jnp.int32, (1, blocks * blk), 1) // blk

    def mask_lanes(k):
        result = jnp.zeros((1, blocks * blk), F32)
        for b in range(blocks):
            result = result + jnp.where(block_of == b, mask_ref[b, k].astype(F32), 0.0)
        return result

    def leaf_part(k):
        for copy in couples[k]:
            copy.wait()
        leaf_ym[...] = leaf_y[...] * mask_lanes(k).astype(BF16)
        rhs_t = sep_rhs[k].T
        adds = layer % (2 ** (k + 1)) == 0
        first = jnp.where(adds, first_row, size)

        def tile(i, _):
            start = pl.multiple_of(i * TILE, TILE)
            columns = pl.ds(start, TILE)
            rows_at = first + lax.broadcasted_iota(jnp.int32, (own_rows, TILE), 0)
            cols_at = start + lax.broadcasted_iota(jnp.int32, (own_rows, TILE), 1)
            place = jnp.where(rows_at == cols_at, 1.0, 0.0).astype(BF16)
            term = dot_cols(rhs_t, place) - dot_rows(leaf_ym[...], couple[k, columns, :])
            part[k, :, :, :, :, columns] = term.astype(BF16).reshape(
                part.shape[1:-1] + (TILE,)
            )
            return 0

        lax.fori_loop(0, size // TILE, tile, 0)
        remote(
            lambda: (
                part.at[k, :, :, 1 - core],
                paired.at[k],
                rc_send.at[k],
                rc_recv.at[k],
                sibling,
            )
        )

    def reduce_first(k):
        arrived(paired.at[k], rc_recv.at[k])
        chip_sum[k] = (part[k, :, :, core].astype(F32) + paired[k].astype(F32)).astype(BF16)
        for h in range(2):
            for d in range(1, SIDE):
                send_part(k, h, d)

    def send_part(k, h, d):
        def parts():
            if h == 0:
                ref = chip_sum.at[k, :, (x + d) % SIDE, :, pl.ds(0, half)]
            else:
                ref = chip_sum.at[k, (y + d) % SIDE, :, :, pl.ds(half, half)]
            return (
                ref,
                in1.at[k, h, d - 1],
                r_send.at[k, 0, h, d - 1],
                r_recv.at[k, 0, h, d - 1],
                x_peer(d) if h == 0 else y_peer(d),
            )

        remote(parts)

    def send_sum(k, h, d):
        remote(
            lambda: (
                sum1.at[k, h, ((y if h == 0 else x) + d) % SIDE],
                in2.at[k, h, d - 1],
                r_send.at[k, 1, h, d - 1],
                r_recv.at[k, 1, h, d - 1],
                y_peer(d) if h == 0 else x_peer(d),
            )
        )

    def reduce_second(k):
        for h in range(2):
            if h == 0:
                value = chip_sum[k, :, x, :, 0:half].astype(F32)
            else:
                value = chip_sum[k, y, :, :, half:].astype(F32)
            for d in range(1, SIDE):
                arrived(in1.at[k, h, d - 1], r_recv.at[k, 0, h, d - 1])
                value = value + in1[k, h, d - 1].astype(F32)
            sum1[k, h] = value.astype(BF16)
            for d in range(1, SIDE):
                send_sum(k, h, d)

    def reduce_end(k):
        for h in range(2):
            value = sum1[k, h, y if h == 0 else x].astype(F32)
            for d in range(1, SIDE):
                arrived(in2.at[k, h, d - 1], r_recv.at[k, 1, h, d - 1])
                value = value + in2[k, h, d - 1].astype(F32)
            total[k, :, h * half : (h + 1) * half] = value

        @pl.when(is_odd)
        def _():
            out_total[k] = total[k].astype(BF16)
            remote(
                lambda: (
                    out_total.at[k],
                    from_odd.at[k],
                    odd_send.at[k],
                    odd_recv.at[k],
                    ((layer + 7) % 8, plane),
                ),
                is_odd,
            )

    def whole_total(k):
        arrived(from_odd.at[k], odd_recv.at[k])
        return total[k] + from_odd[k].astype(F32)

    def divide(value):
        picks = jnp.where(
            lax.broadcasted_iota(jnp.int32, (value.shape[0], EXTRA), 1) < 3, 1.0, 0.0
        ).astype(BF16)
        parts = mat0[:, :, :, :, size:].reshape(size, EXTRA)
        return value / dot_rows(picks, parts)

    def forward(residual):
        solved = dot_rows(residual.astype(BF16), whole(0)).astype(BF16)
        sep_y[...] = solved
        sep_z[...] = divide(solved.astype(F32))

    two_of = (layer // 4) * 4 + 1
    two_slot = (layer % 4) // 2

    leaf_part(0)
    mat_second(0)
    leaf_part(1)
    reduce_first(0)
    leaf_part(2)
    mat_second(1)
    reduce_first(1)
    reduce_second(0)
    mat_third(0)
    reduce_first(2)
    reduce_end(0)
    reduce_second(1)

    @pl.when(is_one)
    def _():
        residual = whole_total(0)
        mat_end(0)
        forward(residual)

    mat_third(1)
    reduce_end(1)
    mat_second(2)
    reduce_second(2)

    def pass_up(k):
        to_two[k - 1] = (whole_total(k) - dot_rows(sep_y[...], whole(k))).astype(BF16)
        remote(
            lambda: (
                to_two.at[k - 1],
                from_one.at[two_slot, k - 1],
                two_send.at[k - 1],
                two_recv.at[two_slot, k - 1],
                (two_of, plane),
            ),
            is_one,
        )

    @pl.when(is_one)
    def _():
        mat_end(1)
        pass_up(1)

    reduce_end(2)
    mat_third(2)

    @pl.when(is_one)
    def _():
        mat_end(2)
        pass_up(2)

    @pl.when(is_two)
    def _():
        mat_end(0)
        mat_end(1)
        for slot in range(2):
            arrived(from_one.at[slot, 0], two_recv.at[slot, 0])
        forward(from_one[0, 0].astype(F32) + from_one[1, 0].astype(F32))
        term = dot_rows(sep_y[...], whole(1))
        for slot in range(2):
            arrived(from_one.at[slot, 1], two_recv.at[slot, 1])
        to_three[...] = (from_one[0, 1].astype(F32) + from_one[1, 1].astype(F32) - term).astype(
            BF16
        )
        remote(
            lambda: (
                to_three,
                from_two.at[layer // 4],
                three_send,
                three_recv.at[layer // 4],
                (3, plane),
            ),
            is_two,
        )

    def finish(k, target):
        answer[k, y, x, core] = dot_cols(target.astype(BF16), whole(0)).astype(BF16)

    def own_answer(k):
        return answer.at[k, y, x, core]

    def send_answer(k, slot, layer_to, when):
        remote(
            lambda: (
                own_answer(k),
                own_answer(k),
                x_send.at[slot],
                x_recv.at[k],
                (layer_to(), plane),
            ),
            when,
        )

    @pl.when(is_three)
    def _():
        mat_end(0)
        for slot in range(2):
            arrived(from_two.at[slot], three_recv.at[slot])
        forward(from_two[0].astype(F32) + from_two[1].astype(F32))
        finish(2, sep_z[...])
        for slot, layer_to in enumerate((1, 5, 2, 4, 0, 6, 7)):
            send_answer(2, slot, lambda layer_to=layer_to: layer_to, is_three)

    @pl.when(jnp.logical_not(is_three))
    def _():
        arrived(own_answer(2), x_recv.at[2])

    @pl.when(is_two)
    def _():
        finish(1, sep_z[...] - dot_cols(own_answer(2)[...], whole(1)))
        for slot, shift in enumerate((7, 1, 2)):
            send_answer(1, 7 + slot, lambda shift=shift: (layer + shift) % 8, is_two)

    def answer_parts(k):
        return (
            lambda: answer.at[k],
            lambda *at: (a_send.at[(k,) + at], a_recv.at[(k,) + at]),
            lambda: (ac_send.at[k], ac_recv.at[k]),
        )

    def answer_first(k, when=None):
        gather_first(*answer_parts(k)[:2], when)

    def answer_second(k):
        gather_second(*answer_parts(k)[:2])

    def answer_third(k):
        gather_third(*answer_parts(k))

    def answer_whole(k):
        return answer[k].reshape(right_sides, size)

    answer_first(2)

    @pl.when(is_one)
    def _():
        sep_z[...] = sep_z[...] - dot_cols(own_answer(2)[...], whole(2))

    answer_second(2)

    @pl.when(jnp.logical_not(is_two))
    def _():
        arrived(own_answer(1), x_recv.at[1])

    @pl.when(is_one)
    def _():
        finish(0, sep_z[...] - dot_cols(own_answer(1)[...], whole(1)))
        send_answer(0, 10, lambda: layer + 1, is_one)
        answer_first(0, is_one)

    own_rows_at = jnp.where(
        first_row + lax.broadcasted_iota(jnp.int32, (own_rows, size), 0)
        == lax.broadcasted_iota(jnp.int32, (own_rows, size), 1),
        1.0,
        0.0,
    ).astype(BF16)

    def leaf_back(k):
        gather_end(answer.at[k], ac_recv.at[k])
        masks = mask_lanes(k)
        sep_out[0, k] = dot_rows(own_rows_at, answer_whole(k)).astype(BF16)
        leaf_ym[...] = jnp.broadcast_to(masks, leaf_ym.shape).astype(BF16)

        def tile(i, _):
            columns = pl.ds(pl.multiple_of(i * TILE, TILE), TILE)
            term = dot_cols(answer_whole(k), couple[k, :, columns]) * leaf_ym[
                :, columns
            ].astype(F32)
            back[:, columns] = term if k == 2 else back[:, columns] + term
            return 0

        lax.fori_loop(0, size // TILE, tile, 0)

    answer_first(1)
    answer_third(2)

    @pl.when(is_odd)
    def _():
        arrived(own_answer(0), x_recv.at[0])
        answer_first(0, is_odd)

    leaf_back(2)
    answer_second(1)
    answer_second(0)
    answer_third(1)
    leaf_back(1)
    answer_third(0)
    leaf_back(0)

    def solve_back(b, _):
        columns = pl.ds(pl.multiple_of(b * blk, blk), blk)
        target = leaf_y[:, columns].astype(F32) / diag[pl.ds(b, 1), :] - back[:, columns]
        leaf_out[b] = dot_rows(lower_t[b], target.astype(BF16)).astype(BF16)
        return 0

    lax.fori_loop(0, blocks, solve_back, 0)

    for when, make in sends:
        if when is None:
            make().wait_send()
    for group in (has_first, has_second, is_one, is_odd, is_two, is_three):

        @pl.when(group)
        def _(group=group):
            for when, make in sends:
                if when is group:
                    make().wait_send()


def body(
    leaf_rhs,
    leaf_inverse,
    leaf_couple,
    couple_mask,
    leaf_diag,
    sep_rhs,
    sep_inverse,
    sep_couple,
    sep_diag,
):
    blocks, levels, size, blk = leaf_couple.shape
    right_sides = leaf_rhs.shape[2]
    own_rows = sep_rhs.shape[1]
    cols = right_sides // (SIDE * SIDE * CORES)
    half = size // 2
    grid = (SIDE, SIDE, CORES)
    vmem = pltpu.VMEM
    dma = pltpu.SemaphoreType.DMA
    hops = (levels, 2, 2, SIDE - 1)
    scratch = [
        vmem(leaf_rhs.shape, BF16),
        vmem(leaf_inverse.shape, BF16),
        vmem((levels, size, blocks * blk), BF16),
        vmem(leaf_diag.shape, F32),
        vmem((levels, own_rows, right_sides), BF16),
        vmem((own_rows, size), BF16),
        vmem(sep_diag.shape, F32),
        vmem(grid + (own_rows, size + EXTRA), BF16),
        vmem(grid + (own_rows, size), BF16),
        vmem(grid + (own_rows, size), BF16),
        vmem((right_sides, blocks * blk), BF16),
        vmem((right_sides, blocks * blk), BF16),
        vmem(leaf_inverse.shape, BF16),
        vmem((levels,) + grid + (cols, size), BF16),
        vmem((levels, SIDE, SIDE, cols, size), BF16),
        vmem((levels, SIDE, SIDE, cols, size), BF16),
        vmem((levels, 2, SIDE - 1, SIDE, cols, half), BF16),
        vmem((levels, 2, SIDE, cols, half), BF16),
        vmem((levels, 2, SIDE - 1, cols, half), BF16),
        vmem((levels, cols, size), F32),
        vmem((levels, cols, size), BF16),
        vmem((levels, cols, size), BF16),
        vmem((2, cols, size), BF16),
        vmem((2, 2, cols, size), BF16),
        vmem((cols, size), BF16),
        vmem((2, cols, size), BF16),
        vmem((cols, size), BF16),
        vmem((cols, size), F32),
        vmem((levels,) + grid + (cols, size), BF16),
        vmem((right_sides, blocks * blk), F32),
        dma((10,)),
        dma((levels, blocks)),
        dma(hops),
        dma(hops),
        dma((levels,)),
        dma((levels,)),
        dma(hops),
        dma(hops),
        dma((levels,)),
        dma((levels,)),
        dma(hops),
        dma(hops),
        dma((levels,)),
        dma((levels,)),
        dma((levels,)),
        dma((levels,)),
        dma((2,)),
        dma((2, 2)),
        dma,
        dma((2,)),
        dma((11,)),
        dma((levels,)),
    ]
    any_space = pl.BlockSpec(memory_space=pl.ANY)
    in_vmem = pl.BlockSpec(memory_space=pltpu.VMEM)
    return pl.pallas_call(
        kernel,
        out_shape=(
            jax.ShapeDtypeStruct(leaf_rhs.shape, BF16),
            jax.ShapeDtypeStruct((1, levels, own_rows, right_sides), BF16),
        ),
        in_specs=[pl.BlockSpec(memory_space=pltpu.SMEM)] + [any_space] * 8,
        out_specs=(in_vmem, in_vmem),
        scratch_shapes=scratch,
        compiler_params=pltpu.CompilerParams(
            collective_id=0, has_side_effects=True, vmem_limit_bytes=56 * 2**20
        ),
    )(
        couple_mask,
        leaf_rhs,
        leaf_inverse,
        leaf_couple,
        leaf_diag,
        sep_rhs,
        sep_inverse,
        sep_couple,
        sep_diag,
    )


def solution(mesh):
    in_specs = (
        P(("layer", "plane"), None, None),
        P(("layer", "plane"), None, None),
        P(("layer", "plane"), None, None, None),
        P(("layer", "plane"), None),
        P(("layer", "plane"), None),
        P(None, "plane", None),
        P(None, "plane", None),
        P(None, None, "plane", None),
        P(None, "plane"),
    )
    out_specs = (P(("layer", "plane"), None, None), P("layer", None, "plane", None))
    return jax.shard_map(body, mesh=mesh, in_specs=in_specs, out_specs=out_specs, check_vma=False)
```

```python
import jax
import jax.numpy as jnp
from jax import lax
from jax.experimental import pallas as pl
from jax.experimental.pallas import tpu as pltpu
from jax.sharding import PartitionSpec as P

BF16 = jnp.bfloat16
F32 = jnp.float32
SIDE = 4
CORES = 2
EXTRA = 128
TILE = 256


def dot_rows(left, right):
    return lax.dot_general(left, right, (((1,), (1,)), ((), ())), preferred_element_type=F32)


def dot_cols(left, right):
    return lax.dot_general(left, right, (((1,), (0,)), ((), ())), preferred_element_type=F32)


def unit_lower(block, first_row):
    row_ids = first_row + lax.broadcasted_iota(jnp.int32, block.shape, 0)
    col_ids = lax.broadcasted_iota(jnp.int32, block.shape, 1)
    value = block.astype(F32)
    value = jnp.where(col_ids < row_ids, value, 0.0)
    return jnp.where(col_ids == row_ids, 1.0, value).astype(BF16)


def kernel(
    mask_ref,
    rhs_hbm,
    inverse_hbm,
    couple_hbm,
    diag_hbm,
    sep_rhs_hbm,
    sep_inverse_hbm,
    sep_couple_hbm,
    sep_diag_hbm,
    leaf_out,
    sep_out,
    rhs,
    inverse,
    couple,
    diag,
    sep_rhs,
    own_inverse,
    own_diag,
    mat0,
    mat1,
    mat2,
    leaf_y,
    leaf_ym,
    lower_t,
    part,
    paired,
    chip_sum,
    in1,
    sum1,
    in2,
    total,
    from_odd,
    out_total,
    to_two,
    from_one,
    to_three,
    from_two,
    sep_y,
    sep_z,
    answer,
    back,
    local_sem,
    couple_sem,
    g_send,
    g_recv,
    gc_send,
    gc_recv,
    r_send,
    r_recv,
    rc_send,
    rc_recv,
    a_send,
    a_recv,
    ac_send,
    ac_recv,
    odd_send,
    odd_recv,
    two_send,
    two_recv,
    three_send,
    three_recv,
    x_send,
    x_recv,
):
    blocks, blk, right_sides = rhs.shape
    own_rows = own_inverse.shape[0]
    size = own_inverse.shape[1]
    half = size // 2
    layer = lax.axis_index("layer")
    plane = lax.axis_index("plane")
    layers = lax.axis_size("layer")
    y = plane // (SIDE * CORES)
    x = (plane // CORES) % SIDE
    core = plane % CORES
    first_row = plane * own_rows

    def at_plane(y_at, x_at, core_at):
        return (layer, (y_at * SIDE + x_at) * CORES + core_at)

    def x_peer(d):
        return at_plane(y, (x + d) % SIDE, core)

    def y_peer(d):
        return at_plane((y + d) % SIDE, x, core)

    sibling = at_plane(y, x, 1 - core)

    is_one = layer % 2 == 0
    is_odd = layer % 2 == 1
    is_two = layer % 4 == 1
    is_three = layer == 3
    has_first = layer != 7
    has_second = jnp.logical_or(is_one, is_two)
    sep_of = [layer // 2, 4 + layer // 4, 6 + layer * 0]
    own_sep = jnp.where(is_one, layer // 2, jnp.where(is_two, 4 + layer // 4, 6))

    sends = []

    def remote(parts, when=None):
        def make():
            src, dst, send_sem, recv_sem, device = parts()
            return pltpu.make_async_remote_copy(
                src_ref=src,
                dst_ref=dst,
                send_sem=send_sem,
                recv_sem=recv_sem,
                device_id=device,
                device_id_type=pl.DeviceIdType.MESH,
            )

        make().start()
        sends.append((when, make))

    def arrived(dst, sem):
        pltpu.make_async_copy(dst, dst, sem).wait()

    barrier = pltpu.get_barrier_semaphore()
    peers = [sibling]
    for d in range(1, SIDE):
        peers += [x_peer(d), y_peer(d)]
    for d in range(1, 8):
        peers.append(((layer + d) % 8, plane))
    for peer in peers:
        pl.semaphore_signal(barrier, inc=1, device_id=peer, device_id_type=pl.DeviceIdType.MESH)

    local = [
        pltpu.make_async_copy(sep_inverse_hbm.at[own_sep], own_inverse, local_sem.at[0]),
        pltpu.make_async_copy(sep_diag_hbm, own_diag, local_sem.at[1]),
        pltpu.make_async_copy(sep_couple_hbm.at[own_sep, 0], mat1.at[y, x, core], local_sem.at[2]),
        pltpu.make_async_copy(sep_couple_hbm.at[own_sep, 1], mat2.at[y, x, core], local_sem.at[3]),
        pltpu.make_async_copy(inverse_hbm, inverse, local_sem.at[4]),
        pltpu.make_async_copy(rhs_hbm, rhs, local_sem.at[5]),
        pltpu.make_async_copy(diag_hbm, diag, local_sem.at[6]),
        pltpu.make_async_copy(sep_rhs_hbm.at[sep_of[0]], sep_rhs.at[0], local_sem.at[7]),
        pltpu.make_async_copy(sep_rhs_hbm.at[sep_of[1]], sep_rhs.at[1], local_sem.at[8]),
        pltpu.make_async_copy(sep_rhs_hbm.at[sep_of[2]], sep_rhs.at[2], local_sem.at[9]),
    ]
    for copy in local:
        copy.start()
    couples = []
    for k in range(3):
        couples.append(
            [
                pltpu.make_async_copy(
                    couple_hbm.at[b, k], couple.at[k, :, pl.ds(b * blk, blk)], couple_sem.at[k, b]
                )
                for b in range(blocks)
            ]
        )
        for copy in couples[k]:
            copy.start()

    def send_first(pick, width, sems, h, d, when):
        def parts():
            ref = pick(y, x, core, lanes(width, h))
            send, recv = sems(0, h, d - 1)
            return ref, ref, send, recv, x_peer(d) if h == 0 else y_peer(d)

        remote(parts, when)

    def send_second(pick, width, sems, h, d, when):
        def parts():
            everywhere = slice(None)
            if h == 0:
                ref = pick(y, everywhere, core, lanes(width, h))
            else:
                ref = pick(everywhere, x, core, lanes(width, h))
            send, recv = sems(1, h, d - 1)
            return ref, ref, send, recv, y_peer(d) if h == 0 else x_peer(d)

        remote(parts, when)

    def lanes(width, h):
        return pl.ds(0, half) if h == 0 else pl.ds(half, width - half)

    def gather_first(pick, width, sems, when=None):
        for h in range(2):
            for d in range(1, SIDE):
                send_first(pick, width, sems, h, d, when)

    def gather_second(pick, width, sems, when=None):
        for h in range(2):
            for d in range(1, SIDE):
                if h == 0:
                    ref = pick(y, (x - d + SIDE) % SIDE, core, lanes(width, h))
                else:
                    ref = pick((y - d + SIDE) % SIDE, x, core, lanes(width, h))
                arrived(ref, sems(0, h, d - 1)[1])
            for d in range(1, SIDE):
                send_second(pick, width, sems, h, d, when)

    def gather_third(pick, width, sems, c_sems, when=None):
        everywhere = slice(None)
        for h in range(2):
            for d in range(1, SIDE):
                if h == 0:
                    ref = pick((y - d + SIDE) % SIDE, everywhere, core, lanes(width, h))
                else:
                    ref = pick(everywhere, (x - d + SIDE) % SIDE, core, lanes(width, h))
                arrived(ref, sems(1, h, d - 1)[1])

        def parts():
            ref = pick(everywhere, everywhere, core, everywhere)
            return (ref, ref) + c_sems() + (sibling,)

        remote(parts, when)

    def gather_end(pick, c_recv):
        everywhere = slice(None)
        arrived(pick(everywhere, everywhere, 1 - core, everywhere), c_recv)

    mats = [mat0, mat1, mat2]
    uses = [has_first, has_second, is_one]

    def whole(m):
        return mats[m][:, :, :, :, 0:size].reshape(size, size)

    def mat_parts(m):
        return (
            lambda y_at, x_at, core_at, at: mats[m].at[y_at, x_at, core_at, :, at],
            mats[m].shape[-1],
            lambda *at: (g_send.at[(m,) + at], g_recv.at[(m,) + at]),
            lambda: (gc_send.at[m], gc_recv.at[m]),
        )

    def mat_first(m):
        @pl.when(uses[m])
        def _():
            gather_first(*mat_parts(m)[:3], uses[m])

    def mat_second(m):
        @pl.when(uses[m])
        def _():
            gather_second(*mat_parts(m)[:3], uses[m])

    def mat_third(m):
        @pl.when(uses[m])
        def _():
            gather_third(*mat_parts(m), uses[m])

    def mat_end(m):
        gather_end(mat_parts(m)[0], gc_recv.at[m])

    local[0].wait()
    local[1].wait()
    eye = lax.broadcasted_iota(jnp.int32, (own_rows, own_rows), 0) == lax.broadcasted_iota(
        jnp.int32, (own_rows, own_rows), 1
    )
    sep_rows = lax.broadcasted_iota(jnp.int32, own_diag.shape, 0) == own_sep
    diag_row = jnp.sum(jnp.where(sep_rows, own_diag[...], 0.0), axis=0, keepdims=True)
    diag_col = jnp.sum(jnp.where(eye, diag_row, 0.0), axis=1, keepdims=True)
    high = diag_col.astype(BF16).astype(F32)
    middle = (diag_col - high).astype(BF16).astype(F32)
    low = diag_col - high - middle
    lane = lax.broadcasted_iota(jnp.int32, (own_rows, EXTRA), 1)
    beside = jnp.where(
        lane == 0, high, jnp.where(lane == 1, middle, jnp.where(lane == 2, low, 0.0))
    ).astype(BF16)
    mat0[y, x, core, :, 0:size] = unit_lower(own_inverse[...], first_row)
    mat0[y, x, core, :, size:] = beside
    for i in range(4, 10):
        local[i].wait()

    def solve_leaf(b, _):
        lower = unit_lower(inverse[b], 0)
        lower_t[b] = lower.astype(F32).T.astype(BF16)
        rhs_t = rhs[b].T
        columns = pl.ds(pl.multiple_of(b * blk, blk), blk)
        leaf_y[:, columns] = dot_rows(rhs_t, lower).astype(BF16)
        return 0

    lax.fori_loop(0, blocks, solve_leaf, 0)

    pl.semaphore_wait(barrier, len(peers))
    mat_first(0)
    local[2].wait()
    local[3].wait()
    mat_first(1)
    mat_first(2)

    block_of = lax.broadcasted_iota(jnp.int32, (1, blocks * blk), 1) // blk

    def mask_lanes(k):
        result = jnp.zeros((1, blocks * blk), F32)
        for b in range(blocks):
            result = result + jnp.where(block_of == b, mask_ref[k, b].astype(F32), 0.0)
        return result

    def leaf_part(k):
        for copy in couples[k]:
            copy.wait()
        leaf_ym[...] = leaf_y[...] * mask_lanes(k).astype(BF16)
        rhs_t = sep_rhs[k].T
        adds = layer % (2 ** (k + 1)) == 0
        first = jnp.where(adds, first_row, size)

        def tile(i, _):
            start = pl.multiple_of(i * TILE, TILE)
            columns = pl.ds(start, TILE)
            rows_at = first + lax.broadcasted_iota(jnp.int32, (own_rows, TILE), 0)
            cols_at = start + lax.broadcasted_iota(jnp.int32, (own_rows, TILE), 1)
            place = jnp.where(rows_at == cols_at, 1.0, 0.0).astype(BF16)
            term = dot_cols(rhs_t, place) - dot_rows(leaf_ym[...], couple[k, columns, :])
            part[k, :, :, :, :, columns] = term.astype(BF16).reshape(
                part.shape[1:-1] + (TILE,)
            )
            return 0

        lax.fori_loop(0, size // TILE, tile, 0)
        remote(
            lambda: (
                part.at[k, 1 - core],
                paired.at[k],
                rc_send.at[k],
                rc_recv.at[k],
                sibling,
            )
        )

    def reduce_first(k):
        arrived(paired.at[k], rc_recv.at[k])
        chip_sum[k] = (part[k, core].astype(F32) + paired[k].astype(F32)).astype(BF16)
        for h in range(2):
            for d in range(1, SIDE):
                send_part(k, h, d)

    def send_part(k, h, d):
        def parts():
            if h == 0:
                ref = chip_sum.at[k, :, (x + d) % SIDE, :, pl.ds(0, half)]
            else:
                ref = chip_sum.at[k, (y + d) % SIDE, :, :, pl.ds(half, half)]
            return (
                ref,
                in1.at[k, h, d - 1],
                r_send.at[k, 0, h, d - 1],
                r_recv.at[k, 0, h, d - 1],
                x_peer(d) if h == 0 else y_peer(d),
            )

        remote(parts)

    def send_sum(k, h, d):
        remote(
            lambda: (
                sum1.at[k, h, ((y if h == 0 else x) + d) % SIDE],
                in2.at[k, h, d - 1],
                r_send.at[k, 1, h, d - 1],
                r_recv.at[k, 1, h, d - 1],
                y_peer(d) if h == 0 else x_peer(d),
            )
        )

    def reduce_second(k):
        for h in range(2):
            if h == 0:
                value = chip_sum[k, :, x, :, 0:half].astype(F32)
            else:
                value = chip_sum[k, y, :, :, half:].astype(F32)
            for d in range(1, SIDE):
                arrived(in1.at[k, h, d - 1], r_recv.at[k, 0, h, d - 1])
                value = value + in1[k, h, d - 1].astype(F32)
            sum1[k, h] = value.astype(BF16)
            for d in range(1, SIDE):
                send_sum(k, h, d)

    def reduce_end(k):
        for h in range(2):
            value = sum1[k, h, y if h == 0 else x].astype(F32)
            for d in range(1, SIDE):
                arrived(in2.at[k, h, d - 1], r_recv.at[k, 1, h, d - 1])
                value = value + in2[k, h, d - 1].astype(F32)
            total[k, :, h * half : (h + 1) * half] = value

        @pl.when(is_odd)
        def _():
            out_total[k] = total[k].astype(BF16)
            remote(
                lambda: (
                    out_total.at[k],
                    from_odd.at[k],
                    odd_send.at[k],
                    odd_recv.at[k],
                    ((layer + 7) % 8, plane),
                ),
                is_odd,
            )

    def whole_total(k):
        arrived(from_odd.at[k], odd_recv.at[k])
        return total[k] + from_odd[k].astype(F32)

    def divide(value):
        picks = jnp.where(
            lax.broadcasted_iota(jnp.int32, (value.shape[0], EXTRA), 1) < 3, 1.0, 0.0
        ).astype(BF16)
        parts = mat0[:, :, :, :, size:].reshape(size, EXTRA)
        return value / dot_rows(picks, parts)

    def forward(residual):
        solved = dot_rows(residual.astype(BF16), whole(0)).astype(BF16)
        sep_y[...] = solved
        sep_z[...] = divide(solved.astype(F32))

    two_of = (layer // 4) * 4 + 1
    two_slot = (layer % 4) // 2

    leaf_part(0)
    leaf_part(1)
    reduce_first(0)
    mat_second(0)
    leaf_part(2)
    reduce_first(1)
    mat_second(1)
    reduce_second(0)
    mat_third(0)
    reduce_end(0)
    reduce_second(1)
    mat_second(2)

    @pl.when(is_one)
    def _():
        residual = whole_total(0)
        mat_end(0)
        forward(residual)

    reduce_first(2)
    reduce_end(1)
    mat_third(1)
    reduce_second(2)

    def pass_up(k):
        to_two[k - 1] = (whole_total(k) - dot_rows(sep_y[...], whole(k))).astype(BF16)
        remote(
            lambda: (
                to_two.at[k - 1],
                from_one.at[two_slot, k - 1],
                two_send.at[k - 1],
                two_recv.at[two_slot, k - 1],
                (two_of, plane),
            ),
            is_one,
        )

    @pl.when(is_one)
    def _():
        mat_end(1)
        pass_up(1)

    reduce_end(2)
    mat_third(2)

    @pl.when(is_one)
    def _():
        mat_end(2)
        pass_up(2)

    @pl.when(is_two)
    def _():
        mat_end(0)
        mat_end(1)
        for slot in range(2):
            arrived(from_one.at[slot, 0], two_recv.at[slot, 0])
        forward(from_one[0, 0].astype(F32) + from_one[1, 0].astype(F32))
        term = dot_rows(sep_y[...], whole(1))
        for slot in range(2):
            arrived(from_one.at[slot, 1], two_recv.at[slot, 1])
        to_three[...] = (from_one[0, 1].astype(F32) + from_one[1, 1].astype(F32) - term).astype(
            BF16
        )
        remote(
            lambda: (
                to_three,
                from_two.at[layer // 4],
                three_send,
                three_recv.at[layer // 4],
                (3, plane),
            ),
            is_two,
        )

    def finish(k, target):
        answer[k, core, y, x] = dot_cols(target.astype(BF16), whole(0)).astype(BF16)

    def own_answer(k):
        return answer.at[k, core, y, x]

    def send_answer(k, slot, layer_to, when):
        remote(
            lambda: (
                own_answer(k),
                own_answer(k),
                x_send.at[slot],
                x_recv.at[k],
                (layer_to(), plane),
            ),
            when,
        )

    @pl.when(is_three)
    def _():
        mat_end(0)
        for slot in range(2):
            arrived(from_two.at[slot], three_recv.at[slot])
        forward(from_two[0].astype(F32) + from_two[1].astype(F32))
        finish(2, sep_z[...])
        for slot, layer_to in enumerate((1, 5, 2, 4, 0, 6, 7)):
            send_answer(2, slot, lambda layer_to=layer_to: layer_to, is_three)

    @pl.when(jnp.logical_not(is_three))
    def _():
        arrived(own_answer(2), x_recv.at[2])

    @pl.when(is_two)
    def _():
        finish(1, sep_z[...] - dot_cols(own_answer(2)[...], whole(1)))
        for slot, shift in enumerate((7, 1, 2)):
            send_answer(1, 7 + slot, lambda shift=shift: (layer + shift) % 8, is_two)

    def answer_parts(k):
        return (
            lambda y_at, x_at, core_at, at: answer.at[k, core_at, y_at, x_at, :, at],
            size,
            lambda *at: (a_send.at[(k,) + at], a_recv.at[(k,) + at]),
            lambda: (ac_send.at[k], ac_recv.at[k]),
        )

    def answer_first(k, when=None):
        gather_first(*answer_parts(k)[:3], when)

    def answer_second(k):
        gather_second(*answer_parts(k)[:3])

    def answer_third(k):
        gather_third(*answer_parts(k))

    def answer_end(k):
        gather_end(answer_parts(k)[0], ac_recv.at[k])

    answer_first(2)

    @pl.when(is_one)
    def _():
        sep_z[...] = sep_z[...] - dot_cols(own_answer(2)[...], whole(2))

    answer_second(2)

    @pl.when(jnp.logical_not(is_two))
    def _():
        arrived(own_answer(1), x_recv.at[1])

    @pl.when(is_one)
    def _():
        finish(0, sep_z[...] - dot_cols(own_answer(1)[...], whole(1)))
        send_answer(0, 10, lambda: layer + 1, is_one)
        answer_first(0, is_one)

    own_rows_at = jnp.where(
        first_row + lax.broadcasted_iota(jnp.int32, (own_rows, size), 0)
        == lax.broadcasted_iota(jnp.int32, (own_rows, size), 1),
        1.0,
        0.0,
    ).astype(BF16)

    side_cols = right_sides // CORES

    def rows_out(k, side):
        value = dot_rows(own_rows_at, answer[k, side].reshape(side_cols, size)).astype(BF16)
        sep_out[0, k, :, pl.ds(pl.multiple_of(side * side_cols, side_cols), side_cols)] = value

    def leaf_back(k):
        answer_end(k)
        rows_out(k, core)
        rows_out(k, 1 - core)
        leaf_ym[...] = jnp.broadcast_to(mask_lanes(k), leaf_ym.shape).astype(BF16)
        value = answer.at[k]

        def tile(i, _):
            columns = pl.ds(pl.multiple_of(i * TILE, TILE), TILE)
            term = dot_cols(
                value[...].reshape(right_sides, size), couple[k, :, columns]
            ) * leaf_ym[:, columns].astype(F32)
            back[:, columns] = back[:, columns] - term
            return 0

        lax.fori_loop(0, size // TILE, tile, 0)

    def leaf_end(side):
        rows = pl.ds(pl.multiple_of(side * side_cols, side_cols), side_cols)

        def tile(i, _):
            start = pl.multiple_of(i * TILE, TILE)
            columns = pl.ds(start, TILE)
            term = dot_cols(answer[0, side].reshape(side_cols, size), couple[0, :, columns])
            target = (back[rows, columns] - term * leaf_ym[0:1, columns].astype(F32)).astype(BF16)
            for j in range(TILE // blk):
                b = i * (TILE // blk) + j
                solved = dot_rows(lower_t[b], target[:, j * blk : (j + 1) * blk])
                leaf_out[b, :, rows] = solved.astype(BF16)
            return 0

        lax.fori_loop(0, size // TILE, tile, 0)

    answer_first(1)
    answer_third(2)

    @pl.when(is_odd)
    def _():
        arrived(own_answer(0), x_recv.at[0])
        answer_first(0, is_odd)

    diag_lanes = jnp.concatenate([diag[b : b + 1, :] for b in range(blocks)], axis=1)
    back[...] = leaf_y[...].astype(F32) / diag_lanes
    leaf_back(2)
    answer_second(1)
    answer_second(0)
    answer_third(1)
    leaf_back(1)
    answer_third(0)
    leaf_ym[0:16, :] = jnp.broadcast_to(mask_lanes(0), (16, size)).astype(BF16)
    rows_out(0, core)
    leaf_end(core)
    answer_end(0)
    leaf_end(1 - core)
    rows_out(0, 1 - core)

    for when, make in sends:
        if when is None:
            make().wait_send()
    for group in (has_first, has_second, is_one, is_odd, is_two, is_three):

        @pl.when(group)
        def _(group=group):
            for when, make in sends:
                if when is group:
                    make().wait_send()


def body(
    leaf_rhs,
    leaf_inverse,
    leaf_couple,
    couple_mask,
    leaf_diag,
    sep_rhs,
    sep_inverse,
    sep_couple,
    sep_diag,
):
    blocks, levels, size, blk = leaf_couple.shape
    right_sides = leaf_rhs.shape[2]
    own_rows = sep_rhs.shape[1]
    cols = right_sides // (SIDE * SIDE * CORES)
    half = size // 2
    grid = (SIDE, SIDE, CORES)
    sides = (CORES, SIDE, SIDE)
    vmem = pltpu.VMEM
    dma = pltpu.SemaphoreType.DMA
    hops = (levels, 2, 2, SIDE - 1)
    scratch = [
        vmem(leaf_rhs.shape, BF16),
        vmem(leaf_inverse.shape, BF16),
        vmem((levels, size, blocks * blk), BF16),
        vmem(leaf_diag.shape, F32),
        vmem((levels, own_rows, right_sides), BF16),
        vmem((own_rows, size), BF16),
        vmem(sep_diag.shape, F32),
        vmem(grid + (own_rows, size + EXTRA), BF16),
        vmem(grid + (own_rows, size), BF16),
        vmem(grid + (own_rows, size), BF16),
        vmem((right_sides, blocks * blk), BF16),
        vmem((right_sides, blocks * blk), BF16),
        vmem(leaf_inverse.shape, BF16),
        vmem((levels,) + sides + (cols, size), BF16),
        vmem((levels, SIDE, SIDE, cols, size), BF16),
        vmem((levels, SIDE, SIDE, cols, size), BF16),
        vmem((levels, 2, SIDE - 1, SIDE, cols, half), BF16),
        vmem((levels, 2, SIDE, cols, half), BF16),
        vmem((levels, 2, SIDE - 1, cols, half), BF16),
        vmem((levels, cols, size), F32),
        vmem((levels, cols, size), BF16),
        vmem((levels, cols, size), BF16),
        vmem((2, cols, size), BF16),
        vmem((2, 2, cols, size), BF16),
        vmem((cols, size), BF16),
        vmem((2, cols, size), BF16),
        vmem((cols, size), BF16),
        vmem((cols, size), F32),
        vmem((levels,) + sides + (cols, size), BF16),
        vmem((right_sides, blocks * blk), F32),
        dma((10,)),
        dma((levels, blocks)),
        dma(hops),
        dma(hops),
        dma((levels,)),
        dma((levels,)),
        dma(hops),
        dma(hops),
        dma((levels,)),
        dma((levels,)),
        dma(hops),
        dma(hops),
        dma((levels,)),
        dma((levels,)),
        dma((levels,)),
        dma((levels,)),
        dma((2,)),
        dma((2, 2)),
        dma,
        dma((2,)),
        dma((11,)),
        dma((levels,)),
    ]
    any_space = pl.BlockSpec(memory_space=pl.ANY)
    in_vmem = pl.BlockSpec(memory_space=pltpu.VMEM)
    return pl.pallas_call(
        kernel,
        out_shape=(
            jax.ShapeDtypeStruct(leaf_rhs.shape, BF16),
            jax.ShapeDtypeStruct((1, levels, own_rows, right_sides), BF16),
        ),
        in_specs=[pl.BlockSpec(memory_space=pltpu.SMEM)] + [any_space] * 8,
        out_specs=(in_vmem, in_vmem),
        scratch_shapes=scratch,
        compiler_params=pltpu.CompilerParams(
            collective_id=0, has_side_effects=True, vmem_limit_bytes=56 * 2**20
        ),
    )(
        couple_mask.T,
        leaf_rhs,
        leaf_inverse,
        leaf_couple,
        leaf_diag,
        sep_rhs,
        sep_inverse,
        sep_couple,
        sep_diag,
    )


def solution(mesh):
    in_specs = (
        P(("layer", "plane"), None, None),
        P(("layer", "plane"), None, None),
        P(("layer", "plane"), None, None, None),
        P(("layer", "plane"), None),
        P(("layer", "plane"), None),
        P(None, "plane", None),
        P(None, "plane", None),
        P(None, None, "plane", None),
        P(None, "plane"),
    )
    out_specs = (P(("layer", "plane"), None, None), P("layer", None, "plane", None))
    return jax.shard_map(body, mesh=mesh, in_specs=in_specs, out_specs=out_specs, check_vma=False)
```

```python
import jax
import jax.numpy as jnp
from jax import lax
from jax.experimental import pallas as pl
from jax.experimental.pallas import tpu as pltpu
from jax.sharding import PartitionSpec as P

BF16 = jnp.bfloat16
F32 = jnp.float32
SIDE = 4
CORES = 2
EXTRA = 128
TILE = 256


def dot_rows(left, right):
    return lax.dot_general(left, right, (((1,), (1,)), ((), ())), preferred_element_type=F32)


def dot_cols(left, right):
    return lax.dot_general(left, right, (((1,), (0,)), ((), ())), preferred_element_type=F32)


def unit_lower(block, first_row):
    row_ids = first_row + lax.broadcasted_iota(jnp.int32, block.shape, 0)
    col_ids = lax.broadcasted_iota(jnp.int32, block.shape, 1)
    value = block.astype(F32)
    value = jnp.where(col_ids < row_ids, value, 0.0)
    return jnp.where(col_ids == row_ids, 1.0, value).astype(BF16)


def kernel(
    mask_ref,
    rhs_hbm,
    inverse_hbm,
    couple_hbm,
    diag_hbm,
    sep_rhs_hbm,
    sep_inverse_hbm,
    sep_couple_hbm,
    sep_diag_hbm,
    leaf_out,
    sep_out,
    rhs,
    inverse,
    couple,
    diag,
    sep_rhs,
    own_inverse,
    own_diag,
    mat0,
    mat1,
    mat2,
    leaf_y,
    leaf_ym,
    lower_t,
    part,
    paired,
    chip_sum,
    in1,
    sum1,
    in2,
    total,
    from_odd,
    out_total,
    from_all,
    to_two,
    from_one,
    to_three,
    from_two,
    sep_y,
    helped_y,
    helped,
    carry,
    carried,
    sep_z,
    answer,
    back,
    local_sem,
    couple_sem,
    g_send,
    g_recv,
    gc_send,
    gc_recv,
    r_send,
    r_recv,
    rc_send,
    rc_recv,
    a_send,
    a_recv,
    ac_send,
    ac_recv,
    odd_send,
    odd_recv,
    two_send,
    two_recv,
    three_send,
    three_recv,
    all_send,
    all_recv,
    y_send,
    y_recv,
    carry_send,
    carry_recv,
    x_send,
    x_recv,
):
    blocks, blk, right_sides = rhs.shape
    own_rows = own_inverse.shape[0]
    size = own_inverse.shape[1]
    half = size // 2
    layer = lax.axis_index("layer")
    plane = lax.axis_index("plane")
    layers = lax.axis_size("layer")
    y = plane // (SIDE * CORES)
    x = (plane // CORES) % SIDE
    core = plane % CORES
    first_row = plane * own_rows

    def at_plane(y_at, x_at, core_at):
        return (layer, (y_at * SIDE + x_at) * CORES + core_at)

    def x_peer(d):
        return at_plane(y, (x + d) % SIDE, core)

    def y_peer(d):
        return at_plane((y + d) % SIDE, x, core)

    sibling = at_plane(y, x, 1 - core)

    is_one = layer % 2 == 0
    is_odd = layer % 2 == 1
    is_two = layer % 4 == 1
    is_three = layer == 3
    not_three = layer != 3
    is_helper = layer % 4 == 3
    is_seven = layer == 7
    has_first = layer != 7
    sep_of = [layer // 2, 4 + layer // 4, 6 + layer * 0]
    own_sep = jnp.where(is_one, layer // 2, jnp.where(is_two, 4 + layer // 4, 6))

    second_sep = jnp.where(is_helper, layer // 2, own_sep)
    second_block = jnp.where(is_helper, 1, 0)
    third_sep = ((layer + 1) % 8) // 2

    sends = []

    def remote(parts, when=None):
        def make():
            src, dst, send_sem, recv_sem, device = parts()
            return pltpu.make_async_remote_copy(
                src_ref=src,
                dst_ref=dst,
                send_sem=send_sem,
                recv_sem=recv_sem,
                device_id=device,
                device_id_type=pl.DeviceIdType.MESH,
            )

        make().start()
        sends.append((when, make))

    def only(when, act):
        if when is None:
            act()
        else:
            pl.when(when)(act)

    def arrived(dst, sem):
        pltpu.make_async_copy(dst, dst, sem).wait()

    barrier = pltpu.get_barrier_semaphore()
    peers = [sibling]
    for d in range(1, SIDE):
        peers += [x_peer(d), y_peer(d)]
    for d in range(1, 8):
        peers.append(((layer + d) % 8, plane))
    for peer in peers:
        pl.semaphore_signal(barrier, inc=1, device_id=peer, device_id_type=pl.DeviceIdType.MESH)

    local = [
        pltpu.make_async_copy(sep_inverse_hbm.at[own_sep], own_inverse, local_sem.at[0]),
        pltpu.make_async_copy(sep_diag_hbm, own_diag, local_sem.at[1]),
        pltpu.make_async_copy(
            sep_couple_hbm.at[second_sep, second_block], mat1.at[y, x, core], local_sem.at[2]
        ),
        pltpu.make_async_copy(
            sep_couple_hbm.at[third_sep, 1], mat2.at[y, x, core], local_sem.at[3]
        ),
        pltpu.make_async_copy(inverse_hbm, inverse, local_sem.at[4]),
        pltpu.make_async_copy(rhs_hbm, rhs, local_sem.at[5]),
        pltpu.make_async_copy(diag_hbm, diag, local_sem.at[6]),
        pltpu.make_async_copy(sep_rhs_hbm.at[sep_of[0]], sep_rhs.at[0], local_sem.at[7]),
        pltpu.make_async_copy(sep_rhs_hbm.at[sep_of[1]], sep_rhs.at[1], local_sem.at[8]),
        pltpu.make_async_copy(sep_rhs_hbm.at[sep_of[2]], sep_rhs.at[2], local_sem.at[9]),
    ]
    for copy in local:
        copy.start()
    couples = []
    for k in range(3):
        couples.append(
            [
                pltpu.make_async_copy(
                    couple_hbm.at[b, k], couple.at[k, :, pl.ds(b * blk, blk)], couple_sem.at[k, b]
                )
                for b in range(blocks)
            ]
        )
        for copy in couples[k]:
            copy.start()

    def send_first(pick, width, sems, h, d, when):
        def parts():
            ref = pick(y, x, core, lanes(width, h))
            send, recv = sems(0, h, d - 1)
            return ref, ref, send, recv, x_peer(d) if h == 0 else y_peer(d)

        remote(parts, when)

    def send_second(pick, width, sems, h, d, when):
        def parts():
            everywhere = slice(None)
            if h == 0:
                ref = pick(y, everywhere, core, lanes(width, h))
            else:
                ref = pick(everywhere, x, core, lanes(width, h))
            send, recv = sems(1, h, d - 1)
            return ref, ref, send, recv, y_peer(d) if h == 0 else x_peer(d)

        remote(parts, when)

    def lanes(width, h):
        return pl.ds(0, half) if h == 0 else pl.ds(half, width - half)

    def gather_first(pick, width, sems, when=None):
        for h in range(2):
            for d in range(1, SIDE):
                send_first(pick, width, sems, h, d, when)

    def gather_second(pick, width, sems, when=None):
        for h in range(2):
            for d in range(1, SIDE):
                if h == 0:
                    ref = pick(y, (x - d + SIDE) % SIDE, core, lanes(width, h))
                else:
                    ref = pick((y - d + SIDE) % SIDE, x, core, lanes(width, h))
                arrived(ref, sems(0, h, d - 1)[1])
            for d in range(1, SIDE):
                send_second(pick, width, sems, h, d, when)

    def gather_third(pick, width, sems, c_sems, when=None):
        everywhere = slice(None)
        for h in range(2):
            for d in range(1, SIDE):
                if h == 0:
                    ref = pick((y - d + SIDE) % SIDE, everywhere, core, lanes(width, h))
                else:
                    ref = pick(everywhere, (x - d + SIDE) % SIDE, core, lanes(width, h))
                arrived(ref, sems(1, h, d - 1)[1])

        def parts():
            ref = pick(everywhere, everywhere, core, everywhere)
            return (ref, ref) + c_sems() + (sibling,)

        remote(parts, when)

    def gather_end(pick, c_recv):
        everywhere = slice(None)
        arrived(pick(everywhere, everywhere, 1 - core, everywhere), c_recv)

    mats = [mat0, mat1, mat2]
    uses = [has_first, None, is_helper]

    def whole(m):
        return mats[m][:, :, :, :, 0:size].reshape(size, size)

    def mat_parts(m):
        return (
            lambda y_at, x_at, core_at, at: mats[m].at[y_at, x_at, core_at, :, at],
            mats[m].shape[-1],
            lambda *at: (g_send.at[(m,) + at], g_recv.at[(m,) + at]),
            lambda: (gc_send.at[m], gc_recv.at[m]),
        )

    def mat_first(m):
        only(uses[m], lambda: gather_first(*mat_parts(m)[:3], uses[m]))

    def mat_second(m):
        only(uses[m], lambda: gather_second(*mat_parts(m)[:3], uses[m]))

    def mat_third(m):
        only(uses[m], lambda: gather_third(*mat_parts(m), uses[m]))

    def mat_end(m):
        gather_end(mat_parts(m)[0], gc_recv.at[m])

    local[0].wait()
    local[1].wait()
    eye = lax.broadcasted_iota(jnp.int32, (own_rows, own_rows), 0) == lax.broadcasted_iota(
        jnp.int32, (own_rows, own_rows), 1
    )
    sep_rows = lax.broadcasted_iota(jnp.int32, own_diag.shape, 0) == own_sep
    diag_row = jnp.sum(jnp.where(sep_rows, own_diag[...], 0.0), axis=0, keepdims=True)
    diag_col = jnp.sum(jnp.where(eye, diag_row, 0.0), axis=1, keepdims=True)
    high = diag_col.astype(BF16).astype(F32)
    middle = (diag_col - high).astype(BF16).astype(F32)
    low = diag_col - high - middle
    lane = lax.broadcasted_iota(jnp.int32, (own_rows, EXTRA), 1)
    beside = jnp.where(
        lane == 0, high, jnp.where(lane == 1, middle, jnp.where(lane == 2, low, 0.0))
    ).astype(BF16)
    mat0[y, x, core, :, 0:size] = unit_lower(own_inverse[...], first_row)
    mat0[y, x, core, :, size:] = beside
    for i in range(4, 10):
        local[i].wait()

    def solve_leaf(b, _):
        lower = unit_lower(inverse[b], 0)
        lower_t[b] = lower.astype(F32).T.astype(BF16)
        rhs_t = rhs[b].T
        columns = pl.ds(pl.multiple_of(b * blk, blk), blk)
        leaf_y[:, columns] = dot_rows(rhs_t, lower).astype(BF16)
        return 0

    lax.fori_loop(0, blocks, solve_leaf, 0)

    pl.semaphore_wait(barrier, len(peers))
    mat_first(0)
    local[2].wait()
    local[3].wait()
    mat_first(1)
    mat_first(2)

    block_of = lax.broadcasted_iota(jnp.int32, (1, blocks * blk), 1) // blk

    def mask_lanes(k):
        result = jnp.zeros((1, blocks * blk), F32)
        for b in range(blocks):
            result = result + jnp.where(block_of == b, mask_ref[k, b].astype(F32), 0.0)
        return result

    def leaf_part(k):
        for copy in couples[k]:
            copy.wait()
        leaf_ym[...] = leaf_y[...] * mask_lanes(k).astype(BF16)
        rhs_t = sep_rhs[k].T
        adds = layer % (2 ** (k + 1)) == 0
        first = jnp.where(adds, first_row, size)

        def tile(i, _):
            start = pl.multiple_of(i * TILE, TILE)
            columns = pl.ds(start, TILE)
            rows_at = first + lax.broadcasted_iota(jnp.int32, (own_rows, TILE), 0)
            cols_at = start + lax.broadcasted_iota(jnp.int32, (own_rows, TILE), 1)
            place = jnp.where(rows_at == cols_at, 1.0, 0.0).astype(BF16)
            term = dot_cols(rhs_t, place) - dot_rows(leaf_ym[...], couple[k, columns, :])
            part[k, :, :, :, :, columns] = term.astype(BF16).reshape(
                part.shape[1:-1] + (TILE,)
            )
            return 0

        lax.fori_loop(0, size // TILE, tile, 0)
        remote(
            lambda: (
                part.at[k, 1 - core],
                paired.at[k],
                rc_send.at[k],
                rc_recv.at[k],
                sibling,
            )
        )

    def reduce_first(k):
        arrived(paired.at[k], rc_recv.at[k])
        chip_sum[k] = (part[k, core].astype(F32) + paired[k].astype(F32)).astype(BF16)
        for h in range(2):
            for d in range(1, SIDE):
                send_part(k, h, d)

    def send_part(k, h, d):
        def parts():
            if h == 0:
                ref = chip_sum.at[k, :, (x + d) % SIDE, :, pl.ds(0, half)]
            else:
                ref = chip_sum.at[k, (y + d) % SIDE, :, :, pl.ds(half, half)]
            return (
                ref,
                in1.at[k, h, d - 1],
                r_send.at[k, 0, h, d - 1],
                r_recv.at[k, 0, h, d - 1],
                x_peer(d) if h == 0 else y_peer(d),
            )

        remote(parts)

    def send_sum(k, h, d):
        remote(
            lambda: (
                sum1.at[k, h, ((y if h == 0 else x) + d) % SIDE],
                in2.at[k, h, d - 1],
                r_send.at[k, 1, h, d - 1],
                r_recv.at[k, 1, h, d - 1],
                y_peer(d) if h == 0 else x_peer(d),
            )
        )

    def reduce_second(k):
        for h in range(2):
            if h == 0:
                value = chip_sum[k, :, x, :, 0:half].astype(F32)
            else:
                value = chip_sum[k, y, :, :, half:].astype(F32)
            for d in range(1, SIDE):
                arrived(in1.at[k, h, d - 1], r_recv.at[k, 0, h, d - 1])
                value = value + in1[k, h, d - 1].astype(F32)
            sum1[k, h] = value.astype(BF16)
            for d in range(1, SIDE):
                send_sum(k, h, d)

    def reduce_end(k):
        for h in range(2):
            value = sum1[k, h, y if h == 0 else x].astype(F32)
            for d in range(1, SIDE):
                arrived(in2.at[k, h, d - 1], r_recv.at[k, 1, h, d - 1])
                value = value + in2[k, h, d - 1].astype(F32)
            total[k, :, h * half : (h + 1) * half] = value

        def send():
            out_total[k] = total[k].astype(BF16)
            if k < 2:
                remote(
                    lambda: (
                        out_total.at[k],
                        from_odd.at[k],
                        odd_send.at[k],
                        odd_recv.at[k],
                        ((layer + 7) % 8, plane),
                    ),
                    is_odd,
                )
            else:
                remote(
                    lambda: (
                        out_total.at[k],
                        from_all.at[slot_of_all()],
                        all_send,
                        all_recv.at[slot_of_all()],
                        (3, plane),
                    ),
                    not_three,
                )

        pl.when(is_odd if k < 2 else not_three)(send)

    def slot_of_all():
        return layer - jnp.where(layer > 3, 1, 0)

    def whole_total(k):
        arrived(from_odd.at[k], odd_recv.at[k])
        return total[k] + from_odd[k].astype(F32)

    def divide(value):
        picks = jnp.where(
            lax.broadcasted_iota(jnp.int32, (value.shape[0], EXTRA), 1) < 3, 1.0, 0.0
        ).astype(BF16)
        parts = mat0[:, :, :, :, size:].reshape(size, EXTRA)
        return value / dot_rows(picks, parts)

    def forward(residual):
        solved = dot_rows(residual.astype(BF16), whole(0)).astype(BF16)
        sep_y[...] = solved
        sep_z[...] = divide(solved.astype(F32))

    two_of = (layer // 4) * 4 + 1
    two_slot = (layer % 4) // 2

    leaf_part(0)
    leaf_part(1)
    reduce_first(0)
    mat_second(0)
    leaf_part(2)
    reduce_first(1)
    mat_second(1)
    reduce_second(0)
    mat_third(0)
    reduce_end(0)
    reduce_second(1)
    mat_second(2)

    @pl.when(is_one)
    def _():
        residual = whole_total(0)
        mat_end(0)
        forward(residual)
        remote(
            lambda: (
                sep_y,
                helped_y.at[1 - two_slot],
                y_send,
                y_recv.at[1 - two_slot],
                ((layer + 7 + 2 * two_slot) % 8, plane),
            ),
            is_one,
        )

    reduce_first(2)
    reduce_end(1)
    mat_third(1)

    @pl.when(is_one)
    def _():
        mat_end(1)
        to_two[...] = (whole_total(1) - dot_rows(sep_y[...], whole(1))).astype(BF16)
        remote(
            lambda: (
                to_two,
                from_one.at[two_slot],
                two_send,
                two_recv.at[two_slot],
                (two_of, plane),
            ),
            is_one,
        )

    reduce_second(2)
    mat_third(2)
    reduce_end(2)

    @pl.when(is_helper)
    def _():
        mat_end(1)
        mat_end(2)
        for slot in range(2):
            arrived(helped_y.at[slot], y_recv.at[slot])
        helped[...] = dot_rows(helped_y[0], whole(1)) + dot_rows(helped_y[1], whole(2))

    def send_three(slot, when):
        remote(
            lambda: (
                to_three,
                from_two.at[slot()],
                three_send,
                three_recv.at[slot()],
                (3, plane),
            ),
            when,
        )

    @pl.when(is_seven)
    def _():
        to_three[...] = helped[...].astype(BF16)
        send_three(lambda: 2, is_seven)

    @pl.when(is_two)
    def _():
        mat_end(0)
        mat_end(1)
        for slot in range(2):
            arrived(from_one.at[slot], two_recv.at[slot])
        forward(from_one[0].astype(F32) + from_one[1].astype(F32))
        to_three[...] = dot_rows(sep_y[...], whole(1)).astype(BF16)
        send_three(lambda: layer // 4, is_two)

    def finish(k, target):
        answer[k, core, y, x] = dot_cols(target.astype(BF16), whole(0)).astype(BF16)

    def own_answer(k):
        return answer.at[k, core, y, x]

    def send_answer(k, slot, layer_to, when):
        remote(
            lambda: (
                own_answer(k),
                own_answer(k),
                x_send.at[slot],
                x_recv.at[k],
                (layer_to(), plane),
            ),
            when,
        )

    @pl.when(is_three)
    def _():
        mat_end(0)
        residual = total[2] - helped[...]
        for slot in range(7):
            arrived(from_all.at[slot], all_recv.at[slot])
            residual = residual + from_all[slot].astype(F32)
        for slot in (2, 0, 1):
            arrived(from_two.at[slot], three_recv.at[slot])
            residual = residual - from_two[slot].astype(F32)
        forward(residual)
        finish(2, sep_z[...])
        for slot, layer_to in enumerate((1, 5, 7, 2, 4, 0, 6)):
            send_answer(2, slot, lambda layer_to=layer_to: layer_to, is_three)

    def send_carry(slot):
        remote(
            lambda: (
                carry.at[slot],
                carried,
                carry_send.at[slot],
                carry_recv,
                ((layer + 7 + 2 * slot) % 8, plane),
            ),
            is_helper,
        )

    @pl.when(jnp.logical_not(is_three))
    def _():
        arrived(own_answer(2), x_recv.at[2])

    @pl.when(is_two)
    def _():
        finish(1, sep_z[...] - dot_cols(own_answer(2)[...], whole(1)))
        for slot, shift in enumerate((7, 1, 2)):
            send_answer(1, 7 + slot, lambda shift=shift: (layer + shift) % 8, is_two)

    def answer_parts(k):
        return (
            lambda y_at, x_at, core_at, at: answer.at[k, core_at, y_at, x_at, :, at],
            size,
            lambda *at: (a_send.at[(k,) + at], a_recv.at[(k,) + at]),
            lambda: (ac_send.at[k], ac_recv.at[k]),
        )

    def answer_first(k, when=None):
        gather_first(*answer_parts(k)[:3], when)

    def answer_second(k):
        gather_second(*answer_parts(k)[:3])

    def answer_third(k):
        gather_third(*answer_parts(k))

    def answer_end(k):
        gather_end(answer_parts(k)[0], ac_recv.at[k])

    @pl.when(is_helper)
    def _():
        for slot in range(2):
            term = dot_cols(own_answer(2)[...], whole(1 + slot))
            carry[slot] = term.astype(BF16)
            send_carry(slot)

    answer_first(2)
    answer_second(2)

    @pl.when(jnp.logical_not(is_two))
    def _():
        arrived(own_answer(1), x_recv.at[1])

    @pl.when(is_one)
    def _():
        term = dot_cols(own_answer(1)[...], whole(1))
        arrived(carried, carry_recv)
        finish(0, sep_z[...] - carried[...].astype(F32) - term)
        send_answer(0, 10, lambda: layer + 1, is_one)
        answer_first(0, is_one)

    own_rows_at = jnp.where(
        first_row + lax.broadcasted_iota(jnp.int32, (own_rows, size), 0)
        == lax.broadcasted_iota(jnp.int32, (own_rows, size), 1),
        1.0,
        0.0,
    ).astype(BF16)

    side_cols = right_sides // CORES

    def rows_out(k, side):
        value = dot_rows(own_rows_at, answer[k, side].reshape(side_cols, size)).astype(BF16)
        sep_out[0, k, :, pl.ds(pl.multiple_of(side * side_cols, side_cols), side_cols)] = value

    def leaf_back(k):
        answer_end(k)
        rows_out(k, core)
        rows_out(k, 1 - core)
        leaf_ym[...] = jnp.broadcast_to(mask_lanes(k), leaf_ym.shape).astype(BF16)
        value = answer.at[k]

        def tile(i, _):
            columns = pl.ds(pl.multiple_of(i * TILE, TILE), TILE)
            term = dot_cols(
                value[...].reshape(right_sides, size), couple[k, :, columns]
            ) * leaf_ym[:, columns].astype(F32)
            back[:, columns] = back[:, columns] - term
            return 0

        lax.fori_loop(0, size // TILE, tile, 0)

    def leaf_end(side):
        rows = pl.ds(pl.multiple_of(side * side_cols, side_cols), side_cols)

        def tile(i, _):
            start = pl.multiple_of(i * TILE, TILE)
            columns = pl.ds(start, TILE)
            term = dot_cols(answer[0, side].reshape(side_cols, size), couple[0, :, columns])
            target = (back[rows, columns] - term * leaf_ym[0:1, columns].astype(F32)).astype(BF16)
            for j in range(TILE // blk):
                b = i * (TILE // blk) + j
                solved = dot_rows(lower_t[b], target[:, j * blk : (j + 1) * blk])
                leaf_out[b, :, rows] = solved.astype(BF16)
            return 0

        lax.fori_loop(0, size // TILE, tile, 0)

    answer_first(1)
    answer_third(2)

    @pl.when(is_odd)
    def _():
        arrived(own_answer(0), x_recv.at[0])
        answer_first(0, is_odd)

    diag_lanes = jnp.concatenate([diag[b : b + 1, :] for b in range(blocks)], axis=1)
    back[...] = leaf_y[...].astype(F32) / diag_lanes
    leaf_back(2)
    answer_second(1)
    answer_second(0)
    answer_third(1)
    leaf_back(1)
    answer_third(0)
    leaf_ym[0:16, :] = jnp.broadcast_to(mask_lanes(0), (16, size)).astype(BF16)
    rows_out(0, core)
    leaf_end(core)
    answer_end(0)
    leaf_end(1 - core)
    rows_out(0, 1 - core)

    for when, make in sends:
        if when is None:
            make().wait_send()
    for group in (has_first, is_helper, is_one, is_odd, is_two, is_three, not_three, is_seven):

        @pl.when(group)
        def _(group=group):
            for when, make in sends:
                if when is group:
                    make().wait_send()


def copy_kernel(leaf_ref, sep_ref, leaf_out, sep_out, sems):
    blocks = leaf_ref.shape[0]
    copies = [
        pltpu.make_async_copy(leaf_ref.at[b], leaf_out.at[b], sems.at[b]) for b in range(blocks)
    ]
    copies.append(pltpu.make_async_copy(sep_ref, sep_out, sems.at[blocks]))
    for copy in copies:
        copy.start()
    for copy in copies:
        copy.wait()


def body(
    leaf_rhs,
    leaf_inverse,
    leaf_couple,
    couple_mask,
    leaf_diag,
    sep_rhs,
    sep_inverse,
    sep_couple,
    sep_diag,
):
    blocks, levels, size, blk = leaf_couple.shape
    right_sides = leaf_rhs.shape[2]
    own_rows = sep_rhs.shape[1]
    cols = right_sides // (SIDE * SIDE * CORES)
    half = size // 2
    grid = (SIDE, SIDE, CORES)
    sides = (CORES, SIDE, SIDE)
    vmem = pltpu.VMEM
    dma = pltpu.SemaphoreType.DMA
    hops = (levels, 2, 2, SIDE - 1)
    scratch = [
        vmem(leaf_rhs.shape, BF16),
        vmem(leaf_inverse.shape, BF16),
        vmem((levels, size, blocks * blk), BF16),
        vmem(leaf_diag.shape, F32),
        vmem((levels, own_rows, right_sides), BF16),
        vmem((own_rows, size), BF16),
        vmem(sep_diag.shape, F32),
        vmem(grid + (own_rows, size + EXTRA), BF16),
        vmem(grid + (own_rows, size), BF16),
        vmem(grid + (own_rows, size), BF16),
        vmem((right_sides, blocks * blk), BF16),
        vmem((right_sides, blocks * blk), BF16),
        vmem(leaf_inverse.shape, BF16),
        vmem((levels,) + sides + (cols, size), BF16),
        vmem((levels, SIDE, SIDE, cols, size), BF16),
        vmem((levels, SIDE, SIDE, cols, size), BF16),
        vmem((levels, 2, SIDE - 1, SIDE, cols, half), BF16),
        vmem((levels, 2, SIDE, cols, half), BF16),
        vmem((levels, 2, SIDE - 1, cols, half), BF16),
        vmem((levels, cols, size), F32),
        vmem((levels, cols, size), BF16),
        vmem((levels, cols, size), BF16),
        vmem((7, cols, size), BF16),
        vmem((cols, size), BF16),
        vmem((2, cols, size), BF16),
        vmem((cols, size), BF16),
        vmem((3, cols, size), BF16),
        vmem((cols, size), BF16),
        vmem((2, cols, size), BF16),
        vmem((cols, size), F32),
        vmem((2, cols, size), BF16),
        vmem((cols, size), BF16),
        vmem((cols, size), F32),
        vmem((levels,) + sides + (cols, size), BF16),
        vmem((right_sides, blocks * blk), F32),
        dma((10,)),
        dma((levels, blocks)),
        dma(hops),
        dma(hops),
        dma((levels,)),
        dma((levels,)),
        dma(hops),
        dma(hops),
        dma((levels,)),
        dma((levels,)),
        dma(hops),
        dma(hops),
        dma((levels,)),
        dma((levels,)),
        dma((2,)),
        dma((2,)),
        dma,
        dma((2,)),
        dma,
        dma((3,)),
        dma,
        dma((7,)),
        dma,
        dma((2,)),
        dma((2,)),
        dma,
        dma((11,)),
        dma((levels,)),
    ]
    any_space = pl.BlockSpec(memory_space=pl.ANY)
    in_vmem = pl.BlockSpec(memory_space=pltpu.VMEM)
    outs = pl.pallas_call(
        kernel,
        out_shape=(
            jax.ShapeDtypeStruct(leaf_rhs.shape, BF16),
            jax.ShapeDtypeStruct((1, levels, own_rows, right_sides), BF16),
        ),
        in_specs=[pl.BlockSpec(memory_space=pltpu.SMEM)] + [any_space] * 8,
        out_specs=(in_vmem, in_vmem),
        scratch_shapes=scratch,
        compiler_params=pltpu.CompilerParams(
            collective_id=0, has_side_effects=True, vmem_limit_bytes=56 * 2**20
        ),
    )(
        couple_mask.T,
        leaf_rhs,
        leaf_inverse,
        leaf_couple,
        leaf_diag,
        sep_rhs,
        sep_inverse,
        sep_couple,
        sep_diag,
    )
    return pl.pallas_call(
        copy_kernel,
        out_shape=tuple(jax.ShapeDtypeStruct(out.shape, out.dtype) for out in outs),
        in_specs=[any_space] * 2,
        out_specs=(any_space, any_space),
        scratch_shapes=[dma((blocks + 1,))],
    )(*outs)


def solution(mesh):
    in_specs = (
        P(("layer", "plane"), None, None),
        P(("layer", "plane"), None, None),
        P(("layer", "plane"), None, None, None),
        P(("layer", "plane"), None),
        P(("layer", "plane"), None),
        P(None, "plane", None),
        P(None, "plane", None),
        P(None, None, "plane", None),
        P(None, "plane"),
    )
    out_specs = (P(("layer", "plane"), None, None), P("layer", None, "plane", None))
    return jax.shard_map(body, mesh=mesh, in_specs=in_specs, out_specs=out_specs, check_vma=False)
```

```python
import jax
import jax.numpy as jnp
from jax import lax
from jax.experimental import pallas as pl
from jax.experimental.pallas import tpu as pltpu
from jax.sharding import PartitionSpec as P

BF16 = jnp.bfloat16
F32 = jnp.float32
SIDE = 4
CORES = 2
EXTRA = 128
TILE = 256


def dot_rows(left, right):
    return lax.dot_general(left, right, (((1,), (1,)), ((), ())), preferred_element_type=F32)


def dot_cols(left, right):
    return lax.dot_general(left, right, (((1,), (0,)), ((), ())), preferred_element_type=F32)


def unit_lower(block, first_row):
    row_ids = first_row + lax.broadcasted_iota(jnp.int32, block.shape, 0)
    col_ids = lax.broadcasted_iota(jnp.int32, block.shape, 1)
    value = block.astype(F32)
    value = jnp.where(col_ids < row_ids, value, 0.0)
    return jnp.where(col_ids == row_ids, 1.0, value).astype(BF16)


def kernel(
    mask_ref,
    rhs_hbm,
    inverse_hbm,
    couple_hbm,
    diag_hbm,
    sep_rhs_hbm,
    sep_inverse_hbm,
    sep_couple_hbm,
    sep_diag_hbm,
    leaf_out,
    sep_out,
    rhs,
    inverse,
    couple,
    diag,
    sep_rhs,
    own_inverse,
    own_diag,
    mat0,
    mat1,
    mat2,
    leaf_y,
    leaf_ym,
    lower_t,
    part,
    paired,
    chip_sum,
    in1,
    sum1,
    in2,
    total,
    from_odd,
    out_total,
    from_all,
    to_two,
    from_one,
    to_three,
    from_two,
    sep_y,
    helped_y,
    helped,
    carry,
    carried,
    sep_z,
    answer,
    back,
    local_sem,
    couple_sem,
    g_send,
    g_recv,
    gc_send,
    gc_recv,
    r_send,
    r_recv,
    rc_send,
    rc_recv,
    a_send,
    a_recv,
    ac_send,
    ac_recv,
    odd_send,
    odd_recv,
    two_send,
    two_recv,
    three_send,
    three_recv,
    all_send,
    all_recv,
    y_send,
    y_recv,
    carry_send,
    carry_recv,
    x_send,
    x_recv,
):
    blocks, blk, right_sides = rhs.shape
    own_rows = own_inverse.shape[0]
    size = own_inverse.shape[1]
    half = size // 2
    layer = lax.axis_index("layer")
    plane = lax.axis_index("plane")
    layers = lax.axis_size("layer")
    y = plane // (SIDE * CORES)
    x = (plane // CORES) % SIDE
    core = plane % CORES
    first_row = plane * own_rows

    def at_plane(y_at, x_at, core_at):
        return (layer, (y_at * SIDE + x_at) * CORES + core_at)

    def x_peer(d):
        return at_plane(y, (x + d) % SIDE, core)

    def y_peer(d):
        return at_plane((y + d) % SIDE, x, core)

    sibling = at_plane(y, x, 1 - core)

    is_one = layer % 2 == 0
    is_odd = layer % 2 == 1
    is_two = layer % 4 == 1
    is_three = layer == 3
    not_three = layer != 3
    is_helper = layer % 4 == 3
    is_seven = layer == 7
    has_first = layer != 7
    sep_of = [layer // 2, 4 + layer // 4, 6 + layer * 0]
    own_sep = jnp.where(is_one, layer // 2, jnp.where(is_two, 4 + layer // 4, 6))

    second_sep = jnp.where(is_helper, layer // 2, own_sep)
    second_block = jnp.where(is_helper, 1, 0)
    third_sep = ((layer + 1) % 8) // 2

    sends = []

    def remote(parts, when=None):
        def make():
            src, dst, send_sem, recv_sem, device = parts()
            return pltpu.make_async_remote_copy(
                src_ref=src,
                dst_ref=dst,
                send_sem=send_sem,
                recv_sem=recv_sem,
                device_id=device,
                device_id_type=pl.DeviceIdType.MESH,
            )

        make().start()
        sends.append((when, make))

    def only(when, act):
        if when is None:
            act()
        else:
            pl.when(when)(act)

    def arrived(dst, sem):
        pltpu.make_async_copy(dst, dst, sem).wait()

    barrier = pltpu.get_barrier_semaphore()
    peers = [sibling]
    for d in range(1, SIDE):
        peers += [x_peer(d), y_peer(d)]
    for d in range(1, 8):
        peers.append(((layer + d) % 8, plane))
    for peer in peers:
        pl.semaphore_signal(barrier, inc=1, device_id=peer, device_id_type=pl.DeviceIdType.MESH)

    local = [
        pltpu.make_async_copy(sep_inverse_hbm.at[own_sep], own_inverse, local_sem.at[0]),
        pltpu.make_async_copy(sep_diag_hbm, own_diag, local_sem.at[1]),
        pltpu.make_async_copy(
            sep_couple_hbm.at[second_sep, second_block], mat1.at[y, x, core], local_sem.at[2]
        ),
        pltpu.make_async_copy(
            sep_couple_hbm.at[third_sep, 1], mat2.at[y, x, core], local_sem.at[3]
        ),
        pltpu.make_async_copy(inverse_hbm, inverse, local_sem.at[4]),
        pltpu.make_async_copy(rhs_hbm, rhs, local_sem.at[5]),
        pltpu.make_async_copy(diag_hbm, diag, local_sem.at[6]),
        pltpu.make_async_copy(sep_rhs_hbm.at[sep_of[0]], sep_rhs.at[0], local_sem.at[7]),
        pltpu.make_async_copy(sep_rhs_hbm.at[sep_of[1]], sep_rhs.at[1], local_sem.at[8]),
        pltpu.make_async_copy(sep_rhs_hbm.at[sep_of[2]], sep_rhs.at[2], local_sem.at[9]),
    ]
    for copy in local:
        copy.start()
    couples = []
    for k in range(3):
        couples.append(
            [
                pltpu.make_async_copy(
                    couple_hbm.at[b, k], couple.at[k, :, pl.ds(b * blk, blk)], couple_sem.at[k, b]
                )
                for b in range(blocks)
            ]
        )
        for copy in couples[k]:
            copy.start()

    def send_first(pick, width, sems, h, d, when):
        def parts():
            ref = pick(y, x, core, lanes(width, h))
            send, recv = sems(0, h, d - 1)
            return ref, ref, send, recv, x_peer(d) if h == 0 else y_peer(d)

        remote(parts, when)

    def send_second(pick, width, sems, h, d, when):
        def parts():
            everywhere = slice(None)
            if h == 0:
                ref = pick(y, everywhere, core, lanes(width, h))
            else:
                ref = pick(everywhere, x, core, lanes(width, h))
            send, recv = sems(1, h, d - 1)
            return ref, ref, send, recv, y_peer(d) if h == 0 else x_peer(d)

        remote(parts, when)

    def lanes(width, h):
        return pl.ds(0, half) if h == 0 else pl.ds(half, width - half)

    def gather_first(pick, width, sems, when=None):
        for h in range(2):
            for d in range(1, SIDE):
                send_first(pick, width, sems, h, d, when)

    def gather_second(pick, width, sems, when=None):
        for h in range(2):
            for d in range(1, SIDE):
                if h == 0:
                    ref = pick(y, (x - d + SIDE) % SIDE, core, lanes(width, h))
                else:
                    ref = pick((y - d + SIDE) % SIDE, x, core, lanes(width, h))
                arrived(ref, sems(0, h, d - 1)[1])
            for d in range(1, SIDE):
                send_second(pick, width, sems, h, d, when)

    def gather_third(pick, width, sems, c_sems, when=None):
        everywhere = slice(None)
        for h in range(2):
            for d in range(1, SIDE):
                if h == 0:
                    ref = pick((y - d + SIDE) % SIDE, everywhere, core, lanes(width, h))
                else:
                    ref = pick(everywhere, (x - d + SIDE) % SIDE, core, lanes(width, h))
                arrived(ref, sems(1, h, d - 1)[1])

        def parts():
            ref = pick(everywhere, everywhere, core, everywhere)
            return (ref, ref) + c_sems() + (sibling,)

        remote(parts, when)

    def gather_end(pick, c_recv):
        everywhere = slice(None)
        arrived(pick(everywhere, everywhere, 1 - core, everywhere), c_recv)

    mats = [mat0, mat1, mat2]
    uses = [has_first, None, is_helper]

    def whole(m):
        return mats[m][:, :, :, :, 0:size].reshape(size, size)

    def mat_parts(m):
        return (
            lambda y_at, x_at, core_at, at: mats[m].at[y_at, x_at, core_at, :, at],
            mats[m].shape[-1],
            lambda *at: (g_send.at[(m,) + at], g_recv.at[(m,) + at]),
            lambda: (gc_send.at[m], gc_recv.at[m]),
        )

    def mat_first(m):
        only(uses[m], lambda: gather_first(*mat_parts(m)[:3], uses[m]))

    def mat_second(m):
        only(uses[m], lambda: gather_second(*mat_parts(m)[:3], uses[m]))

    def mat_third(m):
        only(uses[m], lambda: gather_third(*mat_parts(m), uses[m]))

    def mat_end(m):
        gather_end(mat_parts(m)[0], gc_recv.at[m])

    local[0].wait()
    local[1].wait()
    eye = lax.broadcasted_iota(jnp.int32, (own_rows, own_rows), 0) == lax.broadcasted_iota(
        jnp.int32, (own_rows, own_rows), 1
    )
    sep_rows = lax.broadcasted_iota(jnp.int32, own_diag.shape, 0) == own_sep
    diag_row = jnp.sum(jnp.where(sep_rows, own_diag[...], 0.0), axis=0, keepdims=True)
    diag_col = jnp.sum(jnp.where(eye, diag_row, 0.0), axis=1, keepdims=True)
    high = diag_col.astype(BF16).astype(F32)
    middle = (diag_col - high).astype(BF16).astype(F32)
    low = diag_col - high - middle
    lane = lax.broadcasted_iota(jnp.int32, (own_rows, EXTRA), 1)
    beside = jnp.where(
        lane == 0, high, jnp.where(lane == 1, middle, jnp.where(lane == 2, low, 0.0))
    ).astype(BF16)
    mat0[y, x, core, :, 0:size] = unit_lower(own_inverse[...], first_row)
    mat0[y, x, core, :, size:] = beside
    for i in range(4, 10):
        local[i].wait()

    def solve_leaf(b, _):
        lower = unit_lower(inverse[b], 0)
        lower_t[b] = lower.astype(F32).T.astype(BF16)
        rhs_t = rhs[b].T
        columns = pl.ds(pl.multiple_of(b * blk, blk), blk)
        leaf_y[:, columns] = dot_rows(rhs_t, lower).astype(BF16)
        return 0

    lax.fori_loop(0, blocks, solve_leaf, 0)

    pl.semaphore_wait(barrier, len(peers))
    mat_first(0)
    local[2].wait()
    local[3].wait()
    mat_first(1)
    mat_first(2)

    block_of = lax.broadcasted_iota(jnp.int32, (1, blocks * blk), 1) // blk

    def mask_lanes(k):
        result = jnp.zeros((1, blocks * blk), F32)
        for b in range(blocks):
            result = result + jnp.where(block_of == b, mask_ref[k, b].astype(F32), 0.0)
        return result

    def leaf_part(k):
        for copy in couples[k]:
            copy.wait()
        leaf_ym[...] = leaf_y[...] * mask_lanes(k).astype(BF16)
        rhs_t = sep_rhs[k].T
        adds = layer % (2 ** (k + 1)) == 0
        first = jnp.where(adds, first_row, size)

        def tile(i, _):
            start = pl.multiple_of(i * TILE, TILE)
            columns = pl.ds(start, TILE)
            rows_at = first + lax.broadcasted_iota(jnp.int32, (own_rows, TILE), 0)
            cols_at = start + lax.broadcasted_iota(jnp.int32, (own_rows, TILE), 1)
            place = jnp.where(rows_at == cols_at, 1.0, 0.0).astype(BF16)
            term = dot_cols(rhs_t, place) - dot_rows(leaf_ym[...], couple[k, columns, :])
            part[k, :, :, :, :, columns] = term.astype(BF16).reshape(
                part.shape[1:-1] + (TILE,)
            )
            return 0

        lax.fori_loop(0, size // TILE, tile, 0)
        remote(
            lambda: (
                part.at[k, 1 - core],
                paired.at[k],
                rc_send.at[k],
                rc_recv.at[k],
                sibling,
            )
        )

    def reduce_first(k):
        arrived(paired.at[k], rc_recv.at[k])
        chip_sum[k] = (part[k, core].astype(F32) + paired[k].astype(F32)).astype(BF16)
        for h in range(2):
            for d in range(1, SIDE):
                send_part(k, h, d)

    def send_part(k, h, d):
        def parts():
            if h == 0:
                ref = chip_sum.at[k, :, (x + d) % SIDE, :, pl.ds(0, half)]
            else:
                ref = chip_sum.at[k, (y + d) % SIDE, :, :, pl.ds(half, half)]
            return (
                ref,
                in1.at[k, h, d - 1],
                r_send.at[k, 0, h, d - 1],
                r_recv.at[k, 0, h, d - 1],
                x_peer(d) if h == 0 else y_peer(d),
            )

        remote(parts)

    def send_sum(k, h, d):
        remote(
            lambda: (
                sum1.at[k, h, ((y if h == 0 else x) + d) % SIDE],
                in2.at[k, h, d - 1],
                r_send.at[k, 1, h, d - 1],
                r_recv.at[k, 1, h, d - 1],
                y_peer(d) if h == 0 else x_peer(d),
            )
        )

    def reduce_second(k):
        for h in range(2):
            if h == 0:
                value = chip_sum[k, :, x, :, 0:half].astype(F32)
            else:
                value = chip_sum[k, y, :, :, half:].astype(F32)
            for d in range(1, SIDE):
                arrived(in1.at[k, h, d - 1], r_recv.at[k, 0, h, d - 1])
                value = value + in1[k, h, d - 1].astype(F32)
            sum1[k, h] = value.astype(BF16)
            for d in range(1, SIDE):
                send_sum(k, h, d)

    def reduce_end(k):
        for h in range(2):
            value = sum1[k, h, y if h == 0 else x].astype(F32)
            for d in range(1, SIDE):
                arrived(in2.at[k, h, d - 1], r_recv.at[k, 1, h, d - 1])
                value = value + in2[k, h, d - 1].astype(F32)
            total[k, :, h * half : (h + 1) * half] = value

        def send():
            out_total[k] = total[k].astype(BF16)
            if k < 2:
                remote(
                    lambda: (
                        out_total.at[k],
                        from_odd.at[k],
                        odd_send.at[k],
                        odd_recv.at[k],
                        ((layer + 7) % 8, plane),
                    ),
                    is_odd,
                )
            else:
                remote(
                    lambda: (
                        out_total.at[k],
                        from_all.at[slot_of_all()],
                        all_send,
                        all_recv.at[slot_of_all()],
                        (3, plane),
                    ),
                    not_three,
                )

        pl.when(is_odd if k < 2 else not_three)(send)

    def slot_of_all():
        return layer - jnp.where(layer > 3, 1, 0)

    def whole_total(k):
        arrived(from_odd.at[k], odd_recv.at[k])
        return total[k] + from_odd[k].astype(F32)

    def divide(value):
        picks = jnp.where(
            lax.broadcasted_iota(jnp.int32, (value.shape[0], EXTRA), 1) < 3, 1.0, 0.0
        ).astype(BF16)
        parts = mat0[:, :, :, :, size:].reshape(size, EXTRA)
        return value / dot_rows(picks, parts)

    def forward(residual):
        solved = dot_rows(residual.astype(BF16), whole(0)).astype(BF16)
        sep_y[...] = solved
        sep_z[...] = divide(solved.astype(F32))

    two_of = (layer // 4) * 4 + 1
    two_slot = (layer % 4) // 2

    leaf_part(0)
    leaf_part(1)
    reduce_first(0)
    mat_second(0)
    leaf_part(2)
    reduce_second(0)
    reduce_first(1)
    mat_second(1)
    reduce_end(0)
    mat_third(0)
    reduce_second(1)
    mat_second(2)

    @pl.when(is_one)
    def _():
        residual = whole_total(0)
        mat_end(0)
        forward(residual)
        remote(
            lambda: (
                sep_y,
                helped_y.at[1 - two_slot],
                y_send,
                y_recv.at[1 - two_slot],
                ((layer + 7 + 2 * two_slot) % 8, plane),
            ),
            is_one,
        )

    reduce_first(2)
    reduce_end(1)
    mat_third(1)

    @pl.when(is_one)
    def _():
        mat_end(1)
        to_two[...] = (whole_total(1) - dot_rows(sep_y[...], whole(1))).astype(BF16)
        remote(
            lambda: (
                to_two,
                from_one.at[two_slot],
                two_send,
                two_recv.at[two_slot],
                (two_of, plane),
            ),
            is_one,
        )

    reduce_second(2)
    mat_third(2)
    reduce_end(2)

    @pl.when(is_helper)
    def _():
        mat_end(1)
        mat_end(2)
        for slot in range(2):
            arrived(helped_y.at[slot], y_recv.at[slot])
        helped[...] = dot_rows(helped_y[0], whole(1)) + dot_rows(helped_y[1], whole(2))

    def send_three(slot, when):
        remote(
            lambda: (
                to_three,
                from_two.at[slot()],
                three_send,
                three_recv.at[slot()],
                (3, plane),
            ),
            when,
        )

    @pl.when(is_seven)
    def _():
        to_three[...] = helped[...].astype(BF16)
        send_three(lambda: 2, is_seven)

    @pl.when(is_two)
    def _():
        mat_end(0)
        mat_end(1)
        for slot in range(2):
            arrived(from_one.at[slot], two_recv.at[slot])
        forward(from_one[0].astype(F32) + from_one[1].astype(F32))
        to_three[...] = dot_rows(sep_y[...], whole(1)).astype(BF16)
        send_three(lambda: layer // 4, is_two)

    def finish(k, target):
        answer[k, core, y, x] = dot_cols(target.astype(BF16), whole(0)).astype(BF16)

    def own_answer(k):
        return answer.at[k, core, y, x]

    def send_answer(k, slot, layer_to, when):
        remote(
            lambda: (
                own_answer(k),
                own_answer(k),
                x_send.at[slot],
                x_recv.at[k],
                (layer_to(), plane),
            ),
            when,
        )

    @pl.when(is_three)
    def _():
        mat_end(0)
        residual = total[2] - helped[...]
        for slot in range(7):
            arrived(from_all.at[slot], all_recv.at[slot])
            residual = residual + from_all[slot].astype(F32)
        for slot in (2, 0, 1):
            arrived(from_two.at[slot], three_recv.at[slot])
            residual = residual - from_two[slot].astype(F32)
        forward(residual)
        finish(2, sep_z[...])
        for slot, layer_to in enumerate((1, 5, 7, 2, 4, 0, 6)):
            send_answer(2, slot, lambda layer_to=layer_to: layer_to, is_three)

    def send_carry(slot):
        remote(
            lambda: (
                carry.at[slot],
                carried,
                carry_send.at[slot],
                carry_recv,
                ((layer + 7 + 2 * slot) % 8, plane),
            ),
            is_helper,
        )

    @pl.when(jnp.logical_not(is_three))
    def _():
        arrived(own_answer(2), x_recv.at[2])

    @pl.when(is_two)
    def _():
        finish(1, sep_z[...] - dot_cols(own_answer(2)[...], whole(1)))
        for slot, shift in enumerate((7, 1, 2)):
            send_answer(1, 7 + slot, lambda shift=shift: (layer + shift) % 8, is_two)

    def answer_parts(k):
        return (
            lambda y_at, x_at, core_at, at: answer.at[k, core_at, y_at, x_at, :, at],
            size,
            lambda *at: (a_send.at[(k,) + at], a_recv.at[(k,) + at]),
            lambda: (ac_send.at[k], ac_recv.at[k]),
        )

    def answer_first(k, when=None):
        gather_first(*answer_parts(k)[:3], when)

    def answer_second(k):
        gather_second(*answer_parts(k)[:3])

    def answer_third(k):
        gather_third(*answer_parts(k))

    def answer_end(k):
        gather_end(answer_parts(k)[0], ac_recv.at[k])

    @pl.when(is_helper)
    def _():
        for slot in range(2):
            term = dot_cols(own_answer(2)[...], whole(1 + slot))
            carry[slot] = term.astype(BF16)
            send_carry(slot)

    answer_first(2)
    answer_second(2)

    @pl.when(jnp.logical_not(is_two))
    def _():
        arrived(own_answer(1), x_recv.at[1])

    @pl.when(is_one)
    def _():
        term = dot_cols(own_answer(1)[...], whole(1))
        arrived(carried, carry_recv)
        finish(0, sep_z[...] - carried[...].astype(F32) - term)
        send_answer(0, 10, lambda: layer + 1, is_one)
        answer_first(0, is_one)

    own_rows_at = jnp.where(
        first_row + lax.broadcasted_iota(jnp.int32, (own_rows, size), 0)
        == lax.broadcasted_iota(jnp.int32, (own_rows, size), 1),
        1.0,
        0.0,
    ).astype(BF16)

    side_cols = right_sides // CORES

    def rows_out(k, side):
        value = dot_rows(own_rows_at, answer[k, side].reshape(side_cols, size)).astype(BF16)
        sep_out[0, k, :, pl.ds(pl.multiple_of(side * side_cols, side_cols), side_cols)] = value

    def leaf_back(k):
        answer_end(k)
        rows_out(k, core)
        rows_out(k, 1 - core)
        leaf_ym[...] = jnp.broadcast_to(mask_lanes(k), leaf_ym.shape).astype(BF16)
        value = answer.at[k]

        def tile(i, _):
            columns = pl.ds(pl.multiple_of(i * TILE, TILE), TILE)
            term = dot_cols(
                value[...].reshape(right_sides, size), couple[k, :, columns]
            ) * leaf_ym[:, columns].astype(F32)
            back[:, columns] = back[:, columns] - term
            return 0

        lax.fori_loop(0, size // TILE, tile, 0)

    def leaf_end(side):
        rows = pl.ds(pl.multiple_of(side * side_cols, side_cols), side_cols)

        def tile(i, _):
            start = pl.multiple_of(i * TILE, TILE)
            columns = pl.ds(start, TILE)
            term = dot_cols(answer[0, side].reshape(side_cols, size), couple[0, :, columns])
            target = (back[rows, columns] - term * leaf_ym[0:1, columns].astype(F32)).astype(BF16)
            for j in range(TILE // blk):
                b = i * (TILE // blk) + j
                solved = dot_rows(lower_t[b], target[:, j * blk : (j + 1) * blk])
                leaf_out[b, :, rows] = solved.astype(BF16)
            return 0

        lax.fori_loop(0, size // TILE, tile, 0)

    answer_first(1)
    answer_third(2)

    @pl.when(is_odd)
    def _():
        arrived(own_answer(0), x_recv.at[0])
        answer_first(0, is_odd)

    diag_lanes = jnp.concatenate([diag[b : b + 1, :] for b in range(blocks)], axis=1)
    back[...] = leaf_y[...].astype(F32) / diag_lanes
    leaf_back(2)
    answer_second(1)
    answer_second(0)
    answer_third(1)
    leaf_back(1)
    answer_third(0)
    leaf_ym[0:16, :] = jnp.broadcast_to(mask_lanes(0), (16, size)).astype(BF16)
    rows_out(0, core)
    leaf_end(core)
    answer_end(0)
    leaf_end(1 - core)
    rows_out(0, 1 - core)

    for when, make in sends:
        if when is None:
            make().wait_send()
    for group in (has_first, is_helper, is_one, is_odd, is_two, is_three, not_three, is_seven):

        @pl.when(group)
        def _(group=group):
            for when, make in sends:
                if when is group:
                    make().wait_send()


def copy_kernel(leaf_ref, sep_ref, leaf_out, sep_out):
    leaf_out[...] = leaf_ref[...]
    sep_out[...] = sep_ref[...]


def body(
    leaf_rhs,
    leaf_inverse,
    leaf_couple,
    couple_mask,
    leaf_diag,
    sep_rhs,
    sep_inverse,
    sep_couple,
    sep_diag,
):
    blocks, levels, size, blk = leaf_couple.shape
    right_sides = leaf_rhs.shape[2]
    own_rows = sep_rhs.shape[1]
    cols = right_sides // (SIDE * SIDE * CORES)
    half = size // 2
    grid = (SIDE, SIDE, CORES)
    sides = (CORES, SIDE, SIDE)
    vmem = pltpu.VMEM
    dma = pltpu.SemaphoreType.DMA
    hops = (levels, 2, 2, SIDE - 1)
    scratch = [
        vmem(leaf_rhs.shape, BF16),
        vmem(leaf_inverse.shape, BF16),
        vmem((levels, size, blocks * blk), BF16),
        vmem(leaf_diag.shape, F32),
        vmem((levels, own_rows, right_sides), BF16),
        vmem((own_rows, size), BF16),
        vmem(sep_diag.shape, F32),
        vmem(grid + (own_rows, size + EXTRA), BF16),
        vmem(grid + (own_rows, size), BF16),
        vmem(grid + (own_rows, size), BF16),
        vmem((right_sides, blocks * blk), BF16),
        vmem((right_sides, blocks * blk), BF16),
        vmem(leaf_inverse.shape, BF16),
        vmem((levels,) + sides + (cols, size), BF16),
        vmem((levels, SIDE, SIDE, cols, size), BF16),
        vmem((levels, SIDE, SIDE, cols, size), BF16),
        vmem((levels, 2, SIDE - 1, SIDE, cols, half), BF16),
        vmem((levels, 2, SIDE, cols, half), BF16),
        vmem((levels, 2, SIDE - 1, cols, half), BF16),
        vmem((levels, cols, size), F32),
        vmem((levels, cols, size), BF16),
        vmem((levels, cols, size), BF16),
        vmem((7, cols, size), BF16),
        vmem((cols, size), BF16),
        vmem((2, cols, size), BF16),
        vmem((cols, size), BF16),
        vmem((3, cols, size), BF16),
        vmem((cols, size), BF16),
        vmem((2, cols, size), BF16),
        vmem((cols, size), F32),
        vmem((2, cols, size), BF16),
        vmem((cols, size), BF16),
        vmem((cols, size), F32),
        vmem((levels,) + sides + (cols, size), BF16),
        vmem((right_sides, blocks * blk), F32),
        dma((10,)),
        dma((levels, blocks)),
        dma(hops),
        dma(hops),
        dma((levels,)),
        dma((levels,)),
        dma(hops),
        dma(hops),
        dma((levels,)),
        dma((levels,)),
        dma(hops),
        dma(hops),
        dma((levels,)),
        dma((levels,)),
        dma((2,)),
        dma((2,)),
        dma,
        dma((2,)),
        dma,
        dma((3,)),
        dma,
        dma((7,)),
        dma,
        dma((2,)),
        dma((2,)),
        dma,
        dma((11,)),
        dma((levels,)),
    ]
    any_space = pl.BlockSpec(memory_space=pl.ANY)
    in_vmem = pl.BlockSpec(memory_space=pltpu.VMEM)
    outs = pl.pallas_call(
        kernel,
        out_shape=(
            jax.ShapeDtypeStruct(leaf_rhs.shape, BF16),
            jax.ShapeDtypeStruct((1, levels, own_rows, right_sides), BF16),
        ),
        in_specs=[pl.BlockSpec(memory_space=pltpu.SMEM)] + [any_space] * 8,
        out_specs=(in_vmem, in_vmem),
        scratch_shapes=scratch,
        compiler_params=pltpu.CompilerParams(
            collective_id=0, has_side_effects=True, vmem_limit_bytes=56 * 2**20
        ),
    )(
        couple_mask.T,
        leaf_rhs,
        leaf_inverse,
        leaf_couple,
        leaf_diag,
        sep_rhs,
        sep_inverse,
        sep_couple,
        sep_diag,
    )
    return pl.pallas_call(
        copy_kernel,
        out_shape=tuple(jax.ShapeDtypeStruct(out.shape, out.dtype) for out in outs),
        in_specs=[in_vmem] * 2,
        out_specs=(in_vmem, in_vmem),
    )(*outs)


def solution(mesh):
    in_specs = (
        P(("layer", "plane"), None, None),
        P(("layer", "plane"), None, None),
        P(("layer", "plane"), None, None, None),
        P(("layer", "plane"), None),
        P(("layer", "plane"), None),
        P(None, "plane", None),
        P(None, "plane", None),
        P(None, None, "plane", None),
        P(None, "plane"),
    )
    out_specs = (P(("layer", "plane"), None, None), P("layer", None, "plane", None))
    return jax.shard_map(body, mesh=mesh, in_specs=in_specs, out_specs=out_specs, check_vma=False)
```

```python
import jax
import jax.numpy as jnp
from jax import lax
from jax.experimental import pallas as pl
from jax.experimental.pallas import tpu as pltpu
from jax.sharding import PartitionSpec as P

BF16 = jnp.bfloat16
F32 = jnp.float32
SIDE = 4
CORES = 2
EXTRA = 128
TILE = 256


def dot_rows(left, right):
    return lax.dot_general(left, right, (((1,), (1,)), ((), ())), preferred_element_type=F32)


def dot_cols(left, right):
    return lax.dot_general(left, right, (((1,), (0,)), ((), ())), preferred_element_type=F32)


def unit_lower(block, first_row):
    row_ids = first_row + lax.broadcasted_iota(jnp.int32, block.shape, 0)
    col_ids = lax.broadcasted_iota(jnp.int32, block.shape, 1)
    value = block.astype(F32)
    value = jnp.where(col_ids < row_ids, value, 0.0)
    return jnp.where(col_ids == row_ids, 1.0, value).astype(BF16)


def kernel(
    mask_ref,
    rhs_hbm,
    inverse_hbm,
    couple_hbm,
    diag_hbm,
    sep_rhs_hbm,
    sep_inverse_hbm,
    sep_couple_hbm,
    sep_diag_hbm,
    leaf_out,
    sep_out,
    rhs,
    inverse,
    couple,
    diag,
    sep_rhs,
    own_inverse,
    own_diag,
    mat0,
    mat1,
    mat2,
    leaf_y,
    leaf_ym,
    lower_t,
    part,
    paired,
    chip_sum,
    in1,
    sum1,
    in2,
    total,
    from_odd,
    out_total,
    from_all,
    to_two,
    from_one,
    to_three,
    from_two,
    sep_y,
    helped_y,
    helped,
    carry,
    carried,
    sep_z,
    answer,
    back,
    local_sem,
    couple_sem,
    g_send,
    g_recv,
    gc_send,
    gc_recv,
    r_send,
    r_recv,
    rc_send,
    rc_recv,
    a_send,
    a_recv,
    ac_send,
    ac_recv,
    odd_send,
    odd_recv,
    two_send,
    two_recv,
    three_send,
    three_recv,
    all_send,
    all_recv,
    y_send,
    y_recv,
    carry_send,
    carry_recv,
    x_send,
    x_recv,
):
    blocks, blk, right_sides = rhs.shape
    own_rows = own_inverse.shape[0]
    size = own_inverse.shape[1]
    half = size // 2
    layer = lax.axis_index("layer")
    plane = lax.axis_index("plane")
    layers = lax.axis_size("layer")
    y = plane // (SIDE * CORES)
    x = (plane // CORES) % SIDE
    core = plane % CORES
    first_row = plane * own_rows

    def at_plane(y_at, x_at, core_at):
        return (layer, (y_at * SIDE + x_at) * CORES + core_at)

    def x_peer(d):
        return at_plane(y, (x + d) % SIDE, core)

    def y_peer(d):
        return at_plane((y + d) % SIDE, x, core)

    sibling = at_plane(y, x, 1 - core)

    is_one = layer % 2 == 0
    is_odd = layer % 2 == 1
    is_two = layer % 4 == 1
    is_three = layer == 3
    not_three = layer != 3
    is_helper = layer % 4 == 3
    is_seven = layer == 7
    has_first = layer != 7
    sep_of = [layer // 2, 4 + layer // 4, 6 + layer * 0]
    own_sep = jnp.where(is_one, layer // 2, jnp.where(is_two, 4 + layer // 4, 6))

    second_sep = jnp.where(is_helper, layer // 2, own_sep)
    second_block = jnp.where(is_helper, 1, 0)
    third_sep = ((layer + 1) % 8) // 2

    sends = []

    def remote(parts, when=None):
        def make():
            src, dst, send_sem, recv_sem, device = parts()
            return pltpu.make_async_remote_copy(
                src_ref=src,
                dst_ref=dst,
                send_sem=send_sem,
                recv_sem=recv_sem,
                device_id=device,
                device_id_type=pl.DeviceIdType.MESH,
            )

        make().start()
        sends.append((when, make))

    def only(when, act):
        if when is None:
            act()
        else:
            pl.when(when)(act)

    def arrived(dst, sem):
        pltpu.make_async_copy(dst, dst, sem).wait()

    barrier = pltpu.get_barrier_semaphore()
    peers = [sibling]
    for d in range(1, SIDE):
        peers += [x_peer(d), y_peer(d)]
    for d in range(1, 8):
        peers.append(((layer + d) % 8, plane))
    for peer in peers:
        pl.semaphore_signal(barrier, inc=1, device_id=peer, device_id_type=pl.DeviceIdType.MESH)

    local = [
        pltpu.make_async_copy(sep_inverse_hbm.at[own_sep], own_inverse, local_sem.at[0]),
        pltpu.make_async_copy(sep_diag_hbm, own_diag, local_sem.at[1]),
        pltpu.make_async_copy(
            sep_couple_hbm.at[second_sep, second_block], mat1.at[y, x, core], local_sem.at[2]
        ),
        pltpu.make_async_copy(
            sep_couple_hbm.at[third_sep, 1], mat2.at[y, x, core], local_sem.at[3]
        ),
        pltpu.make_async_copy(inverse_hbm, inverse, local_sem.at[4]),
        pltpu.make_async_copy(rhs_hbm, rhs, local_sem.at[5]),
        pltpu.make_async_copy(diag_hbm, diag, local_sem.at[6]),
        pltpu.make_async_copy(sep_rhs_hbm.at[sep_of[0]], sep_rhs.at[0], local_sem.at[7]),
        pltpu.make_async_copy(sep_rhs_hbm.at[sep_of[1]], sep_rhs.at[1], local_sem.at[8]),
        pltpu.make_async_copy(sep_rhs_hbm.at[sep_of[2]], sep_rhs.at[2], local_sem.at[9]),
    ]
    for copy in local:
        copy.start()
    couples = []
    for k in range(3):
        couples.append(
            [
                pltpu.make_async_copy(
                    couple_hbm.at[b, k], couple.at[k, :, pl.ds(b * blk, blk)], couple_sem.at[k, b]
                )
                for b in range(blocks)
            ]
        )
        for copy in couples[k]:
            copy.start()

    def send_first(pick, width, sems, h, d, when):
        def parts():
            ref = pick(y, x, core, lanes(width, h))
            send, recv = sems(0, h, d - 1)
            return ref, ref, send, recv, x_peer(d) if h == 0 else y_peer(d)

        remote(parts, when)

    def send_second(pick, width, sems, h, d, when):
        def parts():
            everywhere = slice(None)
            if h == 0:
                ref = pick(y, everywhere, core, lanes(width, h))
            else:
                ref = pick(everywhere, x, core, lanes(width, h))
            send, recv = sems(1, h, d - 1)
            return ref, ref, send, recv, y_peer(d) if h == 0 else x_peer(d)

        remote(parts, when)

    def lanes(width, h):
        return pl.ds(0, half) if h == 0 else pl.ds(half, width - half)

    def gather_first(pick, width, sems, when=None):
        for h in range(2):
            for d in range(1, SIDE):
                send_first(pick, width, sems, h, d, when)

    def gather_second(pick, width, sems, when=None):
        for h in range(2):
            for d in range(1, SIDE):
                if h == 0:
                    ref = pick(y, (x - d + SIDE) % SIDE, core, lanes(width, h))
                else:
                    ref = pick((y - d + SIDE) % SIDE, x, core, lanes(width, h))
                arrived(ref, sems(0, h, d - 1)[1])
            for d in range(1, SIDE):
                send_second(pick, width, sems, h, d, when)

    def gather_third(pick, width, sems, c_sems, when=None):
        everywhere = slice(None)
        for h in range(2):
            for d in range(1, SIDE):
                if h == 0:
                    ref = pick((y - d + SIDE) % SIDE, everywhere, core, lanes(width, h))
                else:
                    ref = pick(everywhere, (x - d + SIDE) % SIDE, core, lanes(width, h))
                arrived(ref, sems(1, h, d - 1)[1])

        def parts():
            ref = pick(everywhere, everywhere, core, everywhere)
            return (ref, ref) + c_sems() + (sibling,)

        remote(parts, when)

    def gather_end(pick, c_recv):
        everywhere = slice(None)
        arrived(pick(everywhere, everywhere, 1 - core, everywhere), c_recv)

    mats = [mat0, mat1, mat2]
    uses = [has_first, None, is_helper]

    def whole(m):
        return mats[m][:, :, :, :, 0:size].reshape(size, size)

    def mat_parts(m):
        return (
            lambda y_at, x_at, core_at, at: mats[m].at[y_at, x_at, core_at, :, at],
            mats[m].shape[-1],
            lambda *at: (g_send.at[(m,) + at], g_recv.at[(m,) + at]),
            lambda: (gc_send.at[m], gc_recv.at[m]),
        )

    def mat_first(m):
        only(uses[m], lambda: gather_first(*mat_parts(m)[:3], uses[m]))

    def mat_second(m):
        only(uses[m], lambda: gather_second(*mat_parts(m)[:3], uses[m]))

    def mat_third(m):
        only(uses[m], lambda: gather_third(*mat_parts(m), uses[m]))

    def mat_end(m):
        gather_end(mat_parts(m)[0], gc_recv.at[m])

    local[0].wait()
    local[1].wait()
    eye = lax.broadcasted_iota(jnp.int32, (own_rows, own_rows), 0) == lax.broadcasted_iota(
        jnp.int32, (own_rows, own_rows), 1
    )
    sep_rows = lax.broadcasted_iota(jnp.int32, own_diag.shape, 0) == own_sep
    diag_row = jnp.sum(jnp.where(sep_rows, own_diag[...], 0.0), axis=0, keepdims=True)
    diag_col = jnp.sum(jnp.where(eye, diag_row, 0.0), axis=1, keepdims=True)
    high = diag_col.astype(BF16).astype(F32)
    middle = (diag_col - high).astype(BF16).astype(F32)
    low = diag_col - high - middle
    lane = lax.broadcasted_iota(jnp.int32, (own_rows, EXTRA), 1)
    beside = jnp.where(
        lane == 0, high, jnp.where(lane == 1, middle, jnp.where(lane == 2, low, 0.0))
    ).astype(BF16)
    mat0[y, x, core, :, 0:size] = unit_lower(own_inverse[...], first_row)
    mat0[y, x, core, :, size:] = beside
    for i in range(4, 10):
        local[i].wait()

    def solve_leaf(b, _):
        lower = unit_lower(inverse[b], 0)
        lower_t[b] = lower.astype(F32).T.astype(BF16)
        rhs_t = rhs[b].T
        columns = pl.ds(pl.multiple_of(b * blk, blk), blk)
        leaf_y[:, columns] = dot_rows(rhs_t, lower).astype(BF16)
        return 0

    lax.fori_loop(0, blocks, solve_leaf, 0)

    pl.semaphore_wait(barrier, len(peers))
    mat_first(0)
    local[2].wait()
    local[3].wait()
    mat_first(1)
    mat_first(2)

    block_of = lax.broadcasted_iota(jnp.int32, (1, blocks * blk), 1) // blk

    def mask_lanes(k):
        result = jnp.zeros((1, blocks * blk), F32)
        for b in range(blocks):
            result = result + jnp.where(block_of == b, mask_ref[k, b].astype(F32), 0.0)
        return result

    def leaf_part(k):
        for copy in couples[k]:
            copy.wait()
        leaf_ym[...] = leaf_y[...] * mask_lanes(k).astype(BF16)
        rhs_t = sep_rhs[k].T
        adds = layer % (2 ** (k + 1)) == 0
        first = jnp.where(adds, first_row, size)

        def tile(i, _):
            start = pl.multiple_of(i * TILE, TILE)
            columns = pl.ds(start, TILE)
            rows_at = first + lax.broadcasted_iota(jnp.int32, (own_rows, TILE), 0)
            cols_at = start + lax.broadcasted_iota(jnp.int32, (own_rows, TILE), 1)
            place = jnp.where(rows_at == cols_at, 1.0, 0.0).astype(BF16)
            term = dot_cols(rhs_t, place) - dot_rows(leaf_ym[...], couple[k, columns, :])
            part[k, :, :, :, :, columns] = term.astype(BF16).reshape(
                part.shape[1:-1] + (TILE,)
            )
            return 0

        lax.fori_loop(0, size // TILE, tile, 0)
        remote(
            lambda: (
                part.at[k, 1 - core],
                paired.at[k],
                rc_send.at[k],
                rc_recv.at[k],
                sibling,
            )
        )

    def reduce_first(k):
        arrived(paired.at[k], rc_recv.at[k])
        chip_sum[k] = (part[k, core].astype(F32) + paired[k].astype(F32)).astype(BF16)
        for h in range(2):
            for d in range(1, SIDE):
                send_part(k, h, d)

    def send_part(k, h, d):
        def parts():
            if h == 0:
                ref = chip_sum.at[k, :, (x + d) % SIDE, :, pl.ds(0, half)]
            else:
                ref = chip_sum.at[k, (y + d) % SIDE, :, :, pl.ds(half, half)]
            return (
                ref,
                in1.at[k, h, d - 1],
                r_send.at[k, 0, h, d - 1],
                r_recv.at[k, 0, h, d - 1],
                x_peer(d) if h == 0 else y_peer(d),
            )

        remote(parts)

    def send_sum(k, h, d):
        remote(
            lambda: (
                sum1.at[k, h, ((y if h == 0 else x) + d) % SIDE],
                in2.at[k, h, d - 1],
                r_send.at[k, 1, h, d - 1],
                r_recv.at[k, 1, h, d - 1],
                y_peer(d) if h == 0 else x_peer(d),
            )
        )

    def reduce_second(k):
        for h in range(2):
            if h == 0:
                value = chip_sum[k, :, x, :, 0:half].astype(F32)
            else:
                value = chip_sum[k, y, :, :, half:].astype(F32)
            for d in range(1, SIDE):
                arrived(in1.at[k, h, d - 1], r_recv.at[k, 0, h, d - 1])
                value = value + in1[k, h, d - 1].astype(F32)
            sum1[k, h] = value.astype(BF16)
            for d in range(1, SIDE):
                send_sum(k, h, d)

    def reduce_end(k):
        for h in range(2):
            value = sum1[k, h, y if h == 0 else x].astype(F32)
            for d in range(1, SIDE):
                arrived(in2.at[k, h, d - 1], r_recv.at[k, 1, h, d - 1])
                value = value + in2[k, h, d - 1].astype(F32)
            total[k, :, h * half : (h + 1) * half] = value

        def send():
            out_total[k] = total[k].astype(BF16)
            if k < 2:
                remote(
                    lambda: (
                        out_total.at[k],
                        from_odd.at[k],
                        odd_send.at[k],
                        odd_recv.at[k],
                        ((layer + 7) % 8, plane),
                    ),
                    is_odd,
                )
            else:
                remote(
                    lambda: (
                        out_total.at[k],
                        from_all.at[slot_of_all()],
                        all_send,
                        all_recv.at[slot_of_all()],
                        (3, plane),
                    ),
                    not_three,
                )

        pl.when(is_odd if k < 2 else not_three)(send)

    def slot_of_all():
        return layer - jnp.where(layer > 3, 1, 0)

    def whole_total(k):
        arrived(from_odd.at[k], odd_recv.at[k])
        return total[k] + from_odd[k].astype(F32)

    def divide(value):
        picks = jnp.where(
            lax.broadcasted_iota(jnp.int32, (value.shape[0], EXTRA), 1) < 3, 1.0, 0.0
        ).astype(BF16)
        parts = mat0[:, :, :, :, size:].reshape(size, EXTRA)
        return value / dot_rows(picks, parts)

    def forward(residual):
        solved = dot_rows(residual.astype(BF16), whole(0)).astype(BF16)
        sep_y[...] = solved
        sep_z[...] = divide(solved.astype(F32))

    two_of = (layer // 4) * 4 + 1
    two_slot = (layer % 4) // 2

    leaf_part(0)
    leaf_part(1)
    reduce_first(0)
    mat_second(0)
    leaf_part(2)
    reduce_first(1)
    reduce_second(0)
    mat_second(1)
    reduce_end(0)
    mat_third(0)
    reduce_second(1)
    mat_second(2)

    @pl.when(is_one)
    def _():
        residual = whole_total(0)
        mat_end(0)
        forward(residual)
        remote(
            lambda: (
                sep_y,
                helped_y.at[1 - two_slot],
                y_send,
                y_recv.at[1 - two_slot],
                ((layer + 7 + 2 * two_slot) % 8, plane),
            ),
            is_one,
        )

    reduce_first(2)
    reduce_end(1)
    mat_third(1)

    @pl.when(is_one)
    def _():
        mat_end(1)
        to_two[...] = (whole_total(1) - dot_rows(sep_y[...], whole(1))).astype(BF16)
        remote(
            lambda: (
                to_two,
                from_one.at[two_slot],
                two_send,
                two_recv.at[two_slot],
                (two_of, plane),
            ),
            is_one,
        )

    reduce_second(2)
    mat_third(2)
    reduce_end(2)

    @pl.when(is_helper)
    def _():
        mat_end(1)
        mat_end(2)
        for slot in range(2):
            arrived(helped_y.at[slot], y_recv.at[slot])
        helped[...] = dot_rows(helped_y[0], whole(1)) + dot_rows(helped_y[1], whole(2))

    def send_three(slot, when):
        remote(
            lambda: (
                to_three,
                from_two.at[slot()],
                three_send,
                three_recv.at[slot()],
                (3, plane),
            ),
            when,
        )

    @pl.when(is_seven)
    def _():
        to_three[...] = helped[...].astype(BF16)
        send_three(lambda: 2, is_seven)

    @pl.when(is_two)
    def _():
        mat_end(0)
        mat_end(1)
        for slot in range(2):
            arrived(from_one.at[slot], two_recv.at[slot])
        forward(from_one[0].astype(F32) + from_one[1].astype(F32))
        to_three[...] = dot_rows(sep_y[...], whole(1)).astype(BF16)
        send_three(lambda: layer // 4, is_two)

    diag_lanes = jnp.concatenate([diag[b : b + 1, :] for b in range(blocks)], axis=1)
    back[...] = leaf_y[...].astype(F32) / diag_lanes

    def finish(k, target):
        answer[k, core, y, x] = dot_cols(target.astype(BF16), whole(0)).astype(BF16)

    def own_answer(k):
        return answer.at[k, core, y, x]

    def send_answer(k, slot, layer_to, when):
        remote(
            lambda: (
                own_answer(k),
                own_answer(k),
                x_send.at[slot],
                x_recv.at[k],
                (layer_to(), plane),
            ),
            when,
        )

    @pl.when(is_three)
    def _():
        mat_end(0)
        residual = total[2] - helped[...]
        for slot in range(7):
            arrived(from_all.at[slot], all_recv.at[slot])
            residual = residual + from_all[slot].astype(F32)
        for slot in (2, 0, 1):
            arrived(from_two.at[slot], three_recv.at[slot])
            residual = residual - from_two[slot].astype(F32)
        forward(residual)
        finish(2, sep_z[...])
        for slot, layer_to in enumerate((1, 5, 7, 2, 4, 0, 6)):
            send_answer(2, slot, lambda layer_to=layer_to: layer_to, is_three)

    def send_carry(slot):
        remote(
            lambda: (
                carry.at[slot],
                carried,
                carry_send.at[slot],
                carry_recv,
                ((layer + 7 + 2 * slot) % 8, plane),
            ),
            is_helper,
        )

    @pl.when(jnp.logical_not(is_three))
    def _():
        arrived(own_answer(2), x_recv.at[2])

    @pl.when(is_two)
    def _():
        finish(1, sep_z[...] - dot_cols(own_answer(2)[...], whole(1)))
        for slot, shift in enumerate((7, 1, 2)):
            send_answer(1, 7 + slot, lambda shift=shift: (layer + shift) % 8, is_two)

    def answer_parts(k):
        return (
            lambda y_at, x_at, core_at, at: answer.at[k, core_at, y_at, x_at, :, at],
            size,
            lambda *at: (a_send.at[(k,) + at], a_recv.at[(k,) + at]),
            lambda: (ac_send.at[k], ac_recv.at[k]),
        )

    def answer_first(k, when=None):
        gather_first(*answer_parts(k)[:3], when)

    def answer_second(k):
        gather_second(*answer_parts(k)[:3])

    def answer_third(k):
        gather_third(*answer_parts(k))

    def answer_end(k):
        gather_end(answer_parts(k)[0], ac_recv.at[k])

    @pl.when(is_helper)
    def _():
        for slot in range(2):
            term = dot_cols(own_answer(2)[...], whole(1 + slot))
            carry[slot] = term.astype(BF16)
            send_carry(slot)

    answer_first(2)
    answer_second(2)

    @pl.when(jnp.logical_not(is_two))
    def _():
        arrived(own_answer(1), x_recv.at[1])

    @pl.when(is_one)
    def _():
        term = dot_cols(own_answer(1)[...], whole(1))
        arrived(carried, carry_recv)
        finish(0, sep_z[...] - carried[...].astype(F32) - term)
        send_answer(0, 10, lambda: layer + 1, is_one)
        answer_first(0, is_one)

    own_rows_at = jnp.where(
        first_row + lax.broadcasted_iota(jnp.int32, (own_rows, size), 0)
        == lax.broadcasted_iota(jnp.int32, (own_rows, size), 1),
        1.0,
        0.0,
    ).astype(BF16)

    side_cols = right_sides // CORES

    def rows_out(k, side):
        value = dot_rows(own_rows_at, answer[k, side].reshape(side_cols, size)).astype(BF16)
        sep_out[0, k, :, pl.ds(pl.multiple_of(side * side_cols, side_cols), side_cols)] = value

    def leaf_back(k):
        answer_end(k)
        rows_out(k, core)
        rows_out(k, 1 - core)
        leaf_ym[...] = jnp.broadcast_to(mask_lanes(k), leaf_ym.shape).astype(BF16)
        value = answer.at[k]

        def tile(i, _):
            columns = pl.ds(pl.multiple_of(i * TILE, TILE), TILE)
            term = dot_cols(
                value[...].reshape(right_sides, size), couple[k, :, columns]
            ) * leaf_ym[:, columns].astype(F32)
            back[:, columns] = back[:, columns] - term
            return 0

        lax.fori_loop(0, size // TILE, tile, 0)

    def leaf_end(side):
        rows = pl.ds(pl.multiple_of(side * side_cols, side_cols), side_cols)

        def tile(i, _):
            start = pl.multiple_of(i * TILE, TILE)
            columns = pl.ds(start, TILE)
            term = dot_cols(answer[0, side].reshape(side_cols, size), couple[0, :, columns])
            target = (back[rows, columns] - term * leaf_ym[0:1, columns].astype(F32)).astype(BF16)
            for j in range(TILE // blk):
                b = i * (TILE // blk) + j
                solved = dot_rows(lower_t[b], target[:, j * blk : (j + 1) * blk])
                leaf_out[b, :, rows] = solved.astype(BF16)
            return 0

        lax.fori_loop(0, size // TILE, tile, 0)

    answer_first(1)
    answer_second(1)

    @pl.when(is_odd)
    def _():
        arrived(own_answer(0), x_recv.at[0])
        answer_first(0, is_odd)

    answer_third(2)
    answer_second(0)
    leaf_back(2)
    answer_third(1)
    leaf_back(1)
    answer_third(0)
    leaf_ym[0:16, :] = jnp.broadcast_to(mask_lanes(0), (16, size)).astype(BF16)
    rows_out(0, core)
    leaf_end(core)
    answer_end(0)
    leaf_end(1 - core)
    rows_out(0, 1 - core)

    for when, make in sends:
        if when is None:
            make().wait_send()
    for group in (has_first, is_helper, is_one, is_odd, is_two, is_three, not_three, is_seven):

        @pl.when(group)
        def _(group=group):
            for when, make in sends:
                if when is group:
                    make().wait_send()


def copy_kernel(leaf_ref, sep_ref, leaf_out, sep_out):
    leaf_out[...] = leaf_ref[...]
    sep_out[...] = sep_ref[...]


def body(
    leaf_rhs,
    leaf_inverse,
    leaf_couple,
    couple_mask,
    leaf_diag,
    sep_rhs,
    sep_inverse,
    sep_couple,
    sep_diag,
):
    blocks, levels, size, blk = leaf_couple.shape
    right_sides = leaf_rhs.shape[2]
    own_rows = sep_rhs.shape[1]
    cols = right_sides // (SIDE * SIDE * CORES)
    half = size // 2
    grid = (SIDE, SIDE, CORES)
    sides = (CORES, SIDE, SIDE)
    vmem = pltpu.VMEM
    dma = pltpu.SemaphoreType.DMA
    hops = (levels, 2, 2, SIDE - 1)
    scratch = [
        vmem(leaf_rhs.shape, BF16),
        vmem(leaf_inverse.shape, BF16),
        vmem((levels, size, blocks * blk), BF16),
        vmem(leaf_diag.shape, F32),
        vmem((levels, own_rows, right_sides), BF16),
        vmem((own_rows, size), BF16),
        vmem(sep_diag.shape, F32),
        vmem(grid + (own_rows, size + EXTRA), BF16),
        vmem(grid + (own_rows, size), BF16),
        vmem(grid + (own_rows, size), BF16),
        vmem((right_sides, blocks * blk), BF16),
        vmem((right_sides, blocks * blk), BF16),
        vmem(leaf_inverse.shape, BF16),
        vmem((levels,) + sides + (cols, size), BF16),
        vmem((levels, SIDE, SIDE, cols, size), BF16),
        vmem((levels, SIDE, SIDE, cols, size), BF16),
        vmem((levels, 2, SIDE - 1, SIDE, cols, half), BF16),
        vmem((levels, 2, SIDE, cols, half), BF16),
        vmem((levels, 2, SIDE - 1, cols, half), BF16),
        vmem((levels, cols, size), F32),
        vmem((levels, cols, size), BF16),
        vmem((levels, cols, size), BF16),
        vmem((7, cols, size), BF16),
        vmem((cols, size), BF16),
        vmem((2, cols, size), BF16),
        vmem((cols, size), BF16),
        vmem((3, cols, size), BF16),
        vmem((cols, size), BF16),
        vmem((2, cols, size), BF16),
        vmem((cols, size), F32),
        vmem((2, cols, size), BF16),
        vmem((cols, size), BF16),
        vmem((cols, size), F32),
        vmem((levels,) + sides + (cols, size), BF16),
        vmem((right_sides, blocks * blk), F32),
        dma((10,)),
        dma((levels, blocks)),
        dma(hops),
        dma(hops),
        dma((levels,)),
        dma((levels,)),
        dma(hops),
        dma(hops),
        dma((levels,)),
        dma((levels,)),
        dma(hops),
        dma(hops),
        dma((levels,)),
        dma((levels,)),
        dma((2,)),
        dma((2,)),
        dma,
        dma((2,)),
        dma,
        dma((3,)),
        dma,
        dma((7,)),
        dma,
        dma((2,)),
        dma((2,)),
        dma,
        dma((11,)),
        dma((levels,)),
    ]
    any_space = pl.BlockSpec(memory_space=pl.ANY)
    in_vmem = pl.BlockSpec(memory_space=pltpu.VMEM)
    outs = pl.pallas_call(
        kernel,
        out_shape=(
            jax.ShapeDtypeStruct(leaf_rhs.shape, BF16),
            jax.ShapeDtypeStruct((1, levels, own_rows, right_sides), BF16),
        ),
        in_specs=[pl.BlockSpec(memory_space=pltpu.SMEM)] + [any_space] * 8,
        out_specs=(in_vmem, in_vmem),
        scratch_shapes=scratch,
        compiler_params=pltpu.CompilerParams(
            collective_id=0, has_side_effects=True, vmem_limit_bytes=56 * 2**20
        ),
    )(
        couple_mask.T,
        leaf_rhs,
        leaf_inverse,
        leaf_couple,
        leaf_diag,
        sep_rhs,
        sep_inverse,
        sep_couple,
        sep_diag,
    )
    return pl.pallas_call(
        copy_kernel,
        out_shape=tuple(jax.ShapeDtypeStruct(out.shape, out.dtype) for out in outs),
        in_specs=[in_vmem] * 2,
        out_specs=(in_vmem, in_vmem),
    )(*outs)


def solution(mesh):
    in_specs = (
        P(("layer", "plane"), None, None),
        P(("layer", "plane"), None, None),
        P(("layer", "plane"), None, None, None),
        P(("layer", "plane"), None),
        P(("layer", "plane"), None),
        P(None, "plane", None),
        P(None, "plane", None),
        P(None, None, "plane", None),
        P(None, "plane"),
    )
    out_specs = (P(("layer", "plane"), None, None), P("layer", None, "plane", None))
    return jax.shard_map(body, mesh=mesh, in_specs=in_specs, out_specs=out_specs, check_vma=False)
```

```python
import jax
import jax.numpy as jnp
from jax import lax
from jax.experimental import pallas as pl
from jax.experimental.pallas import tpu as pltpu
from jax.sharding import PartitionSpec as P

BF16 = jnp.bfloat16
F32 = jnp.float32
SIDE = 4
CORES = 2
EXTRA = 128
TILE = 256


def dot_rows(left, right):
    return lax.dot_general(left, right, (((1,), (1,)), ((), ())), preferred_element_type=F32)


def dot_cols(left, right):
    return lax.dot_general(left, right, (((1,), (0,)), ((), ())), preferred_element_type=F32)


def unit_lower(block, first_row):
    row_ids = first_row + lax.broadcasted_iota(jnp.int32, block.shape, 0)
    col_ids = lax.broadcasted_iota(jnp.int32, block.shape, 1)
    value = block.astype(F32)
    value = jnp.where(col_ids < row_ids, value, 0.0)
    return jnp.where(col_ids == row_ids, 1.0, value).astype(BF16)


def kernel(
    mask_ref,
    rhs_hbm,
    inverse_hbm,
    couple_hbm,
    diag_hbm,
    sep_rhs_hbm,
    sep_inverse_hbm,
    sep_couple_hbm,
    sep_diag_hbm,
    leaf_out,
    sep_out,
    rhs,
    inverse,
    couple,
    diag,
    sep_rhs,
    own_inverse,
    own_diag,
    mat0,
    mat1,
    mat2,
    mat3,
    mat4,
    pair_inverse,
    leaf_y,
    leaf_ym,
    lower_t,
    part,
    paired,
    chip_sum,
    in1,
    sum1,
    in2,
    total,
    from_odd,
    out_total,
    from_all,
    to_two,
    from_one,
    to_three,
    from_two,
    sep_y,
    helped_y,
    helped,
    carry,
    carried,
    sep_z,
    pair_z,
    answer,
    back,
    local_sem,
    couple_sem,
    g_send,
    g_recv,
    gc_send,
    gc_recv,
    r_send,
    r_recv,
    rc_send,
    rc_recv,
    a_send,
    a_recv,
    ac_send,
    ac_recv,
    odd_send,
    odd_recv,
    two_send,
    two_recv,
    three_send,
    three_recv,
    all_send,
    all_recv,
    y_send,
    y_pair_send,
    y_recv,
    carry_send,
    carry_recv,
    x_send,
    x_recv,
):
    blocks, blk, right_sides = rhs.shape
    own_rows = own_inverse.shape[0]
    size = own_inverse.shape[1]
    half = size // 2
    layer = lax.axis_index("layer")
    plane = lax.axis_index("plane")
    layers = lax.axis_size("layer")
    y = plane // (SIDE * CORES)
    x = (plane // CORES) % SIDE
    core = plane % CORES
    first_row = plane * own_rows

    def at_plane(y_at, x_at, core_at):
        return (layer, (y_at * SIDE + x_at) * CORES + core_at)

    def x_peer(d):
        return at_plane(y, (x + d) % SIDE, core)

    def y_peer(d):
        return at_plane((y + d) % SIDE, x, core)

    sibling = at_plane(y, x, 1 - core)

    is_one = layer % 2 == 0
    is_odd = layer % 2 == 1
    is_two = layer % 4 == 1
    is_three = layer == 3
    not_three = layer != 3
    is_helper = layer % 4 == 3
    is_seven = layer == 7
    is_base = layer % 4 == 0
    has_first = layer != 7
    sep_of = [layer // 2, 4 + layer // 4, 6 + layer * 0]
    own_sep = jnp.where(is_one, layer // 2, jnp.where(is_two, 4 + layer // 4, 6))

    second_sep = jnp.where(is_helper, layer // 2, own_sep)
    second_block = jnp.where(is_helper, 1, 0)
    third_sep = ((layer + 1) % 8) // 2

    sends = []

    def remote(parts, when=None):
        def make():
            src, dst, send_sem, recv_sem, device = parts()
            return pltpu.make_async_remote_copy(
                src_ref=src,
                dst_ref=dst,
                send_sem=send_sem,
                recv_sem=recv_sem,
                device_id=device,
                device_id_type=pl.DeviceIdType.MESH,
            )

        make().start()
        sends.append((when, make))

    def only(when, act):
        if when is None:
            act()
        else:
            pl.when(when)(act)

    def arrived(dst, sem):
        pltpu.make_async_copy(dst, dst, sem).wait()

    barrier = pltpu.get_barrier_semaphore()
    peers = [sibling]
    for d in range(1, SIDE):
        peers += [x_peer(d), y_peer(d)]
    for d in range(1, 8):
        peers.append(((layer + d) % 8, plane))
    for peer in peers:
        pl.semaphore_signal(barrier, inc=1, device_id=peer, device_id_type=pl.DeviceIdType.MESH)

    local = [
        pltpu.make_async_copy(sep_inverse_hbm.at[own_sep], own_inverse, local_sem.at[0]),
        pltpu.make_async_copy(sep_diag_hbm, own_diag, local_sem.at[1]),
        pltpu.make_async_copy(
            sep_couple_hbm.at[second_sep, second_block], mat1.at[y, x, core], local_sem.at[2]
        ),
        pltpu.make_async_copy(
            sep_couple_hbm.at[third_sep, 1], mat2.at[y, x, core], local_sem.at[3]
        ),
        pltpu.make_async_copy(inverse_hbm, inverse, local_sem.at[4]),
        pltpu.make_async_copy(rhs_hbm, rhs, local_sem.at[5]),
        pltpu.make_async_copy(diag_hbm, diag, local_sem.at[6]),
        pltpu.make_async_copy(sep_rhs_hbm.at[sep_of[0]], sep_rhs.at[0], local_sem.at[7]),
        pltpu.make_async_copy(sep_rhs_hbm.at[sep_of[1]], sep_rhs.at[1], local_sem.at[8]),
        pltpu.make_async_copy(sep_rhs_hbm.at[sep_of[2]], sep_rhs.at[2], local_sem.at[9]),
        pltpu.make_async_copy(sep_inverse_hbm.at[sep_of[0]], pair_inverse, local_sem.at[10]),
        pltpu.make_async_copy(
            sep_couple_hbm.at[sep_of[0], 0], mat4.at[y, x, core], local_sem.at[11]
        ),
    ]
    for copy in local:
        copy.start()
    couples = []
    for k in range(3):
        couples.append(
            [
                pltpu.make_async_copy(
                    couple_hbm.at[b, k], couple.at[k, :, pl.ds(b * blk, blk)], couple_sem.at[k, b]
                )
                for b in range(blocks)
            ]
        )
        for copy in couples[k]:
            copy.start()

    def send_first(pick, width, sems, h, d, when):
        def parts():
            ref = pick(y, x, core, lanes(width, h))
            send, recv = sems(0, h, d - 1)
            return ref, ref, send, recv, x_peer(d) if h == 0 else y_peer(d)

        remote(parts, when)

    def send_second(pick, width, sems, h, d, when):
        def parts():
            everywhere = slice(None)
            if h == 0:
                ref = pick(y, everywhere, core, lanes(width, h))
            else:
                ref = pick(everywhere, x, core, lanes(width, h))
            send, recv = sems(1, h, d - 1)
            return ref, ref, send, recv, y_peer(d) if h == 0 else x_peer(d)

        remote(parts, when)

    def lanes(width, h):
        return pl.ds(0, half) if h == 0 else pl.ds(half, width - half)

    def gather_first(pick, width, sems, when=None):
        for h in range(2):
            for d in range(1, SIDE):
                send_first(pick, width, sems, h, d, when)

    def gather_second(pick, width, sems, when=None):
        for h in range(2):
            for d in range(1, SIDE):
                if h == 0:
                    ref = pick(y, (x - d + SIDE) % SIDE, core, lanes(width, h))
                else:
                    ref = pick((y - d + SIDE) % SIDE, x, core, lanes(width, h))
                arrived(ref, sems(0, h, d - 1)[1])
            for d in range(1, SIDE):
                send_second(pick, width, sems, h, d, when)

    def gather_third(pick, width, sems, c_sems, when=None):
        everywhere = slice(None)
        for h in range(2):
            for d in range(1, SIDE):
                if h == 0:
                    ref = pick((y - d + SIDE) % SIDE, everywhere, core, lanes(width, h))
                else:
                    ref = pick(everywhere, (x - d + SIDE) % SIDE, core, lanes(width, h))
                arrived(ref, sems(1, h, d - 1)[1])

        def parts():
            ref = pick(everywhere, everywhere, core, everywhere)
            return (ref, ref) + c_sems() + (sibling,)

        remote(parts, when)

    def gather_end(pick, c_recv):
        everywhere = slice(None)
        arrived(pick(everywhere, everywhere, 1 - core, everywhere), c_recv)

    mats = [mat0, mat1, mat2, mat3, mat4]
    uses = [has_first, None, is_helper, is_odd, is_odd]

    def whole(m):
        return mats[m][:, :, :, :, 0:size].reshape(size, size)

    def mat_parts(m):
        return (
            lambda y_at, x_at, core_at, at: mats[m].at[y_at, x_at, core_at, :, at],
            mats[m].shape[-1],
            lambda *at: (g_send.at[(m,) + at], g_recv.at[(m,) + at]),
            lambda: (gc_send.at[m], gc_recv.at[m]),
        )

    def mat_first(m):
        only(uses[m], lambda: gather_first(*mat_parts(m)[:3], uses[m]))

    def mat_second(m):
        only(uses[m], lambda: gather_second(*mat_parts(m)[:3], uses[m]))

    def mat_third(m):
        only(uses[m], lambda: gather_third(*mat_parts(m), uses[m]))

    def mat_end(m):
        gather_end(mat_parts(m)[0], gc_recv.at[m])

    local[0].wait()
    local[1].wait()
    eye = lax.broadcasted_iota(jnp.int32, (own_rows, own_rows), 0) == lax.broadcasted_iota(
        jnp.int32, (own_rows, own_rows), 1
    )

    def diag_beside(sep):
        sep_rows = lax.broadcasted_iota(jnp.int32, own_diag.shape, 0) == sep
        diag_row = jnp.sum(jnp.where(sep_rows, own_diag[...], 0.0), axis=0, keepdims=True)
        diag_col = jnp.sum(jnp.where(eye, diag_row, 0.0), axis=1, keepdims=True)
        high = diag_col.astype(BF16).astype(F32)
        middle = (diag_col - high).astype(BF16).astype(F32)
        low = diag_col - high - middle
        lane = lax.broadcasted_iota(jnp.int32, (own_rows, EXTRA), 1)
        return jnp.where(
            lane == 0, high, jnp.where(lane == 1, middle, jnp.where(lane == 2, low, 0.0))
        ).astype(BF16)

    mat0[y, x, core, :, 0:size] = unit_lower(own_inverse[...], first_row)
    mat0[y, x, core, :, size:] = diag_beside(own_sep)
    for i in range(4, 12):
        local[i].wait()

    def solve_leaf(b, _):
        lower = unit_lower(inverse[b], 0)
        lower_t[b] = lower.astype(F32).T.astype(BF16)
        rhs_t = rhs[b].T
        columns = pl.ds(pl.multiple_of(b * blk, blk), blk)
        leaf_y[:, columns] = dot_rows(rhs_t, lower).astype(BF16)
        return 0

    lax.fori_loop(0, blocks, solve_leaf, 0)
    mat3[y, x, core, :, 0:size] = unit_lower(pair_inverse[...], first_row)
    mat3[y, x, core, :, size:] = diag_beside(sep_of[0])

    pl.semaphore_wait(barrier, len(peers))
    mat_first(0)
    local[2].wait()
    local[3].wait()
    mat_first(1)
    mat_first(2)

    block_of = lax.broadcasted_iota(jnp.int32, (1, blocks * blk), 1) // blk

    def mask_lanes(k):
        result = jnp.zeros((1, blocks * blk), F32)
        for b in range(blocks):
            result = result + jnp.where(block_of == b, mask_ref[k, b].astype(F32), 0.0)
        return result

    def leaf_part(k):
        for copy in couples[k]:
            copy.wait()
        leaf_ym[...] = leaf_y[...] * mask_lanes(k).astype(BF16)
        rhs_t = sep_rhs[k].T
        adds = layer % (2 ** (k + 1)) == 0
        first = jnp.where(adds, first_row, size)

        def tile(i, _):
            start = pl.multiple_of(i * TILE, TILE)
            columns = pl.ds(start, TILE)
            rows_at = first + lax.broadcasted_iota(jnp.int32, (own_rows, TILE), 0)
            cols_at = start + lax.broadcasted_iota(jnp.int32, (own_rows, TILE), 1)
            place = jnp.where(rows_at == cols_at, 1.0, 0.0).astype(BF16)
            term = dot_cols(rhs_t, place) - dot_rows(leaf_ym[...], couple[k, columns, :])
            part[k, :, :, :, :, columns] = term.astype(BF16).reshape(
                part.shape[1:-1] + (TILE,)
            )
            return 0

        lax.fori_loop(0, size // TILE, tile, 0)
        remote(
            lambda: (
                part.at[k, 1 - core],
                paired.at[k],
                rc_send.at[k],
                rc_recv.at[k],
                sibling,
            )
        )

    def reduce_first(k):
        arrived(paired.at[k], rc_recv.at[k])
        chip_sum[k] = (part[k, core].astype(F32) + paired[k].astype(F32)).astype(BF16)
        for h in range(2):
            for d in range(1, SIDE):
                send_part(k, h, d)

    def send_part(k, h, d):
        def parts():
            if h == 0:
                ref = chip_sum.at[k, :, (x + d) % SIDE, :, pl.ds(0, half)]
            else:
                ref = chip_sum.at[k, (y + d) % SIDE, :, :, pl.ds(half, half)]
            return (
                ref,
                in1.at[k, h, d - 1],
                r_send.at[k, 0, h, d - 1],
                r_recv.at[k, 0, h, d - 1],
                x_peer(d) if h == 0 else y_peer(d),
            )

        remote(parts)

    def send_sum(k, h, d):
        remote(
            lambda: (
                sum1.at[k, h, ((y if h == 0 else x) + d) % SIDE],
                in2.at[k, h, d - 1],
                r_send.at[k, 1, h, d - 1],
                r_recv.at[k, 1, h, d - 1],
                y_peer(d) if h == 0 else x_peer(d),
            )
        )

    def reduce_second(k):
        for h in range(2):
            if h == 0:
                value = chip_sum[k, :, x, :, 0:half].astype(F32)
            else:
                value = chip_sum[k, y, :, :, half:].astype(F32)
            for d in range(1, SIDE):
                arrived(in1.at[k, h, d - 1], r_recv.at[k, 0, h, d - 1])
                value = value + in1[k, h, d - 1].astype(F32)
            sum1[k, h] = value.astype(BF16)
            for d in range(1, SIDE):
                send_sum(k, h, d)

    def reduce_end(k):
        for h in range(2):
            value = sum1[k, h, y if h == 0 else x].astype(F32)
            for d in range(1, SIDE):
                arrived(in2.at[k, h, d - 1], r_recv.at[k, 1, h, d - 1])
                value = value + in2[k, h, d - 1].astype(F32)
            total[k, :, h * half : (h + 1) * half] = value

        def send():
            out_total[k] = total[k].astype(BF16)
            if k < 2:
                remote(
                    lambda: (
                        out_total.at[k],
                        from_odd.at[k],
                        odd_send.at[k],
                        odd_recv.at[k],
                        ((layer + 7) % 8, plane),
                    ),
                    is_odd,
                )
            else:
                remote(
                    lambda: (
                        out_total.at[k],
                        from_all.at[slot_of_all()],
                        all_send,
                        all_recv.at[slot_of_all()],
                        (3, plane),
                    ),
                    not_three,
                )

        pl.when(is_odd if k < 2 else not_three)(send)

    def slot_of_all():
        return layer - jnp.where(layer > 3, 1, 0)

    def whole_total(k):
        arrived(from_odd.at[k], odd_recv.at[k])
        return total[k] + from_odd[k].astype(F32)

    def divide(value, m=0):
        picks = jnp.where(
            lax.broadcasted_iota(jnp.int32, (value.shape[0], EXTRA), 1) < 3, 1.0, 0.0
        ).astype(BF16)
        parts = mats[m][:, :, :, :, size:].reshape(size, EXTRA)
        return value / dot_rows(picks, parts)

    def forward(residual):
        solved = dot_rows(residual.astype(BF16), whole(0)).astype(BF16)
        sep_y[...] = solved
        sep_z[...] = divide(solved.astype(F32))

    two_of = (layer // 4) * 4 + 1
    two_slot = (layer % 4) // 2

    leaf_part(0)
    leaf_part(1)
    reduce_first(0)
    mat_second(0)
    leaf_part(2)
    reduce_first(1)
    reduce_second(0)
    mat_second(1)
    reduce_end(0)
    mat_third(0)
    reduce_second(1)
    mat_second(2)

    @pl.when(is_one)
    def _():
        residual = whole_total(0)
        mat_end(0)
        forward(residual)
        remote(
            lambda: (
                sep_y,
                helped_y.at[1 - two_slot],
                y_send,
                y_recv.at[1 - two_slot],
                ((layer + 7 + 2 * two_slot) % 8, plane),
            ),
            is_one,
        )

    @pl.when(is_base)
    def _():
        remote(
            lambda: (sep_y, helped_y.at[0], y_pair_send, y_recv.at[0], (layer + 1, plane)),
            is_base,
        )

    reduce_first(2)
    reduce_end(1)
    mat_third(1)
    mat_first(3)
    mat_first(4)

    @pl.when(is_one)
    def _():
        mat_end(1)
        to_two[...] = (whole_total(1) - dot_rows(sep_y[...], whole(1))).astype(BF16)
        remote(
            lambda: (
                to_two,
                from_one.at[two_slot],
                two_send,
                two_recv.at[two_slot],
                (two_of, plane),
            ),
            is_one,
        )

    reduce_second(2)
    mat_third(2)
    reduce_end(2)
    mat_second(3)
    mat_second(4)

    @pl.when(is_helper)
    def _():
        mat_end(1)
        mat_end(2)
        for slot in range(2):
            arrived(helped_y.at[slot], y_recv.at[slot])
        helped[...] = dot_rows(helped_y[0], whole(1)) + dot_rows(helped_y[1], whole(2))

    def send_three(slot, when):
        remote(
            lambda: (
                to_three,
                from_two.at[slot()],
                three_send,
                three_recv.at[slot()],
                (3, plane),
            ),
            when,
        )

    @pl.when(is_seven)
    def _():
        to_three[...] = helped[...].astype(BF16)
        send_three(lambda: 2, is_seven)

    @pl.when(is_two)
    def _():
        mat_end(0)
        mat_end(1)
        for slot in range(2):
            arrived(from_one.at[slot], two_recv.at[slot])
        forward(from_one[0].astype(F32) + from_one[1].astype(F32))
        to_three[...] = dot_rows(sep_y[...], whole(1)).astype(BF16)
        send_three(lambda: layer // 4, is_two)

    diag_lanes = jnp.concatenate([diag[b : b + 1, :] for b in range(blocks)], axis=1)
    back[...] = leaf_y[...].astype(F32) / diag_lanes

    def finish(k, target, m=0):
        answer[k, core, y, x] = dot_cols(target.astype(BF16), whole(m)).astype(BF16)

    def own_answer(k):
        return answer.at[k, core, y, x]

    def send_answer(k, slot, layer_to, when):
        remote(
            lambda: (
                own_answer(k),
                own_answer(k),
                x_send.at[slot],
                x_recv.at[k],
                (layer_to(), plane),
            ),
            when,
        )

    @pl.when(is_three)
    def _():
        mat_end(0)
        residual = total[2] - helped[...]
        for slot in range(7):
            arrived(from_all.at[slot], all_recv.at[slot])
            residual = residual + from_all[slot].astype(F32)
        for slot in (2, 0, 1):
            arrived(from_two.at[slot], three_recv.at[slot])
            residual = residual - from_two[slot].astype(F32)
        forward(residual)
        finish(2, sep_z[...])
        for slot, layer_to in enumerate((1, 5, 7, 2, 4, 0, 6)):
            send_answer(2, slot, lambda layer_to=layer_to: layer_to, is_three)

    def send_carry(slot, to):
        remote(
            lambda: (
                carry.at[slot],
                carried,
                carry_send.at[to],
                carry_recv,
                ((layer + (7, 1, 2)[to]) % 8, plane),
            ),
            is_helper,
        )

    mat_third(3)
    mat_third(4)

    @pl.when(is_odd)
    def _():
        mat_end(3)

    @pl.when(is_two)
    def _():
        arrived(helped_y.at[0], y_recv.at[0])

    @pl.when(is_odd)
    def _():
        pair_z[...] = divide(helped_y[0].astype(F32), 3)
        mat_end(4)

    @pl.when(jnp.logical_not(is_three))
    def _():
        arrived(own_answer(2), x_recv.at[2])

    @pl.when(is_two)
    def _():
        finish(1, sep_z[...] - dot_cols(own_answer(2)[...], whole(1)))
        for slot, shift in enumerate((7, 1, 2)):
            send_answer(1, 7 + slot, lambda shift=shift: (layer + shift) % 8, is_two)

    def answer_parts(k):
        return (
            lambda y_at, x_at, core_at, at: answer.at[k, core_at, y_at, x_at, :, at],
            size,
            lambda *at: (a_send.at[(k,) + at], a_recv.at[(k,) + at]),
            lambda: (ac_send.at[k], ac_recv.at[k]),
        )

    def answer_first(k):
        gather_first(*answer_parts(k)[:3])

    def answer_second(k):
        gather_second(*answer_parts(k)[:3])

    def answer_third(k):
        gather_third(*answer_parts(k))

    def answer_end(k):
        gather_end(answer_parts(k)[0], ac_recv.at[k])

    @pl.when(is_helper)
    def _():
        for slot in range(2):
            term = dot_cols(own_answer(2)[...], whole(1 + slot))
            carry[slot] = term.astype(BF16)
            send_carry(slot, slot)
        send_carry(1, 2)

    answer_first(2)
    answer_second(2)

    @pl.when(jnp.logical_not(is_two))
    def _():
        arrived(own_answer(1), x_recv.at[1])

    @pl.when(jnp.logical_not(is_helper))
    def _():
        arrived(carried, carry_recv)

    @pl.when(is_helper)
    def _():
        carried[...] = carry[0]

    @pl.when(is_one)
    def _():
        term = dot_cols(own_answer(1)[...], whole(1))
        finish(0, sep_z[...] - carried[...].astype(F32) - term)

    @pl.when(is_odd)
    def _():
        term = dot_cols(own_answer(1)[...], whole(4))
        finish(0, pair_z[...] - carried[...].astype(F32) - term, 3)

    answer_first(0)

    own_rows_at = jnp.where(
        first_row + lax.broadcasted_iota(jnp.int32, (own_rows, size), 0)
        == lax.broadcasted_iota(jnp.int32, (own_rows, size), 1),
        1.0,
        0.0,
    ).astype(BF16)

    side_cols = right_sides // CORES

    def rows_out(k, side):
        value = dot_rows(own_rows_at, answer[k, side].reshape(side_cols, size)).astype(BF16)
        sep_out[0, k, :, pl.ds(pl.multiple_of(side * side_cols, side_cols), side_cols)] = value

    def leaf_back(k):
        answer_end(k)
        rows_out(k, core)
        rows_out(k, 1 - core)
        leaf_ym[...] = jnp.broadcast_to(mask_lanes(k), leaf_ym.shape).astype(BF16)
        value = answer.at[k]

        def tile(i, _):
            columns = pl.ds(pl.multiple_of(i * TILE, TILE), TILE)
            term = dot_cols(
                value[...].reshape(right_sides, size), couple[k, :, columns]
            ) * leaf_ym[:, columns].astype(F32)
            back[:, columns] = back[:, columns] - term
            return 0

        lax.fori_loop(0, size // TILE, tile, 0)

    def leaf_end(side):
        rows = pl.ds(pl.multiple_of(side * side_cols, side_cols), side_cols)

        def tile(i, _):
            start = pl.multiple_of(i * TILE, TILE)
            columns = pl.ds(start, TILE)
            term = dot_cols(answer[0, side].reshape(side_cols, size), couple[0, :, columns])
            target = (back[rows, columns] - term * leaf_ym[0:1, columns].astype(F32)).astype(BF16)
            for j in range(TILE // blk):
                b = i * (TILE // blk) + j
                solved = dot_rows(lower_t[b], target[:, j * blk : (j + 1) * blk])
                leaf_out[b, :, rows] = solved.astype(BF16)
            return 0

        lax.fori_loop(0, size // TILE, tile, 0)

    answer_first(1)
    answer_second(1)
    answer_third(2)
    answer_second(0)
    leaf_back(2)
    answer_third(1)
    leaf_back(1)
    answer_third(0)
    leaf_ym[0:16, :] = jnp.broadcast_to(mask_lanes(0), (16, size)).astype(BF16)
    rows_out(0, core)
    leaf_end(core)
    answer_end(0)
    leaf_end(1 - core)
    rows_out(0, 1 - core)

    for when, make in sends:
        if when is None:
            make().wait_send()
    for group in (has_first, is_helper, is_one, is_odd, is_two, is_three, not_three, is_seven, is_base):

        @pl.when(group)
        def _(group=group):
            for when, make in sends:
                if when is group:
                    make().wait_send()


def copy_kernel(leaf_ref, sep_ref, leaf_out, sep_out):
    leaf_out[...] = leaf_ref[...]
    sep_out[...] = sep_ref[...]


def body(
    leaf_rhs,
    leaf_inverse,
    leaf_couple,
    couple_mask,
    leaf_diag,
    sep_rhs,
    sep_inverse,
    sep_couple,
    sep_diag,
):
    blocks, levels, size, blk = leaf_couple.shape
    right_sides = leaf_rhs.shape[2]
    own_rows = sep_rhs.shape[1]
    cols = right_sides // (SIDE * SIDE * CORES)
    half = size // 2
    grid = (SIDE, SIDE, CORES)
    sides = (CORES, SIDE, SIDE)
    vmem = pltpu.VMEM
    dma = pltpu.SemaphoreType.DMA
    hops = (levels, 2, 2, SIDE - 1)
    scratch = [
        vmem(leaf_rhs.shape, BF16),
        vmem(leaf_inverse.shape, BF16),
        vmem((levels, size, blocks * blk), BF16),
        vmem(leaf_diag.shape, F32),
        vmem((levels, own_rows, right_sides), BF16),
        vmem((own_rows, size), BF16),
        vmem(sep_diag.shape, F32),
        vmem(grid + (own_rows, size + EXTRA), BF16),
        vmem(grid + (own_rows, size), BF16),
        vmem(grid + (own_rows, size), BF16),
        vmem(grid + (own_rows, size + EXTRA), BF16),
        vmem(grid + (own_rows, size), BF16),
        vmem((own_rows, size), BF16),
        vmem((right_sides, blocks * blk), BF16),
        vmem((right_sides, blocks * blk), BF16),
        vmem(leaf_inverse.shape, BF16),
        vmem((levels,) + sides + (cols, size), BF16),
        vmem((levels, SIDE, SIDE, cols, size), BF16),
        vmem((levels, SIDE, SIDE, cols, size), BF16),
        vmem((levels, 2, SIDE - 1, SIDE, cols, half), BF16),
        vmem((levels, 2, SIDE, cols, half), BF16),
        vmem((levels, 2, SIDE - 1, cols, half), BF16),
        vmem((levels, cols, size), F32),
        vmem((levels, cols, size), BF16),
        vmem((levels, cols, size), BF16),
        vmem((7, cols, size), BF16),
        vmem((cols, size), BF16),
        vmem((2, cols, size), BF16),
        vmem((cols, size), BF16),
        vmem((3, cols, size), BF16),
        vmem((cols, size), BF16),
        vmem((2, cols, size), BF16),
        vmem((cols, size), F32),
        vmem((2, cols, size), BF16),
        vmem((cols, size), BF16),
        vmem((cols, size), F32),
        vmem((cols, size), F32),
        vmem((levels,) + sides + (cols, size), BF16),
        vmem((right_sides, blocks * blk), F32),
        dma((12,)),
        dma((levels, blocks)),
        dma((5,) + hops[1:]),
        dma((5,) + hops[1:]),
        dma((5,)),
        dma((5,)),
        dma(hops),
        dma(hops),
        dma((levels,)),
        dma((levels,)),
        dma(hops),
        dma(hops),
        dma((levels,)),
        dma((levels,)),
        dma((2,)),
        dma((2,)),
        dma,
        dma((2,)),
        dma,
        dma((3,)),
        dma,
        dma((7,)),
        dma,
        dma,
        dma((2,)),
        dma((3,)),
        dma,
        dma((11,)),
        dma((levels,)),
    ]
    any_space = pl.BlockSpec(memory_space=pl.ANY)
    in_vmem = pl.BlockSpec(memory_space=pltpu.VMEM)
    outs = pl.pallas_call(
        kernel,
        out_shape=(
            jax.ShapeDtypeStruct(leaf_rhs.shape, BF16),
            jax.ShapeDtypeStruct((1, levels, own_rows, right_sides), BF16),
        ),
        in_specs=[pl.BlockSpec(memory_space=pltpu.SMEM)] + [any_space] * 8,
        out_specs=(in_vmem, in_vmem),
        scratch_shapes=scratch,
        compiler_params=pltpu.CompilerParams(
            collective_id=0, has_side_effects=True, vmem_limit_bytes=56 * 2**20
        ),
    )(
        couple_mask.T,
        leaf_rhs,
        leaf_inverse,
        leaf_couple,
        leaf_diag,
        sep_rhs,
        sep_inverse,
        sep_couple,
        sep_diag,
    )
    return pl.pallas_call(
        copy_kernel,
        out_shape=tuple(jax.ShapeDtypeStruct(out.shape, out.dtype) for out in outs),
        in_specs=[in_vmem] * 2,
        out_specs=(in_vmem, in_vmem),
    )(*outs)


def solution(mesh):
    in_specs = (
        P(("layer", "plane"), None, None),
        P(("layer", "plane"), None, None),
        P(("layer", "plane"), None, None, None),
        P(("layer", "plane"), None),
        P(("layer", "plane"), None),
        P(None, "plane", None),
        P(None, "plane", None),
        P(None, None, "plane", None),
        P(None, "plane"),
    )
    out_specs = (P(("layer", "plane"), None, None), P("layer", None, "plane", None))
    return jax.shard_map(body, mesh=mesh, in_specs=in_specs, out_specs=out_specs, check_vma=False)
```

```python
import jax
import jax.numpy as jnp
from jax import lax
from jax.experimental import pallas as pl
from jax.experimental.pallas import tpu as pltpu
from jax.sharding import PartitionSpec as P

BF16 = jnp.bfloat16
F32 = jnp.float32
SIDE = 4
CORES = 2
EXTRA = 128
TILE = 256


def dot_rows(left, right):
    return lax.dot_general(left, right, (((1,), (1,)), ((), ())), preferred_element_type=F32)


def dot_cols(left, right):
    return lax.dot_general(left, right, (((1,), (0,)), ((), ())), preferred_element_type=F32)


def unit_lower(block, first_row):
    row_ids = first_row + lax.broadcasted_iota(jnp.int32, block.shape, 0)
    col_ids = lax.broadcasted_iota(jnp.int32, block.shape, 1)
    value = block.astype(F32)
    value = jnp.where(col_ids < row_ids, value, 0.0)
    return jnp.where(col_ids == row_ids, 1.0, value).astype(BF16)


def kernel(
    mask_ref,
    rhs_hbm,
    inverse_hbm,
    couple_hbm,
    diag_hbm,
    sep_rhs_hbm,
    sep_inverse_hbm,
    sep_couple_hbm,
    sep_diag_hbm,
    leaf_out,
    sep_out,
    rhs,
    inverse,
    couple,
    diag,
    sep_rhs,
    own_inverse,
    own_diag,
    mat0,
    mat1,
    mat2,
    leaf_y,
    leaf_ym,
    lower_t,
    part,
    paired,
    chip_sum,
    in1,
    sum1,
    in2,
    total,
    from_odd,
    out_total,
    from_all,
    to_two,
    from_one,
    to_three,
    from_two,
    sep_y,
    helped_y,
    helped,
    carry,
    carried,
    sep_z,
    answer,
    back,
    local_sem,
    couple_sem,
    g_send,
    g_recv,
    gc_send,
    gc_recv,
    r_send,
    r_recv,
    rc_send,
    rc_recv,
    a_send,
    a_recv,
    ac_send,
    ac_recv,
    odd_send,
    odd_recv,
    two_send,
    two_recv,
    three_send,
    three_recv,
    all_send,
    all_recv,
    y_send,
    y_recv,
    carry_send,
    carry_recv,
    x_send,
    x_recv,
):
    blocks, blk, right_sides = rhs.shape
    own_rows = own_inverse.shape[0]
    size = own_inverse.shape[1]
    half = size // 2
    layer = lax.axis_index("layer")
    plane = lax.axis_index("plane")
    layers = lax.axis_size("layer")
    y = plane // (SIDE * CORES)
    x = (plane // CORES) % SIDE
    core = plane % CORES
    first_row = plane * own_rows

    def at_plane(y_at, x_at, core_at):
        return (layer, (y_at * SIDE + x_at) * CORES + core_at)

    def x_peer(d):
        return at_plane(y, (x + d) % SIDE, core)

    def y_peer(d):
        return at_plane((y + d) % SIDE, x, core)

    sibling = at_plane(y, x, 1 - core)

    is_one = layer % 2 == 0
    is_odd = layer % 2 == 1
    is_two = layer % 4 == 1
    is_three = layer == 3
    not_three = layer != 3
    is_helper = layer % 4 == 3
    is_seven = layer == 7
    has_first = layer != 7
    sep_of = [layer // 2, 4 + layer // 4, 6 + layer * 0]
    own_sep = jnp.where(is_one, layer // 2, jnp.where(is_two, 4 + layer // 4, 6))

    second_sep = jnp.where(is_helper, layer // 2, own_sep)
    second_block = jnp.where(is_helper, 1, 0)
    third_sep = ((layer + 1) % 8) // 2

    sends = []

    def remote(parts, when=None):
        def make():
            src, dst, send_sem, recv_sem, device = parts()
            return pltpu.make_async_remote_copy(
                src_ref=src,
                dst_ref=dst,
                send_sem=send_sem,
                recv_sem=recv_sem,
                device_id=device,
                device_id_type=pl.DeviceIdType.MESH,
            )

        make().start()
        sends.append((when, make))

    def only(when, act):
        if when is None:
            act()
        else:
            pl.when(when)(act)

    def arrived(dst, sem):
        pltpu.make_async_copy(dst, dst, sem).wait()

    barrier = pltpu.get_barrier_semaphore()
    peers = [sibling]
    for d in range(1, SIDE):
        peers += [x_peer(d), y_peer(d)]
    for d in range(1, 8):
        peers.append(((layer + d) % 8, plane))
    for peer in peers:
        pl.semaphore_signal(barrier, inc=1, device_id=peer, device_id_type=pl.DeviceIdType.MESH)

    local = [
        pltpu.make_async_copy(sep_inverse_hbm.at[own_sep], own_inverse, local_sem.at[0]),
        pltpu.make_async_copy(sep_diag_hbm, own_diag, local_sem.at[1]),
        pltpu.make_async_copy(
            sep_couple_hbm.at[second_sep, second_block], mat1.at[y, x, core], local_sem.at[2]
        ),
        pltpu.make_async_copy(
            sep_couple_hbm.at[third_sep, 1], mat2.at[y, x, core], local_sem.at[3]
        ),
        pltpu.make_async_copy(inverse_hbm, inverse, local_sem.at[4]),
        pltpu.make_async_copy(rhs_hbm, rhs, local_sem.at[5]),
        pltpu.make_async_copy(diag_hbm, diag, local_sem.at[6]),
        pltpu.make_async_copy(sep_rhs_hbm.at[sep_of[0]], sep_rhs.at[0], local_sem.at[7]),
        pltpu.make_async_copy(sep_rhs_hbm.at[sep_of[1]], sep_rhs.at[1], local_sem.at[8]),
        pltpu.make_async_copy(sep_rhs_hbm.at[sep_of[2]], sep_rhs.at[2], local_sem.at[9]),
    ]
    for copy in local:
        copy.start()
    couples = []
    for k in range(3):
        couples.append(
            [
                pltpu.make_async_copy(
                    couple_hbm.at[b, k], couple.at[k, :, pl.ds(b * blk, blk)], couple_sem.at[k, b]
                )
                for b in range(blocks)
            ]
        )
        for copy in couples[k]:
            copy.start()

    def send_first(pick, width, sems, h, d, when):
        def parts():
            ref = pick(y, x, core, lanes(width, h))
            send, recv = sems(0, h, d - 1)
            return ref, ref, send, recv, x_peer(d) if h == 0 else y_peer(d)

        remote(parts, when)

    def send_second(pick, width, sems, h, d, when):
        def parts():
            everywhere = slice(None)
            if h == 0:
                ref = pick(y, everywhere, core, lanes(width, h))
            else:
                ref = pick(everywhere, x, core, lanes(width, h))
            send, recv = sems(1, h, d - 1)
            return ref, ref, send, recv, y_peer(d) if h == 0 else x_peer(d)

        remote(parts, when)

    def lanes(width, h):
        return pl.ds(0, half) if h == 0 else pl.ds(half, width - half)

    def gather_first(pick, width, sems, when=None):
        for h in range(2):
            for d in range(1, SIDE):
                send_first(pick, width, sems, h, d, when)

    def gather_second(pick, width, sems, when=None):
        for h in range(2):
            for d in range(1, SIDE):
                if h == 0:
                    ref = pick(y, (x - d + SIDE) % SIDE, core, lanes(width, h))
                else:
                    ref = pick((y - d + SIDE) % SIDE, x, core, lanes(width, h))
                arrived(ref, sems(0, h, d - 1)[1])
            for d in range(1, SIDE):
                send_second(pick, width, sems, h, d, when)

    def gather_third(pick, width, sems, c_sems, when=None):
        everywhere = slice(None)
        for h in range(2):
            for d in range(1, SIDE):
                if h == 0:
                    ref = pick((y - d + SIDE) % SIDE, everywhere, core, lanes(width, h))
                else:
                    ref = pick(everywhere, (x - d + SIDE) % SIDE, core, lanes(width, h))
                arrived(ref, sems(1, h, d - 1)[1])

        def parts():
            ref = pick(everywhere, everywhere, core, everywhere)
            return (ref, ref) + c_sems() + (sibling,)

        remote(parts, when)

    def gather_end(pick, c_recv):
        everywhere = slice(None)
        arrived(pick(everywhere, everywhere, 1 - core, everywhere), c_recv)

    mats = [mat0, mat1, mat2]
    uses = [has_first, None, is_helper]

    def whole(m):
        return mats[m][:, :, :, :, 0:size].reshape(size, size)

    def mat_parts(m):
        return (
            lambda y_at, x_at, core_at, at: mats[m].at[y_at, x_at, core_at, :, at],
            mats[m].shape[-1],
            lambda *at: (g_send.at[(m,) + at], g_recv.at[(m,) + at]),
            lambda: (gc_send.at[m], gc_recv.at[m]),
        )

    def mat_first(m):
        only(uses[m], lambda: gather_first(*mat_parts(m)[:3], uses[m]))

    def mat_second(m):
        only(uses[m], lambda: gather_second(*mat_parts(m)[:3], uses[m]))

    def mat_third(m):
        only(uses[m], lambda: gather_third(*mat_parts(m), uses[m]))

    def mat_end(m):
        gather_end(mat_parts(m)[0], gc_recv.at[m])

    local[0].wait()
    local[1].wait()
    eye = lax.broadcasted_iota(jnp.int32, (own_rows, own_rows), 0) == lax.broadcasted_iota(
        jnp.int32, (own_rows, own_rows), 1
    )
    sep_rows = lax.broadcasted_iota(jnp.int32, own_diag.shape, 0) == own_sep
    diag_row = jnp.sum(jnp.where(sep_rows, own_diag[...], 0.0), axis=0, keepdims=True)
    diag_col = jnp.sum(jnp.where(eye, diag_row, 0.0), axis=1, keepdims=True)
    high = diag_col.astype(BF16).astype(F32)
    middle = (diag_col - high).astype(BF16).astype(F32)
    low = diag_col - high - middle
    lane = lax.broadcasted_iota(jnp.int32, (own_rows, EXTRA), 1)
    beside = jnp.where(
        lane == 0, high, jnp.where(lane == 1, middle, jnp.where(lane == 2, low, 0.0))
    ).astype(BF16)
    mat0[y, x, core, :, 0:size] = unit_lower(own_inverse[...], first_row)
    mat0[y, x, core, :, size:] = beside
    for i in range(4, 10):
        local[i].wait()

    def solve_leaf(b, _):
        lower = unit_lower(inverse[b], 0)
        lower_t[b] = lower.astype(F32).T.astype(BF16)
        rhs_t = rhs[b].T
        columns = pl.ds(pl.multiple_of(b * blk, blk), blk)
        leaf_y[:, columns] = dot_rows(rhs_t, lower).astype(BF16)
        return 0

    lax.fori_loop(0, blocks, solve_leaf, 0)

    pl.semaphore_wait(barrier, len(peers))
    mat_first(0)
    local[2].wait()
    local[3].wait()
    mat_first(1)
    mat_first(2)

    block_of = lax.broadcasted_iota(jnp.int32, (1, blocks * blk), 1) // blk

    def mask_lanes(k):
        result = jnp.zeros((1, blocks * blk), F32)
        for b in range(blocks):
            result = result + jnp.where(block_of == b, mask_ref[k, b].astype(F32), 0.0)
        return result

    def leaf_part(k):
        for copy in couples[k]:
            copy.wait()
        leaf_ym[...] = leaf_y[...] * mask_lanes(k).astype(BF16)
        rhs_t = sep_rhs[k].T
        adds = layer % (2 ** (k + 1)) == 0
        first = jnp.where(adds, first_row, size)

        def tile(i, _):
            start = pl.multiple_of(i * TILE, TILE)
            columns = pl.ds(start, TILE)
            rows_at = first + lax.broadcasted_iota(jnp.int32, (own_rows, TILE), 0)
            cols_at = start + lax.broadcasted_iota(jnp.int32, (own_rows, TILE), 1)
            place = jnp.where(rows_at == cols_at, 1.0, 0.0).astype(BF16)
            term = dot_cols(rhs_t, place) - dot_rows(leaf_ym[...], couple[k, columns, :])
            part[k, :, :, :, :, columns] = term.astype(BF16).reshape(
                part.shape[1:-1] + (TILE,)
            )
            return 0

        lax.fori_loop(0, size // TILE, tile, 0)
        remote(
            lambda: (
                part.at[k, 1 - core],
                paired.at[k],
                rc_send.at[k],
                rc_recv.at[k],
                sibling,
            )
        )

    def reduce_first(k):
        arrived(paired.at[k], rc_recv.at[k])
        chip_sum[k] = (part[k, core].astype(F32) + paired[k].astype(F32)).astype(BF16)
        for h in range(2):
            for d in range(1, SIDE):
                send_part(k, h, d)

    def send_part(k, h, d):
        def parts():
            if h == 0:
                ref = chip_sum.at[k, :, (x + d) % SIDE, :, pl.ds(0, half)]
            else:
                ref = chip_sum.at[k, (y + d) % SIDE, :, :, pl.ds(half, half)]
            return (
                ref,
                in1.at[k, h, d - 1],
                r_send.at[k, 0, h, d - 1],
                r_recv.at[k, 0, h, d - 1],
                x_peer(d) if h == 0 else y_peer(d),
            )

        remote(parts)

    def send_sum(k, h, d):
        remote(
            lambda: (
                sum1.at[k, h, ((y if h == 0 else x) + d) % SIDE],
                in2.at[k, h, d - 1],
                r_send.at[k, 1, h, d - 1],
                r_recv.at[k, 1, h, d - 1],
                y_peer(d) if h == 0 else x_peer(d),
            )
        )

    def reduce_second(k):
        for h in range(2):
            if h == 0:
                value = chip_sum[k, :, x, :, 0:half].astype(F32)
            else:
                value = chip_sum[k, y, :, :, half:].astype(F32)
            for d in range(1, SIDE):
                arrived(in1.at[k, h, d - 1], r_recv.at[k, 0, h, d - 1])
                value = value + in1[k, h, d - 1].astype(F32)
            sum1[k, h] = value.astype(BF16)
            for d in range(1, SIDE):
                send_sum(k, h, d)

    def reduce_end(k):
        for h in range(2):
            value = sum1[k, h, y if h == 0 else x].astype(F32)
            for d in range(1, SIDE):
                arrived(in2.at[k, h, d - 1], r_recv.at[k, 1, h, d - 1])
                value = value + in2[k, h, d - 1].astype(F32)
            total[k, :, h * half : (h + 1) * half] = value

        def send():
            out_total[k] = total[k].astype(BF16)
            if k < 2:
                remote(
                    lambda: (
                        out_total.at[k],
                        from_odd.at[k],
                        odd_send.at[k],
                        odd_recv.at[k],
                        ((layer + 7) % 8, plane),
                    ),
                    is_odd,
                )
            else:
                remote(
                    lambda: (
                        out_total.at[k],
                        from_all.at[slot_of_all()],
                        all_send,
                        all_recv.at[slot_of_all()],
                        (3, plane),
                    ),
                    not_three,
                )

        pl.when(is_odd if k < 2 else not_three)(send)

    def slot_of_all():
        return layer - jnp.where(layer > 3, 1, 0)

    def whole_total(k):
        arrived(from_odd.at[k], odd_recv.at[k])
        return total[k] + from_odd[k].astype(F32)

    def divide(value):
        picks = jnp.where(
            lax.broadcasted_iota(jnp.int32, (value.shape[0], EXTRA), 1) < 3, 1.0, 0.0
        ).astype(BF16)
        parts = mat0[:, :, :, :, size:].reshape(size, EXTRA)
        return value / dot_rows(picks, parts)

    def forward(residual):
        solved = dot_rows(residual.astype(BF16), whole(0)).astype(BF16)
        sep_y[...] = solved
        sep_z[...] = divide(solved.astype(F32))

    two_of = (layer // 4) * 4 + 1
    two_slot = (layer % 4) // 2

    leaf_part(0)
    leaf_part(1)
    reduce_first(0)
    mat_second(0)
    leaf_part(2)
    reduce_first(1)
    reduce_second(0)
    mat_second(1)
    reduce_end(0)
    mat_third(0)
    reduce_second(1)
    reduce_first(2)
    mat_second(2)

    @pl.when(is_one)
    def _():
        residual = whole_total(0)
        mat_end(0)
        forward(residual)
        remote(
            lambda: (
                sep_y,
                helped_y.at[1 - two_slot],
                y_send,
                y_recv.at[1 - two_slot],
                ((layer + 7 + 2 * two_slot) % 8, plane),
            ),
            is_one,
        )

    reduce_end(1)
    mat_third(1)
    reduce_second(2)

    @pl.when(is_one)
    def _():
        mat_end(1)
        to_two[...] = (whole_total(1) - dot_rows(sep_y[...], whole(1))).astype(BF16)
        remote(
            lambda: (
                to_two,
                from_one.at[two_slot],
                two_send,
                two_recv.at[two_slot],
                (two_of, plane),
            ),
            is_one,
        )

    reduce_end(2)
    mat_third(2)

    @pl.when(is_helper)
    def _():
        mat_end(1)
        mat_end(2)
        for slot in range(2):
            arrived(helped_y.at[slot], y_recv.at[slot])
        helped[...] = dot_rows(helped_y[0], whole(1)) + dot_rows(helped_y[1], whole(2))

    def send_three(slot, when):
        remote(
            lambda: (
                to_three,
                from_two.at[slot()],
                three_send,
                three_recv.at[slot()],
                (3, plane),
            ),
            when,
        )

    @pl.when(is_seven)
    def _():
        to_three[...] = helped[...].astype(BF16)
        send_three(lambda: 2, is_seven)

    @pl.when(is_two)
    def _():
        mat_end(0)
        mat_end(1)
        for slot in range(2):
            arrived(from_one.at[slot], two_recv.at[slot])
        forward(from_one[0].astype(F32) + from_one[1].astype(F32))
        to_three[...] = dot_rows(sep_y[...], whole(1)).astype(BF16)
        send_three(lambda: layer // 4, is_two)

    diag_lanes = jnp.concatenate([diag[b : b + 1, :] for b in range(blocks)], axis=1)
    back[...] = leaf_y[...].astype(F32) / diag_lanes

    def finish(k, target):
        answer[k, core, y, x] = dot_cols(target.astype(BF16), whole(0)).astype(BF16)

    def own_answer(k):
        return answer.at[k, core, y, x]

    def send_answer(k, slot, layer_to, when):
        remote(
            lambda: (
                own_answer(k),
                own_answer(k),
                x_send.at[slot],
                x_recv.at[k],
                (layer_to(), plane),
            ),
            when,
        )

    @pl.when(is_three)
    def _():
        mat_end(0)
        residual = total[2] - helped[...]
        for slot in range(7):
            arrived(from_all.at[slot], all_recv.at[slot])
            residual = residual + from_all[slot].astype(F32)
        for slot in (2, 0, 1):
            arrived(from_two.at[slot], three_recv.at[slot])
            residual = residual - from_two[slot].astype(F32)
        forward(residual)
        finish(2, sep_z[...])
        for slot, layer_to in enumerate((1, 5, 7, 2, 4, 0, 6)):
            send_answer(2, slot, lambda layer_to=layer_to: layer_to, is_three)

    def send_carry(slot):
        remote(
            lambda: (
                carry.at[slot],
                carried,
                carry_send.at[slot],
                carry_recv,
                ((layer + 7 + 2 * slot) % 8, plane),
            ),
            is_helper,
        )

    @pl.when(jnp.logical_not(is_three))
    def _():
        arrived(own_answer(2), x_recv.at[2])

    @pl.when(is_two)
    def _():
        finish(1, sep_z[...] - dot_cols(own_answer(2)[...], whole(1)))
        for slot, shift in enumerate((7, 1, 2)):
            send_answer(1, 7 + slot, lambda shift=shift: (layer + shift) % 8, is_two)

    def answer_parts(k):
        return (
            lambda y_at, x_at, core_at, at: answer.at[k, core_at, y_at, x_at, :, at],
            size,
            lambda *at: (a_send.at[(k,) + at], a_recv.at[(k,) + at]),
            lambda: (ac_send.at[k], ac_recv.at[k]),
        )

    def answer_first(k, when=None):
        gather_first(*answer_parts(k)[:3], when)

    def answer_second(k):
        gather_second(*answer_parts(k)[:3])

    def answer_third(k):
        gather_third(*answer_parts(k))

    def answer_end(k):
        gather_end(answer_parts(k)[0], ac_recv.at[k])

    @pl.when(is_helper)
    def _():
        for slot in range(2):
            term = dot_cols(own_answer(2)[...], whole(1 + slot))
            carry[slot] = term.astype(BF16)
            send_carry(slot)

    answer_first(2)
    answer_second(2)

    @pl.when(jnp.logical_not(is_two))
    def _():
        arrived(own_answer(1), x_recv.at[1])

    @pl.when(is_one)
    def _():
        term = dot_cols(own_answer(1)[...], whole(1))
        arrived(carried, carry_recv)
        finish(0, sep_z[...] - carried[...].astype(F32) - term)
        send_answer(0, 10, lambda: layer + 1, is_one)
        answer_first(0, is_one)

    own_rows_at = jnp.where(
        first_row + lax.broadcasted_iota(jnp.int32, (own_rows, size), 0)
        == lax.broadcasted_iota(jnp.int32, (own_rows, size), 1),
        1.0,
        0.0,
    ).astype(BF16)

    side_cols = right_sides // CORES

    def rows_out(k, side):
        value = dot_rows(own_rows_at, answer[k, side].reshape(side_cols, size)).astype(BF16)
        sep_out[0, k, :, pl.ds(pl.multiple_of(side * side_cols, side_cols), side_cols)] = value

    def leaf_back(k):
        answer_end(k)
        rows_out(k, core)
        rows_out(k, 1 - core)
        leaf_ym[...] = jnp.broadcast_to(mask_lanes(k), leaf_ym.shape).astype(BF16)
        value = answer.at[k]

        def tile(i, _):
            columns = pl.ds(pl.multiple_of(i * TILE, TILE), TILE)
            term = dot_cols(
                value[...].reshape(right_sides, size), couple[k, :, columns]
            ) * leaf_ym[:, columns].astype(F32)
            back[:, columns] = back[:, columns] - term
            return 0

        lax.fori_loop(0, size // TILE, tile, 0)

    def leaf_end(side):
        rows = pl.ds(pl.multiple_of(side * side_cols, side_cols), side_cols)

        def tile(i, _):
            start = pl.multiple_of(i * TILE, TILE)
            columns = pl.ds(start, TILE)
            term = dot_cols(answer[0, side].reshape(side_cols, size), couple[0, :, columns])
            target = (back[rows, columns] - term * leaf_ym[0:1, columns].astype(F32)).astype(BF16)
            for j in range(TILE // blk):
                b = i * (TILE // blk) + j
                solved = dot_rows(lower_t[b], target[:, j * blk : (j + 1) * blk])
                leaf_out[b, :, rows] = solved.astype(BF16)
            return 0

        lax.fori_loop(0, size // TILE, tile, 0)

    answer_first(1)
    answer_second(1)

    @pl.when(is_odd)
    def _():
        arrived(own_answer(0), x_recv.at[0])
        answer_first(0, is_odd)

    answer_third(2)
    answer_second(0)
    leaf_back(2)
    answer_third(1)
    leaf_back(1)
    answer_third(0)
    leaf_ym[0:16, :] = jnp.broadcast_to(mask_lanes(0), (16, size)).astype(BF16)
    rows_out(0, core)
    leaf_end(core)
    answer_end(0)
    leaf_end(1 - core)
    rows_out(0, 1 - core)

    for when, make in sends:
        if when is None:
            make().wait_send()
    for group in (has_first, is_helper, is_one, is_odd, is_two, is_three, not_three, is_seven):

        @pl.when(group)
        def _(group=group):
            for when, make in sends:
                if when is group:
                    make().wait_send()


def copy_kernel(leaf_ref, sep_ref, leaf_out, sep_out):
    leaf_out[...] = leaf_ref[...]
    sep_out[...] = sep_ref[...]


def body(
    leaf_rhs,
    leaf_inverse,
    leaf_couple,
    couple_mask,
    leaf_diag,
    sep_rhs,
    sep_inverse,
    sep_couple,
    sep_diag,
):
    blocks, levels, size, blk = leaf_couple.shape
    right_sides = leaf_rhs.shape[2]
    own_rows = sep_rhs.shape[1]
    cols = right_sides // (SIDE * SIDE * CORES)
    half = size // 2
    grid = (SIDE, SIDE, CORES)
    sides = (CORES, SIDE, SIDE)
    vmem = pltpu.VMEM
    dma = pltpu.SemaphoreType.DMA
    hops = (levels, 2, 2, SIDE - 1)
    scratch = [
        vmem(leaf_rhs.shape, BF16),
        vmem(leaf_inverse.shape, BF16),
        vmem((levels, size, blocks * blk), BF16),
        vmem(leaf_diag.shape, F32),
        vmem((levels, own_rows, right_sides), BF16),
        vmem((own_rows, size), BF16),
        vmem(sep_diag.shape, F32),
        vmem(grid + (own_rows, size + EXTRA), BF16),
        vmem(grid + (own_rows, size), BF16),
        vmem(grid + (own_rows, size), BF16),
        vmem((right_sides, blocks * blk), BF16),
        vmem((right_sides, blocks * blk), BF16),
        vmem(leaf_inverse.shape, BF16),
        vmem((levels,) + sides + (cols, size), BF16),
        vmem((levels, SIDE, SIDE, cols, size), BF16),
        vmem((levels, SIDE, SIDE, cols, size), BF16),
        vmem((levels, 2, SIDE - 1, SIDE, cols, half), BF16),
        vmem((levels, 2, SIDE, cols, half), BF16),
        vmem((levels, 2, SIDE - 1, cols, half), BF16),
        vmem((levels, cols, size), F32),
        vmem((levels, cols, size), BF16),
        vmem((levels, cols, size), BF16),
        vmem((7, cols, size), BF16),
        vmem((cols, size), BF16),
        vmem((2, cols, size), BF16),
        vmem((cols, size), BF16),
        vmem((3, cols, size), BF16),
        vmem((cols, size), BF16),
        vmem((2, cols, size), BF16),
        vmem((cols, size), F32),
        vmem((2, cols, size), BF16),
        vmem((cols, size), BF16),
        vmem((cols, size), F32),
        vmem((levels,) + sides + (cols, size), BF16),
        vmem((right_sides, blocks * blk), F32),
        dma((10,)),
        dma((levels, blocks)),
        dma(hops),
        dma(hops),
        dma((levels,)),
        dma((levels,)),
        dma(hops),
        dma(hops),
        dma((levels,)),
        dma((levels,)),
        dma(hops),
        dma(hops),
        dma((levels,)),
        dma((levels,)),
        dma((2,)),
        dma((2,)),
        dma,
        dma((2,)),
        dma,
        dma((3,)),
        dma,
        dma((7,)),
        dma,
        dma((2,)),
        dma((2,)),
        dma,
        dma((11,)),
        dma((levels,)),
    ]
    any_space = pl.BlockSpec(memory_space=pl.ANY)
    in_vmem = pl.BlockSpec(memory_space=pltpu.VMEM)
    leaf_block = pl.BlockSpec((blocks // 4,) + leaf_rhs.shape[1:], lambda i: (i, 0, 0))
    sep_block = pl.BlockSpec((1, levels, own_rows, right_sides), lambda i: (0, 0, 0, 0))
    outs = pl.pallas_call(
        kernel,
        out_shape=(
            jax.ShapeDtypeStruct(leaf_rhs.shape, BF16),
            jax.ShapeDtypeStruct((1, levels, own_rows, right_sides), BF16),
        ),
        in_specs=[pl.BlockSpec(memory_space=pltpu.SMEM)] + [any_space] * 8,
        out_specs=(in_vmem, in_vmem),
        scratch_shapes=scratch,
        compiler_params=pltpu.CompilerParams(
            collective_id=0, has_side_effects=True, vmem_limit_bytes=56 * 2**20
        ),
    )(
        couple_mask.T,
        leaf_rhs,
        leaf_inverse,
        leaf_couple,
        leaf_diag,
        sep_rhs,
        sep_inverse,
        sep_couple,
        sep_diag,
    )
    return pl.pallas_call(
        copy_kernel,
        out_shape=tuple(jax.ShapeDtypeStruct(out.shape, out.dtype) for out in outs),
        grid=(4,),
        in_specs=[leaf_block, sep_block],
        out_specs=(leaf_block, sep_block),
    )(*outs)


def solution(mesh):
    in_specs = (
        P(("layer", "plane"), None, None),
        P(("layer", "plane"), None, None),
        P(("layer", "plane"), None, None, None),
        P(("layer", "plane"), None),
        P(("layer", "plane"), None),
        P(None, "plane", None),
        P(None, "plane", None),
        P(None, None, "plane", None),
        P(None, "plane"),
    )
    out_specs = (P(("layer", "plane"), None, None), P("layer", None, "plane", None))
    return jax.shard_map(body, mesh=mesh, in_specs=in_specs, out_specs=out_specs, check_vma=False)
```

```python
import jax
import jax.numpy as jnp
from jax import lax
from jax.experimental import pallas as pl
from jax.experimental.pallas import tpu as pltpu
from jax.sharding import PartitionSpec as P

BF16 = jnp.bfloat16
F32 = jnp.float32
SIDE = 4
CORES = 2
EXTRA = 128
TILE = 256


def dot_rows(left, right):
    return lax.dot_general(left, right, (((1,), (1,)), ((), ())), preferred_element_type=F32)


def dot_cols(left, right):
    return lax.dot_general(left, right, (((1,), (0,)), ((), ())), preferred_element_type=F32)


def unit_lower(block, first_row):
    row_ids = first_row + lax.broadcasted_iota(jnp.int32, block.shape, 0)
    col_ids = lax.broadcasted_iota(jnp.int32, block.shape, 1)
    value = block.astype(F32)
    value = jnp.where(col_ids < row_ids, value, 0.0)
    return jnp.where(col_ids == row_ids, 1.0, value).astype(BF16)


def kernel(
    mask_ref,
    rhs_hbm,
    inverse_hbm,
    couple_hbm,
    diag_hbm,
    sep_rhs_hbm,
    sep_inverse_hbm,
    sep_couple_hbm,
    sep_diag_hbm,
    leaf_out,
    sep_out,
    rhs,
    inverse,
    couple,
    diag,
    sep_rhs,
    own_inverse,
    own_diag,
    mat0,
    mat1,
    mat2,
    leaf_y,
    leaf_ym,
    lower_t,
    part,
    paired,
    chip_sum,
    in1,
    sum1,
    in2,
    total,
    from_odd,
    out_total,
    from_all,
    to_two,
    from_one,
    to_three,
    from_two,
    sep_y,
    helped_y,
    helped,
    carry,
    carried,
    sep_z,
    answer,
    back,
    local_sem,
    couple_sem,
    g_send,
    g_recv,
    gc_send,
    gc_recv,
    r_send,
    r_recv,
    rc_send,
    rc_recv,
    a_send,
    a_recv,
    ac_send,
    ac_recv,
    odd_send,
    odd_recv,
    two_send,
    two_recv,
    three_send,
    three_recv,
    all_send,
    all_recv,
    y_send,
    y_recv,
    carry_send,
    carry_recv,
    x_send,
    x_recv,
):
    blocks, blk, right_sides = rhs.shape
    own_rows = own_inverse.shape[0]
    size = own_inverse.shape[1]
    half = size // 2
    layer = lax.axis_index("layer")
    plane = lax.axis_index("plane")
    layers = lax.axis_size("layer")
    y = plane // (SIDE * CORES)
    x = (plane // CORES) % SIDE
    core = plane % CORES
    first_row = plane * own_rows

    def at_plane(y_at, x_at, core_at):
        return (layer, (y_at * SIDE + x_at) * CORES + core_at)

    def x_peer(d):
        return at_plane(y, (x + d) % SIDE, core)

    def y_peer(d):
        return at_plane((y + d) % SIDE, x, core)

    sibling = at_plane(y, x, 1 - core)

    is_one = layer % 2 == 0
    is_odd = layer % 2 == 1
    is_two = layer % 4 == 1
    is_three = layer == 3
    not_three = layer != 3
    is_helper = layer % 4 == 3
    is_seven = layer == 7
    has_first = layer != 7
    sep_of = [layer // 2, 4 + layer // 4, 6 + layer * 0]
    own_sep = jnp.where(is_one, layer // 2, jnp.where(is_two, 4 + layer // 4, 6))

    second_sep = jnp.where(is_helper, layer // 2, own_sep)
    second_block = jnp.where(is_helper, 1, 0)
    third_sep = ((layer + 1) % 8) // 2

    sends = []

    def remote(parts, when=None):
        def make():
            src, dst, send_sem, recv_sem, device = parts()
            return pltpu.make_async_remote_copy(
                src_ref=src,
                dst_ref=dst,
                send_sem=send_sem,
                recv_sem=recv_sem,
                device_id=device,
                device_id_type=pl.DeviceIdType.MESH,
            )

        make().start()
        sends.append((when, make))

    def only(when, act):
        if when is None:
            act()
        else:
            pl.when(when)(act)

    def arrived(dst, sem):
        pltpu.make_async_copy(dst, dst, sem).wait()

    barrier = pltpu.get_barrier_semaphore()
    peers = [sibling]
    for d in range(1, SIDE):
        peers += [x_peer(d), y_peer(d)]
    for d in range(1, 8):
        peers.append(((layer + d) % 8, plane))
    for peer in peers:
        pl.semaphore_signal(barrier, inc=1, device_id=peer, device_id_type=pl.DeviceIdType.MESH)

    local = [
        pltpu.make_async_copy(sep_inverse_hbm.at[own_sep], own_inverse, local_sem.at[0]),
        pltpu.make_async_copy(sep_diag_hbm, own_diag, local_sem.at[1]),
        pltpu.make_async_copy(
            sep_couple_hbm.at[second_sep, second_block], mat1.at[y, x, core], local_sem.at[2]
        ),
        pltpu.make_async_copy(
            sep_couple_hbm.at[third_sep, 1], mat2.at[y, x, core], local_sem.at[3]
        ),
        pltpu.make_async_copy(inverse_hbm, inverse, local_sem.at[4]),
        pltpu.make_async_copy(rhs_hbm, rhs, local_sem.at[5]),
        pltpu.make_async_copy(diag_hbm, diag, local_sem.at[6]),
        pltpu.make_async_copy(sep_rhs_hbm.at[sep_of[0]], sep_rhs.at[0], local_sem.at[7]),
        pltpu.make_async_copy(sep_rhs_hbm.at[sep_of[1]], sep_rhs.at[1], local_sem.at[8]),
        pltpu.make_async_copy(sep_rhs_hbm.at[sep_of[2]], sep_rhs.at[2], local_sem.at[9]),
    ]
    for copy in local:
        copy.start()
    couples = []
    for k in range(3):
        couples.append(
            [
                pltpu.make_async_copy(
                    couple_hbm.at[b, k], couple.at[k, :, pl.ds(b * blk, blk)], couple_sem.at[k, b]
                )
                for b in range(blocks)
            ]
        )
        for copy in couples[k]:
            copy.start()

    def send_first(pick, width, sems, h, d, when):
        def parts():
            ref = pick(y, x, core, lanes(width, h))
            send, recv = sems(0, h, d - 1)
            return ref, ref, send, recv, x_peer(d) if h == 0 else y_peer(d)

        remote(parts, when)

    def send_second(pick, width, sems, h, d, when):
        def parts():
            everywhere = slice(None)
            if h == 0:
                ref = pick(y, everywhere, core, lanes(width, h))
            else:
                ref = pick(everywhere, x, core, lanes(width, h))
            send, recv = sems(1, h, d - 1)
            return ref, ref, send, recv, y_peer(d) if h == 0 else x_peer(d)

        remote(parts, when)

    def lanes(width, h):
        return pl.ds(0, half) if h == 0 else pl.ds(half, width - half)

    def gather_first(pick, width, sems, when=None):
        for h in range(2):
            for d in range(1, SIDE):
                send_first(pick, width, sems, h, d, when)

    def gather_second(pick, width, sems, when=None):
        for h in range(2):
            for d in range(1, SIDE):
                if h == 0:
                    ref = pick(y, (x - d + SIDE) % SIDE, core, lanes(width, h))
                else:
                    ref = pick((y - d + SIDE) % SIDE, x, core, lanes(width, h))
                arrived(ref, sems(0, h, d - 1)[1])
            for d in range(1, SIDE):
                send_second(pick, width, sems, h, d, when)

    def gather_third(pick, width, sems, c_sems, when=None):
        everywhere = slice(None)
        for h in range(2):
            for d in range(1, SIDE):
                if h == 0:
                    ref = pick((y - d + SIDE) % SIDE, everywhere, core, lanes(width, h))
                else:
                    ref = pick(everywhere, (x - d + SIDE) % SIDE, core, lanes(width, h))
                arrived(ref, sems(1, h, d - 1)[1])

        def parts():
            ref = pick(everywhere, everywhere, core, everywhere)
            return (ref, ref) + c_sems() + (sibling,)

        remote(parts, when)

    def gather_end(pick, c_recv):
        everywhere = slice(None)
        arrived(pick(everywhere, everywhere, 1 - core, everywhere), c_recv)

    mats = [mat0, mat1, mat2]
    uses = [has_first, None, is_helper]

    def whole(m):
        return mats[m][:, :, :, :, 0:size].reshape(size, size)

    def mat_parts(m):
        return (
            lambda y_at, x_at, core_at, at: mats[m].at[y_at, x_at, core_at, :, at],
            mats[m].shape[-1],
            lambda *at: (g_send.at[(m,) + at], g_recv.at[(m,) + at]),
            lambda: (gc_send.at[m], gc_recv.at[m]),
        )

    def mat_first(m):
        only(uses[m], lambda: gather_first(*mat_parts(m)[:3], uses[m]))

    def mat_second(m):
        only(uses[m], lambda: gather_second(*mat_parts(m)[:3], uses[m]))

    def mat_third(m):
        only(uses[m], lambda: gather_third(*mat_parts(m), uses[m]))

    def mat_end(m):
        gather_end(mat_parts(m)[0], gc_recv.at[m])

    local[0].wait()
    local[1].wait()
    eye = lax.broadcasted_iota(jnp.int32, (own_rows, own_rows), 0) == lax.broadcasted_iota(
        jnp.int32, (own_rows, own_rows), 1
    )
    sep_rows = lax.broadcasted_iota(jnp.int32, own_diag.shape, 0) == own_sep
    diag_row = jnp.sum(jnp.where(sep_rows, own_diag[...], 0.0), axis=0, keepdims=True)
    diag_col = jnp.sum(jnp.where(eye, diag_row, 0.0), axis=1, keepdims=True)
    high = diag_col.astype(BF16).astype(F32)
    middle = (diag_col - high).astype(BF16).astype(F32)
    low = diag_col - high - middle
    lane = lax.broadcasted_iota(jnp.int32, (own_rows, EXTRA), 1)
    beside = jnp.where(
        lane == 0, high, jnp.where(lane == 1, middle, jnp.where(lane == 2, low, 0.0))
    ).astype(BF16)
    mat0[y, x, core, :, 0:size] = unit_lower(own_inverse[...], first_row)
    mat0[y, x, core, :, size:] = beside
    pl.semaphore_wait(barrier, len(peers))
    mat_first(0)
    local[2].wait()
    local[3].wait()
    mat_first(1)
    mat_first(2)

    for i in range(4, 10):
        local[i].wait()

    def solve_leaf(b, _):
        lower = unit_lower(inverse[b], 0)
        lower_t[b] = lower.astype(F32).T.astype(BF16)
        rhs_t = rhs[b].T
        columns = pl.ds(pl.multiple_of(b * blk, blk), blk)
        leaf_y[:, columns] = dot_rows(rhs_t, lower).astype(BF16)
        return 0

    lax.fori_loop(0, blocks, solve_leaf, 0)

    block_of = lax.broadcasted_iota(jnp.int32, (1, blocks * blk), 1) // blk

    def mask_lanes(k):
        result = jnp.zeros((1, blocks * blk), F32)
        for b in range(blocks):
            result = result + jnp.where(block_of == b, mask_ref[k, b].astype(F32), 0.0)
        return result

    def leaf_part(k):
        for copy in couples[k]:
            copy.wait()
        leaf_ym[...] = leaf_y[...] * mask_lanes(k).astype(BF16)
        rhs_t = sep_rhs[k].T
        adds = layer % (2 ** (k + 1)) == 0
        first = jnp.where(adds, first_row, size)

        def tile(i, _):
            start = pl.multiple_of(i * TILE, TILE)
            columns = pl.ds(start, TILE)
            rows_at = first + lax.broadcasted_iota(jnp.int32, (own_rows, TILE), 0)
            cols_at = start + lax.broadcasted_iota(jnp.int32, (own_rows, TILE), 1)
            place = jnp.where(rows_at == cols_at, 1.0, 0.0).astype(BF16)
            term = dot_cols(rhs_t, place) - dot_rows(leaf_ym[...], couple[k, columns, :])
            part[k, :, :, :, :, columns] = term.astype(BF16).reshape(
                part.shape[1:-1] + (TILE,)
            )
            return 0

        lax.fori_loop(0, size // TILE, tile, 0)
        remote(
            lambda: (
                part.at[k, 1 - core],
                paired.at[k],
                rc_send.at[k],
                rc_recv.at[k],
                sibling,
            )
        )

    def reduce_first(k):
        arrived(paired.at[k], rc_recv.at[k])
        chip_sum[k] = (part[k, core].astype(F32) + paired[k].astype(F32)).astype(BF16)
        for h in range(2):
            for d in range(1, SIDE):
                send_part(k, h, d)

    def send_part(k, h, d):
        def parts():
            if h == 0:
                ref = chip_sum.at[k, :, (x + d) % SIDE, :, pl.ds(0, half)]
            else:
                ref = chip_sum.at[k, (y + d) % SIDE, :, :, pl.ds(half, half)]
            return (
                ref,
                in1.at[k, h, d - 1],
                r_send.at[k, 0, h, d - 1],
                r_recv.at[k, 0, h, d - 1],
                x_peer(d) if h == 0 else y_peer(d),
            )

        remote(parts)

    def send_sum(k, h, d):
        remote(
            lambda: (
                sum1.at[k, h, ((y if h == 0 else x) + d) % SIDE],
                in2.at[k, h, d - 1],
                r_send.at[k, 1, h, d - 1],
                r_recv.at[k, 1, h, d - 1],
                y_peer(d) if h == 0 else x_peer(d),
            )
        )

    def reduce_second(k):
        for h in range(2):
            if h == 0:
                value = chip_sum[k, :, x, :, 0:half].astype(F32)
            else:
                value = chip_sum[k, y, :, :, half:].astype(F32)
            for d in range(1, SIDE):
                arrived(in1.at[k, h, d - 1], r_recv.at[k, 0, h, d - 1])
                value = value + in1[k, h, d - 1].astype(F32)
            sum1[k, h] = value.astype(BF16)
            for d in range(1, SIDE):
                send_sum(k, h, d)

    def reduce_end(k):
        for h in range(2):
            value = sum1[k, h, y if h == 0 else x].astype(F32)
            for d in range(1, SIDE):
                arrived(in2.at[k, h, d - 1], r_recv.at[k, 1, h, d - 1])
                value = value + in2[k, h, d - 1].astype(F32)
            total[k, :, h * half : (h + 1) * half] = value

        def send():
            out_total[k] = total[k].astype(BF16)
            if k < 2:
                remote(
                    lambda: (
                        out_total.at[k],
                        from_odd.at[k],
                        odd_send.at[k],
                        odd_recv.at[k],
                        ((layer + 7) % 8, plane),
                    ),
                    is_odd,
                )
            else:
                remote(
                    lambda: (
                        out_total.at[k],
                        from_all.at[slot_of_all()],
                        all_send,
                        all_recv.at[slot_of_all()],
                        (3, plane),
                    ),
                    not_three,
                )

        pl.when(is_odd if k < 2 else not_three)(send)

    def slot_of_all():
        return layer - jnp.where(layer > 3, 1, 0)

    def whole_total(k):
        arrived(from_odd.at[k], odd_recv.at[k])
        return total[k] + from_odd[k].astype(F32)

    def divide(value):
        picks = jnp.where(
            lax.broadcasted_iota(jnp.int32, (value.shape[0], EXTRA), 1) < 3, 1.0, 0.0
        ).astype(BF16)
        parts = mat0[:, :, :, :, size:].reshape(size, EXTRA)
        return value / dot_rows(picks, parts)

    def forward(residual):
        solved = dot_rows(residual.astype(BF16), whole(0)).astype(BF16)
        sep_y[...] = solved
        sep_z[...] = divide(solved.astype(F32))

    two_of = (layer // 4) * 4 + 1
    two_slot = (layer % 4) // 2

    leaf_part(0)
    mat_second(0)
    leaf_part(1)
    reduce_first(0)
    leaf_part(2)
    reduce_first(1)
    reduce_second(0)
    mat_second(1)
    reduce_end(0)
    mat_third(0)
    reduce_second(1)
    mat_second(2)

    @pl.when(is_one)
    def _():
        residual = whole_total(0)
        mat_end(0)
        forward(residual)
        remote(
            lambda: (
                sep_y,
                helped_y.at[1 - two_slot],
                y_send,
                y_recv.at[1 - two_slot],
                ((layer + 7 + 2 * two_slot) % 8, plane),
            ),
            is_one,
        )

    reduce_first(2)
    reduce_end(1)
    mat_third(1)

    @pl.when(is_one)
    def _():
        mat_end(1)
        to_two[...] = (whole_total(1) - dot_rows(sep_y[...], whole(1))).astype(BF16)
        remote(
            lambda: (
                to_two,
                from_one.at[two_slot],
                two_send,
                two_recv.at[two_slot],
                (two_of, plane),
            ),
            is_one,
        )

    reduce_second(2)
    mat_third(2)
    reduce_end(2)

    @pl.when(is_helper)
    def _():
        mat_end(1)
        mat_end(2)
        for slot in range(2):
            arrived(helped_y.at[slot], y_recv.at[slot])
        helped[...] = dot_rows(helped_y[0], whole(1)) + dot_rows(helped_y[1], whole(2))

    def send_three(slot, when):
        remote(
            lambda: (
                to_three,
                from_two.at[slot()],
                three_send,
                three_recv.at[slot()],
                (3, plane),
            ),
            when,
        )

    @pl.when(is_seven)
    def _():
        to_three[...] = helped[...].astype(BF16)
        send_three(lambda: 2, is_seven)

    @pl.when(is_two)
    def _():
        mat_end(0)
        mat_end(1)
        for slot in range(2):
            arrived(from_one.at[slot], two_recv.at[slot])
        forward(from_one[0].astype(F32) + from_one[1].astype(F32))
        to_three[...] = dot_rows(sep_y[...], whole(1)).astype(BF16)
        send_three(lambda: layer // 4, is_two)

    diag_lanes = jnp.concatenate([diag[b : b + 1, :] for b in range(blocks)], axis=1)
    back[...] = leaf_y[...].astype(F32) / diag_lanes

    def finish(k, target):
        answer[k, core, y, x] = dot_cols(target.astype(BF16), whole(0)).astype(BF16)

    def own_answer(k):
        return answer.at[k, core, y, x]

    def send_answer(k, slot, layer_to, when):
        remote(
            lambda: (
                own_answer(k),
                own_answer(k),
                x_send.at[slot],
                x_recv.at[k],
                (layer_to(), plane),
            ),
            when,
        )

    @pl.when(is_three)
    def _():
        mat_end(0)
        residual = total[2] - helped[...]
        for slot in range(7):
            arrived(from_all.at[slot], all_recv.at[slot])
            residual = residual + from_all[slot].astype(F32)
        for slot in (2, 0, 1):
            arrived(from_two.at[slot], three_recv.at[slot])
            residual = residual - from_two[slot].astype(F32)
        forward(residual)
        finish(2, sep_z[...])
        for slot, layer_to in enumerate((1, 5, 7, 2, 4, 0, 6)):
            send_answer(2, slot, lambda layer_to=layer_to: layer_to, is_three)

    def send_carry(slot):
        remote(
            lambda: (
                carry.at[slot],
                carried,
                carry_send.at[slot],
                carry_recv,
                ((layer + 7 + 2 * slot) % 8, plane),
            ),
            is_helper,
        )

    @pl.when(jnp.logical_not(is_three))
    def _():
        arrived(own_answer(2), x_recv.at[2])

    @pl.when(is_two)
    def _():
        finish(1, sep_z[...] - dot_cols(own_answer(2)[...], whole(1)))
        for slot, shift in enumerate((7, 1, 2)):
            send_answer(1, 7 + slot, lambda shift=shift: (layer + shift) % 8, is_two)

    def answer_parts(k):
        return (
            lambda y_at, x_at, core_at, at: answer.at[k, core_at, y_at, x_at, :, at],
            size,
            lambda *at: (a_send.at[(k,) + at], a_recv.at[(k,) + at]),
            lambda: (ac_send.at[k], ac_recv.at[k]),
        )

    def answer_first(k, when=None):
        gather_first(*answer_parts(k)[:3], when)

    def answer_second(k):
        gather_second(*answer_parts(k)[:3])

    def answer_third(k):
        gather_third(*answer_parts(k))

    def answer_end(k):
        gather_end(answer_parts(k)[0], ac_recv.at[k])

    @pl.when(is_helper)
    def _():
        for slot in range(2):
            term = dot_cols(own_answer(2)[...], whole(1 + slot))
            carry[slot] = term.astype(BF16)
            send_carry(slot)

    answer_first(2)
    answer_second(2)

    @pl.when(jnp.logical_not(is_two))
    def _():
        arrived(own_answer(1), x_recv.at[1])

    @pl.when(is_one)
    def _():
        term = dot_cols(own_answer(1)[...], whole(1))
        arrived(carried, carry_recv)
        finish(0, sep_z[...] - carried[...].astype(F32) - term)
        send_answer(0, 10, lambda: layer + 1, is_one)
        answer_first(0, is_one)

    own_rows_at = jnp.where(
        first_row + lax.broadcasted_iota(jnp.int32, (own_rows, size), 0)
        == lax.broadcasted_iota(jnp.int32, (own_rows, size), 1),
        1.0,
        0.0,
    ).astype(BF16)

    side_cols = right_sides // CORES

    def rows_out(k, side):
        value = dot_rows(own_rows_at, answer[k, side].reshape(side_cols, size)).astype(BF16)
        sep_out[0, k, :, pl.ds(pl.multiple_of(side * side_cols, side_cols), side_cols)] = value

    def leaf_back(k):
        answer_end(k)
        rows_out(k, core)
        rows_out(k, 1 - core)
        leaf_ym[...] = jnp.broadcast_to(mask_lanes(k), leaf_ym.shape).astype(BF16)
        value = answer.at[k]

        def tile(i, _):
            columns = pl.ds(pl.multiple_of(i * TILE, TILE), TILE)
            term = dot_cols(
                value[...].reshape(right_sides, size), couple[k, :, columns]
            ) * leaf_ym[:, columns].astype(F32)
            back[:, columns] = back[:, columns] - term
            return 0

        lax.fori_loop(0, size // TILE, tile, 0)

    def leaf_end(side):
        rows = pl.ds(pl.multiple_of(side * side_cols, side_cols), side_cols)

        def tile(i, _):
            start = pl.multiple_of(i * TILE, TILE)
            columns = pl.ds(start, TILE)
            term = dot_cols(answer[0, side].reshape(side_cols, size), couple[0, :, columns])
            target = (back[rows, columns] - term * leaf_ym[0:1, columns].astype(F32)).astype(BF16)
            for j in range(TILE // blk):
                b = i * (TILE // blk) + j
                solved = dot_rows(lower_t[b], target[:, j * blk : (j + 1) * blk])
                leaf_out[b, :, rows] = solved.astype(BF16)
            return 0

        lax.fori_loop(0, size // TILE, tile, 0)

    answer_first(1)
    answer_second(1)

    @pl.when(is_odd)
    def _():
        arrived(own_answer(0), x_recv.at[0])
        answer_first(0, is_odd)

    answer_third(2)
    answer_second(0)
    leaf_back(2)
    answer_third(1)
    leaf_back(1)
    answer_third(0)
    leaf_ym[0:16, :] = jnp.broadcast_to(mask_lanes(0), (16, size)).astype(BF16)
    rows_out(0, core)
    leaf_end(core)
    answer_end(0)
    leaf_end(1 - core)
    rows_out(0, 1 - core)

    for when, make in sends:
        if when is None:
            make().wait_send()
    for group in (has_first, is_helper, is_one, is_odd, is_two, is_three, not_three, is_seven):

        @pl.when(group)
        def _(group=group):
            for when, make in sends:
                if when is group:
                    make().wait_send()


def copy_kernel(leaf_ref, sep_ref, leaf_out, sep_out):
    leaf_out[...] = leaf_ref[...]
    sep_out[...] = sep_ref[...]


def body(
    leaf_rhs,
    leaf_inverse,
    leaf_couple,
    couple_mask,
    leaf_diag,
    sep_rhs,
    sep_inverse,
    sep_couple,
    sep_diag,
):
    blocks, levels, size, blk = leaf_couple.shape
    right_sides = leaf_rhs.shape[2]
    own_rows = sep_rhs.shape[1]
    cols = right_sides // (SIDE * SIDE * CORES)
    half = size // 2
    grid = (SIDE, SIDE, CORES)
    sides = (CORES, SIDE, SIDE)
    vmem = pltpu.VMEM
    dma = pltpu.SemaphoreType.DMA
    hops = (levels, 2, 2, SIDE - 1)
    scratch = [
        vmem(leaf_rhs.shape, BF16),
        vmem(leaf_inverse.shape, BF16),
        vmem((levels, size, blocks * blk), BF16),
        vmem(leaf_diag.shape, F32),
        vmem((levels, own_rows, right_sides), BF16),
        vmem((own_rows, size), BF16),
        vmem(sep_diag.shape, F32),
        vmem(grid + (own_rows, size + EXTRA), BF16),
        vmem(grid + (own_rows, size), BF16),
        vmem(grid + (own_rows, size), BF16),
        vmem((right_sides, blocks * blk), BF16),
        vmem((right_sides, blocks * blk), BF16),
        vmem(leaf_inverse.shape, BF16),
        vmem((levels,) + sides + (cols, size), BF16),
        vmem((levels, SIDE, SIDE, cols, size), BF16),
        vmem((levels, SIDE, SIDE, cols, size), BF16),
        vmem((levels, 2, SIDE - 1, SIDE, cols, half), BF16),
        vmem((levels, 2, SIDE, cols, half), BF16),
        vmem((levels, 2, SIDE - 1, cols, half), BF16),
        vmem((levels, cols, size), F32),
        vmem((levels, cols, size), BF16),
        vmem((levels, cols, size), BF16),
        vmem((7, cols, size), BF16),
        vmem((cols, size), BF16),
        vmem((2, cols, size), BF16),
        vmem((cols, size), BF16),
        vmem((3, cols, size), BF16),
        vmem((cols, size), BF16),
        vmem((2, cols, size), BF16),
        vmem((cols, size), F32),
        vmem((2, cols, size), BF16),
        vmem((cols, size), BF16),
        vmem((cols, size), F32),
        vmem((levels,) + sides + (cols, size), BF16),
        vmem((right_sides, blocks * blk), F32),
        dma((10,)),
        dma((levels, blocks)),
        dma(hops),
        dma(hops),
        dma((levels,)),
        dma((levels,)),
        dma(hops),
        dma(hops),
        dma((levels,)),
        dma((levels,)),
        dma(hops),
        dma(hops),
        dma((levels,)),
        dma((levels,)),
        dma((2,)),
        dma((2,)),
        dma,
        dma((2,)),
        dma,
        dma((3,)),
        dma,
        dma((7,)),
        dma,
        dma((2,)),
        dma((2,)),
        dma,
        dma((11,)),
        dma((levels,)),
    ]
    any_space = pl.BlockSpec(memory_space=pl.ANY)
    in_vmem = pl.BlockSpec(memory_space=pltpu.VMEM)
    leaf_block = pl.BlockSpec((blocks // 4,) + leaf_rhs.shape[1:], lambda i: (i, 0, 0))
    sep_block = pl.BlockSpec((1, levels, own_rows, right_sides), lambda i: (0, 0, 0, 0))
    outs = pl.pallas_call(
        kernel,
        out_shape=(
            jax.ShapeDtypeStruct(leaf_rhs.shape, BF16),
            jax.ShapeDtypeStruct((1, levels, own_rows, right_sides), BF16),
        ),
        in_specs=[pl.BlockSpec(memory_space=pltpu.SMEM)] + [any_space] * 8,
        out_specs=(in_vmem, in_vmem),
        scratch_shapes=scratch,
        compiler_params=pltpu.CompilerParams(
            collective_id=0, has_side_effects=True, vmem_limit_bytes=56 * 2**20
        ),
    )(
        couple_mask.T,
        leaf_rhs,
        leaf_inverse,
        leaf_couple,
        leaf_diag,
        sep_rhs,
        sep_inverse,
        sep_couple,
        sep_diag,
    )
    return pl.pallas_call(
        copy_kernel,
        out_shape=tuple(jax.ShapeDtypeStruct(out.shape, out.dtype) for out in outs),
        grid=(4,),
        in_specs=[leaf_block, sep_block],
        out_specs=(leaf_block, sep_block),
    )(*outs)


def solution(mesh):
    in_specs = (
        P(("layer", "plane"), None, None),
        P(("layer", "plane"), None, None),
        P(("layer", "plane"), None, None, None),
        P(("layer", "plane"), None),
        P(("layer", "plane"), None),
        P(None, "plane", None),
        P(None, "plane", None),
        P(None, None, "plane", None),
        P(None, "plane"),
    )
    out_specs = (P(("layer", "plane"), None, None), P("layer", None, "plane", None))
    return jax.shard_map(body, mesh=mesh, in_specs=in_specs, out_specs=out_specs, check_vma=False)
```
